256 devices in a mesh: tmpl: 2 (over x_hi), row: 16 (over z, core), col: 8 (over x_lo, y).
Axes of the slice: x: 4 (x_hi: 2, x_lo: 2; x = x_hi * 2 + x_lo), y: 4, z: 8, core: 2. Of those that a mesh axis runs over, the one named last changes fastest.
Arguments:
- template_pair: bfloat16 [4, 256, 256, 64], P('tmpl', 'row', 'col'), may hold values from -6 to 6
- template_mask: int32 [4], P('tmpl'), may hold values from 0 to 1, as said below
- pair_mask: int32 [256, 256], P('row', 'col'), may hold values 0 or 1
- main_pair: bfloat16 [256, 256, 128], P('row', 'col'), may hold values from -6 to 6
- update_cotangent: bfloat16 [256, 256, 128], P('row', 'col'), may hold values from -2.390625 to 2.390625
- gain_in: float32 [64], replicated, may hold values from 0.1 to 1.9
- proj_a: bfloat16 [64, 64], replicated, may hold values from -0.75 to 0.75
- gate_a: bfloat16 [64, 64], replicated, may hold values from -0.75 to 0.75
- proj_b: bfloat16 [64, 64], replicated, may hold values from -0.75 to 0.75
- gate_b: bfloat16 [64, 64], replicated, may hold values from -0.75 to 0.75
- gain_mid: float32 [64], replicated, may hold values from 0.1 to 1.9
- proj_out: bfloat16 [64, 64], replicated, may hold values from -0.75 to 0.75
- gate_out: bfloat16 [64, 64], replicated, may hold values from -0.75 to 0.75
- gain_final: float32 [64], replicated, may hold values from 0.1 to 1.9
- key_weight: bfloat16 [64, 64], replicated, may hold values from -0.75 to 0.75
- value_weight: bfloat16 [64, 64], replicated, may hold values from -0.75 to 0.75
- query_weight: bfloat16 [128, 64], replicated, may hold values from -0.5 to 0.5
- output_weight: bfloat16 [64, 128], replicated, may hold values from -0.75 to 0.75
Outputs:
- pair_grad: bfloat16 [4, 256, 256, 64], P('tmpl', 'row', 'col')
- main_grad: bfloat16 [256, 256, 128], P('row', 'col')
The draws below stay inside these ranges and needn't reach their ends.
Inputs may be any that keep to these rules, and one draw needn't show every extreme that they name: `template_mask`: exactly one of the 4 templates is absent (0); all others are present (1).
All inputs are finite; a program needn't handle non-finite values. No bound on the sum of `pair_mask` on one device may be relied on, other than what follows from the above.
Results may differ from the reference program's by a relative error of at most 0.027.
Values may be sent and summed in bfloat16 or wider, within the bound.
No kernel may reach another device: no remote copies, remote signals or barrier semaphores. Data moves between devices by JAX's collectives and lax.ppermute only.
A program may use at most 128 MiB of HBM per device.

```python
import math
import jax
import jax.numpy as jnp
from jax import lax

TPW = 64
HID = 64
MPW = 128
HEADS = 4
HEAD_DIM = 16
QK = 64
TEMPLATES = 4
CROP = 256


def draw_template_mask(key, part):
    key = jax.random.fold_in(key, 11)
    absent = jax.random.randint(key, (), 0, TEMPLATES)
    return (jnp.arange(TEMPLATES) != absent).astype(jnp.int32)


def plant(array, rng, low, high):
    spot = [jax.random.randint(jax.random.fold_in(rng, axis), (), 0, length) for axis, length in enumerate(array.shape)]
    longest = array.shape.index(max(array.shape))
    neighbour = spot[:longest] + [(spot[longest] + 1) % array.shape[longest]] + spot[longest + 1:]
    return array.at[tuple(spot)].set(low).at[tuple(neighbour)].set(high)


def shard_levels(stream_key, extent, pieces, smallest, largest):
    def one(position, parts):
        heights = jax.random.uniform(jax.random.fold_in(jax.random.fold_in(stream_key, 6), position), (parts,), jnp.float32, smallest / len(pieces), largest / len(pieces))
        return jnp.repeat(jnp.exp(heights), extent[position] // parts).reshape((-1,) + (1,) * (len(extent) - position - 1))

    loudness = one(*pieces[0])
    for cut in pieces[1:]:
        loudness = loudness * one(*cut)
    return loudness


def centred(stream_key, shape, spread, limit, split=(), held_as=jnp.bfloat16):
    array = jax.random.normal(stream_key, shape, jnp.float32) * spread
    if len(split) > 0:
        array = shard_levels(stream_key, shape, split, -0.22, 0.18) * array
    return jnp.clip(array, min=-limit, max=limit).astype(held_as)


def setup_inputs(seed: int = 0) -> dict:
    key_list = jax.random.split(jax.random.key(seed), 19)
    return {
        "template_pair": centred(key_list[0], (TEMPLATES, CROP, CROP, TPW), 1.0, 6.0, ((0, 2), (1, 16), (2, 8))),
        "template_mask": draw_template_mask(jax.random.fold_in(key_list[18], 71), 0),
        "pair_mask": plant((jax.random.randint(key_list[2], (CROP, CROP), 0, 4) < 3).astype(jnp.int32), jax.random.fold_in(key_list[2], 1), 0, 1),
        "main_pair": centred(key_list[3], (CROP, CROP, MPW), 1.0, 6.0, ((0, 16), (1, 8))),
        "update_cotangent": centred(key_list[4], (CROP, CROP, MPW), 0.4, 2.390625, ((0, 16), (1, 8))),
        "gain_in": jnp.clip(1.0 + 0.18 * jax.random.normal(key_list[5], (TPW,), jnp.float32), 0.1, 1.9),
        "proj_a": centred(key_list[6], (TPW, HID), TPW ** -0.5, 0.75),
        "gate_a": centred(key_list[7], (TPW, HID), TPW ** -0.5, 0.75),
        "proj_b": centred(key_list[8], (TPW, HID), TPW ** -0.5, 0.75),
        "gate_b": centred(key_list[9], (TPW, HID), TPW ** -0.5, 0.75),
        "gain_mid": jnp.clip(1.0 + 0.18 * jax.random.normal(key_list[10], (HID,), jnp.float32), 0.1, 1.9),
        "proj_out": centred(key_list[11], (HID, TPW), HID ** -0.5, 0.75),
        "gate_out": centred(key_list[12], (TPW, TPW), TPW ** -0.5, 0.75),
        "gain_final": jnp.clip(1.0 + 0.18 * jax.random.normal(key_list[13], (TPW,), jnp.float32), 0.1, 1.9),
        "key_weight": centred(key_list[14], (TPW, QK), TPW ** -0.5, 0.75),
        "value_weight": centred(key_list[15], (TPW, QK), TPW ** -0.5, 0.75),
        "query_weight": centred(key_list[16], (MPW, QK), MPW ** -0.5, 0.5),
        "output_weight": centred(key_list[17], (QK, MPW), QK ** -0.5, 0.75),
    }


EPS = 1e-05

def normalize(inputs, gain_vec):
    mean_val = lax.optimization_barrier(jnp.mean(inputs, axis=-1, keepdims=True))
    centered = inputs - mean_val
    variance = lax.optimization_barrier(jnp.mean(centered * centered, axis=-1, keepdims=True))
    return centered * lax.rsqrt(variance + EPS) * gain_vec.astype(jnp.float32)

def project(normed, weight):
    return jnp.dot(normed, weight, preferred_element_type=jnp.float32)

def front(pair_in, mask_cells, gain_in, proj_a, gate_a, proj_b, gate_b):
    normed = normalize(pair_in.astype(jnp.float32), gain_in).astype(jnp.bfloat16)
    keep_mask = mask_cells.astype(jnp.float32)[..., None]
    left_proj = (keep_mask * jax.nn.sigmoid(project(normed, gate_a)) * project(normed, proj_a)).astype(jnp.bfloat16)
    right_proj = (keep_mask * jax.nn.sigmoid(project(normed, gate_b)) * project(normed, proj_b)).astype(jnp.bfloat16)
    return (left_proj, right_proj)

def back(pair_in, product, gain_in, gain_mid, proj_out, gate_out, gain_final, key_weight, value_weight):
    normed = normalize(pair_in.astype(jnp.float32), gain_in).astype(jnp.bfloat16)
    gating = jax.nn.sigmoid(project(normed, gate_out))
    mixed_norm = normalize(product.astype(jnp.float32), gain_mid).astype(jnp.bfloat16)
    updated = pair_in.astype(jnp.float32) + gating * project(mixed_norm, proj_out)
    final_norm = normalize(updated, gain_final).astype(jnp.bfloat16)
    return (project(final_norm, key_weight).astype(jnp.bfloat16), project(final_norm, value_weight).astype(jnp.bfloat16))

def split_heads(array_in):
    return array_in.reshape(array_in.shape[:-1] + (HEADS, array_in.shape[-1] // HEADS))

def reference(template_pair, template_mask, pair_mask, main_pair, update_cotangent, gain_in, proj_a, gate_a, proj_b, gate_b, gain_mid, proj_out, gate_out, gain_final, key_weight, value_weight, query_weight, output_weight):

    def front_of(pair_in):
        return front(pair_in, pair_mask, gain_in, proj_a, gate_a, proj_b, gate_b)
    (left_proj, right_proj), front_vjp = jax.vjp(front_of, template_pair)
    product = jnp.einsum('sikc,sjkc->sijc', left_proj.astype(jnp.float32), right_proj.astype(jnp.float32)).astype(jnp.bfloat16)

    def back_of(pair_in, product_in):
        return back(pair_in, product_in, gain_in, gain_mid, proj_out, gate_out, gain_final, key_weight, value_weight)
    (key_proj, value_proj), back_vjp = jax.vjp(back_of, template_pair, product)
    query_proj = project(main_pair, query_weight).astype(jnp.bfloat16)
    grad_out = project(update_cotangent, output_weight.T)
    present = template_mask.astype(jnp.float32)[:, None, None, None]
    score_scale = 1.0 / math.sqrt(HEAD_DIM)
    query_heads = split_heads(query_proj.astype(jnp.float32))[None]
    key_heads = split_heads(key_proj.astype(jnp.float32))
    value_heads = split_heads(value_proj.astype(jnp.float32))
    out_heads = split_heads(grad_out)[None]
    exp_terms = present * jnp.exp(lax.optimization_barrier(jnp.sum(query_heads * key_heads, -1)) * score_scale)
    weight_sum = lax.optimization_barrier(jnp.sum(exp_terms, 0))
    weights = exp_terms / weight_sum
    along_heads = lax.optimization_barrier(jnp.sum(out_heads * value_heads, -1))
    average = lax.optimization_barrier(jnp.sum(weights * along_heads, 0))
    slope_term = weights * (along_heads - average)
    query_sum = lax.optimization_barrier(jnp.sum(slope_term[..., None] * key_heads, 0)) * score_scale
    query_grad = query_sum.reshape(query_proj.shape).astype(jnp.bfloat16)
    main_grad = project(query_grad, query_weight.T).astype(jnp.bfloat16)
    key_grad = (slope_term[..., None] * query_heads * score_scale).reshape(key_proj.shape).astype(jnp.bfloat16)
    value_grad = (weights[..., None] * out_heads).reshape(value_proj.shape).astype(jnp.bfloat16)
    back_grad, product_grad = back_vjp((key_grad, value_grad))
    left_grad = jnp.einsum('sijc,sjkc->sikc', product_grad.astype(jnp.float32), right_proj.astype(jnp.float32)).astype(jnp.bfloat16)
    right_grad = jnp.einsum('sijc,sikc->sjkc', product_grad.astype(jnp.float32), left_proj.astype(jnp.float32)).astype(jnp.bfloat16)
    front_grad, = front_vjp((left_grad, right_grad))
    pair_grad = (front_grad.astype(jnp.float32) + back_grad.astype(jnp.float32)).astype(jnp.bfloat16)
    return (pair_grad, main_grad)
```

```python
import functools
import math

import jax
import jax.numpy as jnp
from jax import lax
from jax.experimental import pallas as pl
from jax.experimental.pallas import tpu as pltpu
from jax.sharding import PartitionSpec as P

EPS = 1e-05
F32 = jnp.float32
BF16 = jnp.bfloat16
HEADS = 4
HEAD_DIM = 16
SCALE = 1.0 / math.sqrt(HEAD_DIM)
GROUP = ("col", "row")


def iota(shape, axis):
    return lax.broadcasted_iota(jnp.int32, shape, axis)


def onehot(cond):
    return jnp.where(cond, 1.0, 0.0).astype(BF16)


def dot(a, b):
    return lax.dot_general(a, b, (((1,), (0,)), ((), ())), preferred_element_type=F32)


def dot_nt(a, b):
    return lax.dot_general(a, b, (((1,), (1,)), ((), ())), preferred_element_type=F32)


def dot_tn(a, b):
    return lax.dot_general(a, b, (((0,), (0,)), ((), ())), preferred_element_type=F32)


def eye64():
    return onehot(iota((64, 64), 0) == iota((64, 64), 1))


def c_to_rc(v):
    return jnp.concatenate(
        [
            jnp.concatenate([v[:, s * 512 + r * 128 : s * 512 + r * 128 + 128] for s in range(2)], axis=1)
            for r in range(4)
        ],
        axis=0,
    )


def rc_to_c(v):
    return jnp.concatenate(
        [v[r * 64 : r * 64 + 64, s * 128 : s * 128 + 128] for s in range(2) for r in range(4)], axis=1
    )


def both(v):
    return jnp.concatenate([v, v], axis=1)


def column(gain_row, repeat):
    pick = iota((64 * repeat, 64), 0) // repeat == iota((64 * repeat, 64), 1)
    return jnp.sum(jnp.where(pick, gain_row, 0.0), axis=1, keepdims=True)


def mean_c(v):
    return jnp.mean(v, axis=0, keepdims=True)


def mean_cr(v):
    part = jnp.sum(v.reshape(32, 8, 256), axis=0)
    return (part + pltpu.roll(part, 4, 0)) * (1.0 / 64.0)


def spread_cr(v):
    return jnp.broadcast_to(v[None], (32, 8, 256)).reshape(256, 256)


def hat_c(v):
    centered = v - mean_c(v)
    rstd = lax.rsqrt(mean_c(centered * centered) + EPS)
    return centered * rstd, rstd


def norm_grad_c(grad, gain, hat, rstd):
    scaled = grad * gain
    return rstd * (scaled - mean_c(scaled) - hat * mean_c(scaled * hat))


def hat_cr(v):
    centered = v - spread_cr(mean_cr(v))
    rstd = spread_cr(lax.rsqrt(mean_cr(centered * centered) + EPS))
    return centered * rstd, rstd


def norm_grad_cr(grad, gain, hat, rstd):
    scaled = grad * gain
    return rstd * (scaled - spread_cr(mean_cr(scaled)) - hat * spread_cr(mean_cr(scaled * hat)))


def wide_pair(wa, wb):
    row, lane = iota((64, 512), 0), iota((64, 512), 1)
    own = row == lane // 8
    base = dot(wa, onehot(own & (lane % 8 < 4))) + dot(wb, onehot(own & (lane % 8 >= 4)))
    return jnp.concatenate([jnp.where(lane % 4 == r, base, 0.0) for r in range(4)], axis=0).astype(BF16)


def wide_out(w):
    row, lane = iota((64, 256), 0), iota((64, 256), 1)
    base = dot_tn(w, onehot(row == lane // 4))
    return jnp.concatenate([jnp.where(lane % 4 == r, base, 0.0) for r in range(4)], axis=0).astype(BF16)


def wide_mask(mask):
    tiled = dot(mask.astype(F32).astype(BF16), onehot(iota((32, 256), 0) == iota((32, 256), 1) % 32))
    i, lane = iota((16, 256), 0), iota((16, 256), 1)
    tiled = jnp.where(i % 4 == (lane % 128) // 32, tiled, 0.0).astype(BF16)
    return dot(onehot(iota((8, 16), 0) % 4 == iota((8, 16), 1) // 4), tiled)


def spread8(v):
    return jnp.broadcast_to(v[None], (64, 8, 256)).reshape(512, 256)


def swap_groups(four):
    lane = iota(four[0].shape, 1) // 32
    for bit in (1, 2):
        low = (lane & bit) == 0
        out = []
        for a in range(4):
            if a & bit == 0:
                out.append(jnp.where(low, four[a], pltpu.roll(four[a ^ bit], 32 * bit, 1)))
            else:
                out.append(jnp.where(low, pltpu.roll(four[a ^ bit], 128 - 32 * bit, 1), four[a]))
        four = out
    return four


def swap_in(blocks):
    lo, hi = swap_groups(blocks[:4]), swap_groups(blocks[4:])
    return [jnp.concatenate([lo[q], hi[q]], axis=1) for q in range(4)]


def swap_out(rows):
    return swap_groups([v[:, :128] for v in rows]) + swap_groups([v[:, 128:] for v in rows])


def sides_first():
    a, b = iota((128, 128), 0), iota((128, 128), 1)
    return onehot((a // 64 == (b // 4) % 2) & ((a % 64) // 4 == b // 8) & (a % 4 == b % 4))


def natural_rows():
    a, b = iota((256, 256), 0), iota((256, 256), 1)
    return onehot((a % 4 == b // 64) & (a // 4 == b % 64))


def front_kernel(x_ref, mask_ref, gain_ref, pa_ref, ga_ref, pb_ref, gb_ref, out_ref, x_out, n_out):
    x = dot_nt(eye64(), x_ref[...].reshape(1024, 64))
    hat, _ = hat_c(x)
    normed = (hat * column(gain_ref[...], 1)).astype(BF16)
    x_out[...] = x.astype(BF16)
    n_out[...] = normed
    rc = c_to_rc(normed)
    gate = dot_tn(wide_pair(ga_ref[...], gb_ref[...]), rc)
    proj = dot_tn(wide_pair(pa_ref[...], pb_ref[...]), rc)
    mask = spread8(wide_mask(mask_ref[...]))
    both_sides = (mask * jax.nn.sigmoid(gate) * proj).astype(BF16)
    out_ref[:512, :] = both_sides[:, :128]
    out_ref[512:, :] = both_sides[:, 128:]


def side_kernel(n_ref, main_ref, cot_ref, go_ref, wq_ref, wo_ref, gat_out, q_out, g_out):
    gat_out[...] = jax.nn.sigmoid(dot_tn(go_ref[...], n_ref[...]))
    q_out[...] = dot_nt(wq_ref[...].T, main_ref[...].reshape(512, 128)).astype(BF16)
    g_out[...] = dot_nt(wo_ref[...], cot_ref[...].reshape(512, 128))


def product_kernel(x_ref, out_ref, a_out, b_out):
    blocks = [x_ref[c * 128 : c * 128 + 128, :].astype(F32) for c in range(8)]
    order = sides_first()
    parts = [dot(order, v.astype(BF16)).astype(BF16) for v in swap_in(blocks)]
    a = jnp.concatenate([v[:64] for v in parts], axis=0)
    b = jnp.concatenate([v[64:] for v in parts], axis=0)
    b = dot(natural_rows(), b).astype(BF16)
    a_out[...] = a
    b_out[...] = b
    prod = dot_nt(a, b)
    for c, v in enumerate(swap_out([prod[q * 64 : q * 64 + 64] for q in range(4)])):
        out_ref[c * 64 : c * 64 + 64, :] = v.astype(BF16)


def heads_sum(v):
    return jnp.sum(v.reshape(HEADS, HEAD_DIM, v.shape[-1]), axis=1)


def heads_spread(v):
    return jnp.broadcast_to(v[:, None, :], (HEADS, HEAD_DIM, v.shape[-1])).reshape(64, v.shape[-1])


def middle(x_ref, prod_ref, gat_ref, gm, gf, po_ref):
    prod = jnp.concatenate([prod_ref[:256, :], prod_ref[256:, :]], axis=1).astype(F32)
    hat_m, rstd_m = hat_cr(prod)
    wide = wide_out(po_ref[...])
    out = rc_to_c(dot(wide, (hat_m * gm).astype(BF16)))
    updated = x_ref[...].astype(F32) + gat_ref[...] * out
    hat_f, rstd_f = hat_c(updated)
    return hat_m, rstd_m, wide, out, hat_f, rstd_f


def score_kernel(
    x_ref, prod_ref, gat_ref, q_ref, g_ref, present_ref, gm_ref, gf_ref, po_ref, kw_ref, vw_ref,
    stat_out, w_out, along_out, key_out,
):
    gm, gf = column(gm_ref[...], 4), column(gf_ref[...], 1)
    _, _, _, _, hat_f, _ = middle(x_ref, prod_ref, gat_ref, gm, gf, po_ref)
    final = (hat_f * gf).astype(BF16)
    key = dot_tn(kw_ref[...], final).astype(BF16)
    val = dot_tn(vw_ref[...], final).astype(BF16)
    key_out[...] = key
    score = heads_sum(both(q_ref[...].astype(F32)) * key.astype(F32)) * SCALE
    along = heads_sum(both(g_ref[...]) * val.astype(F32))
    s0 = jnp.where(present_ref[0] > 0, score[:, :512], -1e30)
    s1 = jnp.where(present_ref[1] > 0, score[:, 512:], -1e30)
    top = jnp.maximum(s0, s1)
    e0, e1 = jnp.exp(s0 - top), jnp.exp(s1 - top)
    total = e0 + e1
    w0, w1 = e0 / total, e1 / total
    w_out[...] = jnp.concatenate([w0, w1], axis=1)
    along_out[...] = along
    stat_out[0] = top + jnp.log(total)
    stat_out[1] = w0 * along[:, :512] + w1 * along[:, 512:]


def grad_kernel(
    x_ref, prod_ref, gat_ref, q_ref, g_ref, key_ref, w_ref, along_ref, mine_ref, other_ref,
    gm_ref, gf_ref, po_ref, kw_ref, vw_ref,
    pg_out, qsum_out, du_out, dgate_out,
):
    gm, gf = column(gm_ref[...], 4), column(gf_ref[...], 1)
    hat_m, rstd_m, wide, out, hat_f, rstd_f = middle(x_ref, prod_ref, gat_ref, gm, gf, po_ref)
    share = jax.nn.sigmoid(mine_ref[0] - other_ref[0])
    average = share * mine_ref[1] + jax.nn.sigmoid(other_ref[0] - mine_ref[0]) * other_ref[1]
    weights = w_ref[...] * both(share)
    slope = weights * (along_ref[...] - both(average))
    slope_wide = heads_spread(slope)
    part = slope_wide * key_ref[...].astype(F32)
    qsum_out[...] = (part[:, :512] + part[:, 512:]) * SCALE
    key_grad = (slope_wide * both(q_ref[...].astype(F32)) * SCALE).astype(BF16)
    value_grad = (heads_spread(weights) * both(g_ref[...])).astype(BF16)
    d_final = dot(kw_ref[...], key_grad) + dot(vw_ref[...], value_grad)
    d_updated = norm_grad_c(d_final, gf, hat_f, rstd_f)
    gat = gat_ref[...]
    du_out[...] = d_updated
    d_out = (d_updated * gat).astype(BF16)
    dgate_out[...] = (d_updated * out * gat * (1.0 - gat)).astype(BF16)
    d_mixed = dot_tn(wide, c_to_rc(d_out))
    pg = norm_grad_cr(d_mixed, gm, hat_m, rstd_m).astype(BF16)
    pg_out[:256, :] = pg[:, :128]
    pg_out[256:, :] = pg[:, 128:]


def coef_kernel(
    n_ref, mask_ref, dgate_ref, go_ref, pa_ref, ga_ref, pb_ref, gb_ref,
    cg_out, cp_out, wg_out, wp_out, dn_out,
):
    wg = wide_pair(ga_ref[...], gb_ref[...])
    wp = wide_pair(pa_ref[...], pb_ref[...])
    rc = c_to_rc(n_ref[...])
    gate = jax.nn.sigmoid(dot_tn(wg, rc))
    proj = dot_tn(wp, rc)
    scaled = spread8(wide_mask(mask_ref[...])) * gate
    cp_out[...] = scaled
    cg_out[...] = scaled * (1.0 - gate) * proj
    wg_out[...] = wg
    wp_out[...] = wp
    dn_out[...] = dot(go_ref[...], dgate_ref[...])


def triangle_kernel(pg_ref, a_ref, b_ref, out_ref):
    blocks = [pg_ref[c * 64 : c * 64 + 64, :].astype(F32) for c in range(8)]
    pg = jnp.concatenate(swap_in(blocks), axis=0).astype(BF16)
    left = dot(pg, b_ref[...]).astype(BF16)
    right = dot_tn(dot(pg, natural_rows()).astype(BF16), a_ref[...]).astype(BF16)
    order = sides_first()
    rows = [
        dot_tn(order, jnp.concatenate([left[q * 64 : q * 64 + 64], right[q * 64 : q * 64 + 64]], axis=0))
        for q in range(4)
    ]
    for c, v in enumerate(swap_out(rows)):
        out_ref[c * 128 : c * 128 + 128, :] = v.astype(BF16)


def finish_kernel(lr_ref, cg_ref, cp_ref, wg_ref, wp_ref, dn_ref, x_ref, du_ref, gain_ref, out_ref):
    grad = jnp.concatenate([lr_ref[:512, :], lr_ref[512:, :]], axis=1).astype(F32)
    d_gate = (grad * cg_ref[...]).astype(BF16)
    d_proj = (grad * cp_ref[...]).astype(BF16)
    d_normed = rc_to_c(dot(wg_ref[...], d_gate) + dot(wp_ref[...], d_proj)) + dn_ref[...]
    hat, rstd = hat_c(x_ref[...].astype(F32))
    grad_x = norm_grad_c(d_normed, column(gain_ref[...], 1), hat, rstd) + du_ref[...]
    out_ref[...] = dot_tn(grad_x.astype(BF16), eye64()).astype(BF16).reshape(2, 16, 32, 64)


def main_kernel(mine_ref, other_ref, wq_ref, out_ref):
    grad = (mine_ref[...] + other_ref[...]).astype(BF16)
    out_ref[...] = dot_tn(grad, wq_ref[...].T).astype(BF16).reshape(16, 32, 128)


def call(kernel, outs, *args, smem=(), flops=0):
    specs = [
        pl.BlockSpec(memory_space=pltpu.SMEM if n in smem else pltpu.VMEM) for n in range(len(args))
    ]
    shapes = [jax.ShapeDtypeStruct(s, t) for s, t in outs]
    nbytes = sum(a.size * a.dtype.itemsize for a in args)
    return pl.pallas_call(
        kernel,
        out_shape=shapes,
        in_specs=specs,
        out_specs=[pl.BlockSpec(memory_space=pltpu.VMEM)] * len(shapes),
        compiler_params=pltpu.CompilerParams(vmem_limit_bytes=24 * 1024 * 1024),
        cost_estimate=pl.CostEstimate(flops=flops, bytes_accessed=nbytes, transcendentals=0),
    )(*args)


def exchange(v):
    return lax.ppermute(v, "tmpl", [(0, 1), (1, 0)])


def spread_chunks(v, rows):
    return lax.all_to_all(v.reshape(128, rows, 128), GROUP, 0, 0, tiled=True).reshape(128 * rows, 128)


def body(
    template_pair, template_mask, pair_mask, main_pair, update_cotangent,
    gain_in, proj_a, gate_a, proj_b, gate_b, gain_mid, proj_out, gate_out, gain_final,
    key_weight, value_weight, query_weight, output_weight,
):
    gi, gm, gf = gain_in.reshape(1, 64), gain_mid.reshape(1, 64), gain_final.reshape(1, 64)
    sides, x, normed = call(
        front_kernel,
        [((1024, 128), BF16), ((64, 1024), BF16), ((64, 1024), BF16)],
        template_pair, pair_mask, gi, proj_a, gate_a, proj_b, gate_b,
    )
    gat, query, grad_out = call(
        side_kernel,
        [((64, 1024), F32), ((64, 512), BF16), ((64, 512), F32)],
        normed, main_pair, update_cotangent, gate_out, query_weight, output_weight,
    )
    sides = spread_chunks(sides, 8)
    prod, a, b = call(
        product_kernel, [((512, 128), BF16), ((256, 256), BF16), ((256, 256), BF16)], sides
    )
    prod = spread_chunks(prod, 4)
    stat, weights, along, key = call(
        score_kernel,
        [((2, 4, 512), F32), ((4, 1024), F32), ((4, 1024), F32), ((64, 1024), BF16)],
        x, prod, gat, query, grad_out, template_mask, gm, gf, proj_out, key_weight, value_weight,
        smem=(5,),
    )
    other = exchange(stat)
    pg, query_sum, d_updated, d_gate = call(
        grad_kernel,
        [((512, 128), BF16), ((64, 512), F32), ((64, 1024), F32), ((64, 1024), BF16)],
        x, prod, gat, query, grad_out, key, weights, along, stat, other,
        gm, gf, proj_out, key_weight, value_weight,
    )
    cg, cp, wg, wp, dn = call(
        coef_kernel,
        [
            ((512, 256), F32), ((512, 256), F32), ((256, 512), BF16), ((256, 512), BF16),
            ((64, 1024), F32),
        ],
        normed, pair_mask, d_gate, gate_out, proj_a, gate_a, proj_b, gate_b,
    )
    pg = spread_chunks(pg, 4)
    (grads,) = call(triangle_kernel, [((1024, 128), BF16)], pg, a, b)
    query_other = exchange(query_sum)
    (main_grad,) = call(main_kernel, [((16, 32, 128), BF16)], query_sum, query_other, query_weight)
    grads = spread_chunks(grads, 8)
    (pair_grad,) = call(
        finish_kernel, [((2, 16, 32, 64), BF16)], grads, cg, cp, wg, wp, dn, x, d_updated, gi
    )
    return (pair_grad, main_grad)


def solution(mesh):
    pixel = P("row", "col", None)
    placed = (
        P("tmpl", "row", "col", None), P("tmpl"), P("row", "col"), pixel, pixel,
    ) + (P(),) * 13
    return jax.shard_map(
        body,
        mesh=mesh,
        in_specs=placed,
        out_specs=(P("tmpl", "row", "col", None), pixel),
        check_vma=False,
    )
```

```python
import functools
import math

import jax
import jax.numpy as jnp
from jax import lax
from jax.experimental import pallas as pl
from jax.experimental.pallas import tpu as pltpu
from jax.sharding import PartitionSpec as P

EPS = 1e-05
F32 = jnp.float32
BF16 = jnp.bfloat16
HEADS = 4
HEAD_DIM = 16
SCALE = 1.0 / math.sqrt(HEAD_DIM)
GROUP = ("row", "col")
TURN = 12
ORDER = [p ^ (8 * TURN) for p in range(128)]


def iota(shape, axis):
    return lax.broadcasted_iota(jnp.int32, shape, axis)


def onehot(cond):
    return jnp.where(cond, 1.0, 0.0).astype(BF16)


def dot(a, b):
    return lax.dot_general(a, b, (((1,), (0,)), ((), ())), preferred_element_type=F32)


def dot_nt(a, b):
    return lax.dot_general(a, b, (((1,), (1,)), ((), ())), preferred_element_type=F32)


def dot_tn(a, b):
    return lax.dot_general(a, b, (((0,), (0,)), ((), ())), preferred_element_type=F32)


def eye64():
    return onehot(iota((64, 64), 0) == iota((64, 64), 1))


def c_to_rc(v):
    return jnp.concatenate(
        [
            jnp.concatenate([v[:, s * 512 + r * 128 : s * 512 + r * 128 + 128] for s in range(2)], axis=1)
            for r in range(4)
        ],
        axis=0,
    )


def rc_to_c(v):
    return jnp.concatenate(
        [v[r * 64 : r * 64 + 64, s * 128 : s * 128 + 128] for s in range(2) for r in range(4)], axis=1
    )


def both(v):
    return jnp.concatenate([v, v], axis=1)


def column(gain_row, repeat):
    pick = iota((64 * repeat, 64), 0) // repeat == iota((64 * repeat, 64), 1)
    return jnp.sum(jnp.where(pick, gain_row, 0.0), axis=1, keepdims=True)


def mean_c(v):
    return jnp.mean(v, axis=0, keepdims=True)


def mean_cr(v):
    part = jnp.sum(v.reshape(32, 8, 256), axis=0)
    return (part + pltpu.roll(part, 4, 0)) * (1.0 / 64.0)


def spread_cr(v):
    return jnp.broadcast_to(v[None], (32, 8, 256)).reshape(256, 256)


def hat_c(v):
    centered = v - mean_c(v)
    rstd = lax.rsqrt(mean_c(centered * centered) + EPS)
    return centered * rstd, rstd


def norm_grad_c(grad, gain, hat, rstd):
    scaled = grad * gain
    return rstd * (scaled - mean_c(scaled) - hat * mean_c(scaled * hat))


def hat_cr(v):
    centered = v - spread_cr(mean_cr(v))
    rstd = spread_cr(lax.rsqrt(mean_cr(centered * centered) + EPS))
    return centered * rstd, rstd


def norm_grad_cr(grad, gain, hat, rstd):
    scaled = grad * gain
    return rstd * (scaled - spread_cr(mean_cr(scaled)) - hat * spread_cr(mean_cr(scaled * hat)))


def wide_pair(wa, wb):
    row, lane = iota((64, 512), 0), iota((64, 512), 1)
    own = row == lane // 8
    base = dot(wa, onehot(own & (lane % 8 < 4))) + dot(wb, onehot(own & (lane % 8 >= 4)))
    return jnp.concatenate([jnp.where(lane % 4 == r, base, 0.0) for r in range(4)], axis=0).astype(BF16)


def wide_out(w):
    row, lane = iota((64, 256), 0), iota((64, 256), 1)
    base = dot_tn(w, onehot(row == lane // 4))
    return jnp.concatenate([jnp.where(lane % 4 == r, base, 0.0) for r in range(4)], axis=0).astype(BF16)


def wide_mask(mask):
    tiled = dot(mask.astype(F32).astype(BF16), onehot(iota((32, 256), 0) == iota((32, 256), 1) % 32))
    i, lane = iota((16, 256), 0), iota((16, 256), 1)
    tiled = jnp.where(i % 4 == (lane % 128) // 32, tiled, 0.0).astype(BF16)
    return dot(onehot(iota((8, 16), 0) % 4 == iota((8, 16), 1) // 4), tiled)


def spread8(v):
    return jnp.broadcast_to(v[None], (64, 8, 256)).reshape(512, 256)


def swap_groups(four):
    lane = iota(four[0].shape, 1) // 32
    for bit in (1, 2):
        low = (lane & bit) == 0
        out = []
        for a in range(4):
            if a & bit == 0:
                out.append(jnp.where(low, four[a], pltpu.roll(four[a ^ bit], 32 * bit, 1)))
            else:
                out.append(jnp.where(low, pltpu.roll(four[a ^ bit], 128 - 32 * bit, 1), four[a]))
        four = out
    return four


def swap_in(blocks):
    lo, hi = swap_groups(blocks[:4]), swap_groups(blocks[4:])
    return [jnp.concatenate([lo[q], hi[q]], axis=1) for q in range(4)]


def swap_out(rows):
    return swap_groups([v[:, :128] for v in rows]) + swap_groups([v[:, 128:] for v in rows])


def pair_up(even, odd):
    even, odd = even.reshape(8, 8, 128), odd.reshape(8, 8, 128)
    top = iota(even.shape, 1) < 4
    return jnp.where(top, even, pltpu.roll(odd, 4, 1)), jnp.where(top, pltpu.roll(even, 4, 1), odd)


def sides_first():
    a, b = iota((128, 128), 0), iota((128, 128), 1)
    return onehot((a // 64 == (b // 4) % 2) & ((a % 64) // 4 == b // 8) & (a % 4 == b % 4))


def natural_rows():
    a, b = iota((256, 256), 0), iota((256, 256), 1)
    return onehot((a % 4 == b // 64) & ((a // 4) ^ (4 * TURN) == b % 64))


def front_kernel(
    x_hbm, mask_hbm, gi_hbm, pa_hbm, ga_hbm, pb_hbm, gb_hbm, go_hbm, main_hbm, cot_hbm, wq_hbm, wo_hbm,
    po_hbm, kw_hbm, vw_hbm, gm_hbm, gf_hbm, present_hbm,
    out_ref, x_out, n_out, gat_out, q_out, g_out, wide_out_ref, kv_out, gm_out, gf_out, gi_out, absent_out,
    x_ref, mask_ref, gi_ref, pa_ref, ga_ref, pb_ref, gb_ref, go_ref, main_ref, cot_ref, wq_ref, wo_ref,
    po_ref, kw_ref, vw_ref, gm_ref, gf_ref, present_ref, sems,
):
    pairs = [
        (x_hbm, x_ref), (gi_hbm, gi_ref), (pa_hbm, pa_ref), (ga_hbm, ga_ref), (pb_hbm, pb_ref),
        (gb_hbm, gb_ref), (mask_hbm, mask_ref), (go_hbm, go_ref), (main_hbm, main_ref), (cot_hbm, cot_ref),
        (wq_hbm, wq_ref), (wo_hbm, wo_ref), (po_hbm, po_ref), (kw_hbm, kw_ref), (vw_hbm, vw_ref),
        (gm_hbm, gm_ref), (gf_hbm, gf_ref), (present_hbm, present_ref),
    ]
    copies = [pltpu.make_async_copy(a, b, sems.at[n]) for n, (a, b) in enumerate(pairs)]
    for copy in copies:
        copy.start()
    for copy in copies[:7]:
        copy.wait()
    x = dot_nt(eye64(), x_ref[...].reshape(1024, 64))
    hat, _ = hat_c(x)
    gi = column(gi_ref[...], 1)
    normed = (hat * gi).astype(BF16)
    x_out[...] = x.astype(BF16)
    n_out[...] = normed
    rc = c_to_rc(normed)
    gate = dot_tn(wide_pair(ga_ref[...], gb_ref[...]), rc)
    proj = dot_tn(wide_pair(pa_ref[...], pb_ref[...]), rc)
    mask = spread8(wide_mask(mask_ref[...]))
    both_sides = (mask * jax.nn.sigmoid(gate) * proj).astype(BF16)
    out_ref[:512, :] = both_sides[:, :128]
    out_ref[512:, :] = both_sides[:, 128:]
    gi_out[...] = jnp.broadcast_to(gi, (64, 128))
    for copy in copies[7:]:
        copy.wait()
    gat_out[...] = jax.nn.sigmoid(dot_tn(go_ref[...], normed))
    q_out[...] = dot_nt(wq_ref[...], main_ref[...].reshape(512, 128)).astype(BF16)
    g_out[...] = dot_nt(wo_ref[...], cot_ref[...].reshape(512, 128))
    wide_out_ref[...] = wide_out(po_ref[...])
    kv_out[...] = jnp.concatenate([kw_ref[...], vw_ref[...]], axis=1)
    gm_out[...] = jnp.broadcast_to(column(gm_ref[...], 4), (256, 128))
    gf_out[...] = jnp.broadcast_to(column(gf_ref[...], 1), (64, 128))
    absent_out[...] = jnp.where(
        jnp.concatenate([jnp.broadcast_to(present_ref[:, s : s + 1], (8, 512)) for s in range(2)], axis=1) > 0,
        0.0, -1e30,
    )


def product_kernel(x_ref, out_ref, a_out, b_out):
    tiles = x_ref[...].astype(F32).reshape(16, 8, 8, 128)
    blocks = [tiles[:, c].reshape(128, 128) for c in range(8)]
    order = sides_first()
    parts = [dot(order, v.astype(BF16)).astype(BF16) for v in swap_in(blocks)]
    a = jnp.concatenate([v[:64] for v in parts], axis=0)
    b = jnp.concatenate([v[64:] for v in parts], axis=0)
    b = dot(natural_rows(), b).astype(BF16)
    a_out[...] = a
    b_out[...] = b
    prod = dot_nt(a, b)
    cols = swap_out([prod[q * 64 : q * 64 + 64] for q in range(4)])
    pairs = [jnp.stack(pair_up(cols[c], cols[c + 1]), axis=1) for c in range(0, 8, 2)]
    out_ref[...] = jnp.stack(pairs, axis=2).reshape(512, 128).astype(BF16)


def heads_sum(v):
    return jnp.sum(v.reshape(HEADS, HEAD_DIM, v.shape[-1]), axis=1)


def heads_spread(v):
    return jnp.broadcast_to(v[:, None, :], (HEADS, HEAD_DIM, v.shape[-1])).reshape(64, v.shape[-1])


def tile_lanes(v, n):
    return jnp.concatenate([v] * n, axis=1)


def score_kernel(
    x_ref, prod_ref, gat_ref, q_ref, g_ref, absent_ref, gm_ref, gf_ref, wide_ref, kv_ref,
    stat_out, w_out, along_out, key_out, hat_m_out, rstd_m_out, out_out, hat_f_out, rstd_f_out,
):
    prod = jnp.concatenate([prod_ref[:256, :], prod_ref[256:, :]], axis=1).astype(F32)
    centered = prod - spread_cr(mean_cr(prod))
    rstd_m = lax.rsqrt(mean_cr(centered * centered) + EPS)
    hat_m = centered * spread_cr(rstd_m)
    out = rc_to_c(dot(wide_ref[...], (hat_m * tile_lanes(gm_ref[...], 2)).astype(BF16)))
    hat_f, rstd_f = hat_c(x_ref[...].astype(F32) + gat_ref[...] * out)
    hat_m_out[...] = hat_m
    rstd_m_out[...] = rstd_m
    out_out[...] = out
    hat_f_out[...] = hat_f
    rstd_f_out[...] = rstd_f
    final = (hat_f * tile_lanes(gf_ref[...], 8)).astype(BF16)
    key_val = dot_tn(kv_ref[...], final).astype(BF16)
    key, val = key_val[:64], key_val[64:]
    key_out[...] = key
    score = heads_sum(both(q_ref[...].astype(F32)) * key.astype(F32)) * SCALE
    along = heads_sum(both(g_ref[...]) * val.astype(F32))
    score = jnp.where(absent_ref[:4, :] < 0.0, -1e30, score)
    s0, s1 = score[:, :512], score[:, 512:]
    top = jnp.maximum(s0, s1)
    e0, e1 = jnp.exp(s0 - top), jnp.exp(s1 - top)
    total = e0 + e1
    w0, w1 = e0 / total, e1 / total
    w_out[...] = jnp.concatenate([w0, w1], axis=1)
    along_out[...] = along
    stat_out[0] = top + jnp.log(total)
    stat_out[1] = w0 * along[:, :512] + w1 * along[:, 512:]


def grad_kernel(
    gat_ref, q_ref, g_ref, key_ref, w_ref, along_ref, mine_ref, other_ref,
    gm_ref, gf_ref, wide_ref, kv_ref, hat_m_ref, rstd_m_ref, out_ref, hat_f_ref, rstd_f_ref,
    pg_out, qsum_out, du_out, dgate_out,
):
    share = jax.nn.sigmoid(mine_ref[0] - other_ref[0])
    average = share * mine_ref[1] + jax.nn.sigmoid(other_ref[0] - mine_ref[0]) * other_ref[1]
    weights = w_ref[...] * both(share)
    slope = weights * (along_ref[...] - both(average))
    slope_wide = heads_spread(slope)
    part = slope_wide * key_ref[...].astype(F32)
    qsum_out[...] = (part[:, :512] + part[:, 512:]) * SCALE
    key_grad = (slope_wide * both(q_ref[...].astype(F32) * SCALE)).astype(BF16)
    value_grad = (heads_spread(weights) * both(g_ref[...])).astype(BF16)
    d_final = dot(kv_ref[...], jnp.concatenate([key_grad, value_grad], axis=0))
    d_updated = norm_grad_c(d_final, tile_lanes(gf_ref[...], 8), hat_f_ref[...], rstd_f_ref[...])
    gat = gat_ref[...]
    du_out[...] = d_updated
    d_out = d_updated * gat
    dgate_out[...] = (d_out * out_ref[...] * (1.0 - gat)).astype(BF16)
    d_mixed = dot_tn(wide_ref[...], c_to_rc(d_out.astype(BF16)))
    pg = norm_grad_cr(
        d_mixed, tile_lanes(gm_ref[...], 2), hat_m_ref[...], spread_cr(rstd_m_ref[...])
    ).astype(BF16)
    pg_out[:256, :] = pg[:, :128]
    pg_out[256:, :] = pg[:, 128:]


def coef_kernel(
    n_ref, mask_ref, dgate_ref, go_ref, pa_ref, ga_ref, pb_ref, gb_ref,
    cg_out, cp_out, wg_out, wp_out, dn_out,
):
    wg = wide_pair(ga_ref[...], gb_ref[...])
    wp = wide_pair(pa_ref[...], pb_ref[...])
    rc = c_to_rc(n_ref[...])
    gate = jax.nn.sigmoid(dot_tn(wg, rc))
    proj = dot_tn(wp, rc)
    scaled = spread8(wide_mask(mask_ref[...])) * gate
    cp_out[...] = scaled
    cg_out[...] = scaled * (1.0 - gate) * proj
    wg_out[...] = wg
    wp_out[...] = wp
    dn_out[...] = dot(go_ref[...], dgate_ref[...])


def triangle_kernel(pg_ref, a_ref, b_ref, out_ref):
    tiles = pg_ref[...].astype(F32).reshape(8, 2, 4, 8, 128)
    blocks = [
        v.reshape(64, 128)
        for m in range(4)
        for v in pair_up(tiles[:, 0, m].reshape(64, 128), tiles[:, 1, m].reshape(64, 128))
    ]
    pg = jnp.concatenate(swap_in(blocks), axis=0).astype(BF16)
    left = dot(pg, b_ref[...]).astype(BF16)
    right = dot_tn(dot(pg, natural_rows()).astype(BF16), a_ref[...]).astype(BF16)
    order = sides_first()
    rows = [
        dot_tn(order, jnp.concatenate([left[q * 64 : q * 64 + 64], right[q * 64 : q * 64 + 64]], axis=0))
        for q in range(4)
    ]
    cols = [v.reshape(16, 8, 128) for v in swap_out(rows)]
    out_ref[...] = jnp.stack(cols, axis=1).reshape(1024, 128).astype(BF16)


def finish_kernel(lr_ref, cg_ref, cp_ref, wg_ref, wp_ref, dn_ref, x_ref, du_ref, gain_ref, out_ref):
    grad = jnp.concatenate([lr_ref[:512, :], lr_ref[512:, :]], axis=1).astype(F32)
    d_gate = (grad * cg_ref[...]).astype(BF16)
    d_proj = (grad * cp_ref[...]).astype(BF16)
    d_normed = rc_to_c(dot(wg_ref[...], d_gate) + dot(wp_ref[...], d_proj)) + dn_ref[...]
    hat, rstd = hat_c(x_ref[...].astype(F32))
    grad_x = norm_grad_c(d_normed, tile_lanes(gain_ref[...], 8), hat, rstd) + du_ref[...]
    out_ref[...] = dot_tn(grad_x.astype(BF16), eye64()).astype(BF16).reshape(2, 16, 32, 64)


def main_kernel(mine_ref, other_ref, wq_ref, out_ref):
    grad = (mine_ref[...] + other_ref[...]).astype(BF16)
    out_ref[...] = dot_tn(grad, wq_ref[...]).astype(BF16).reshape(16, 32, 128)


def call(kernel, outs, *args, flops=0):
    shapes = [jax.ShapeDtypeStruct(s, t) for s, t in outs]
    nbytes = sum(a.size * a.dtype.itemsize for a in args)
    return pl.pallas_call(
        kernel,
        out_shape=shapes,
        in_specs=[pl.BlockSpec(memory_space=pltpu.VMEM)] * len(args),
        out_specs=[pl.BlockSpec(memory_space=pltpu.VMEM)] * len(shapes),
        compiler_params=pltpu.CompilerParams(vmem_limit_bytes=24 * 1024 * 1024),
        cost_estimate=pl.CostEstimate(flops=flops, bytes_accessed=nbytes, transcendentals=0),
    )(*args)


def call_copying(kernel, outs, *args):
    shapes = [jax.ShapeDtypeStruct(s, t) for s, t in outs]
    return pl.pallas_call(
        kernel,
        out_shape=shapes,
        in_specs=[pl.BlockSpec(memory_space=pl.ANY)] * len(args),
        out_specs=[pl.BlockSpec(memory_space=pltpu.VMEM)] * len(shapes),
        scratch_shapes=[pltpu.VMEM(a.shape, a.dtype) for a in args]
        + [pltpu.SemaphoreType.DMA((len(args),))],
        compiler_params=pltpu.CompilerParams(vmem_limit_bytes=24 * 1024 * 1024),
    )(*[pltpu.with_memory_space_constraint(a, pltpu.HBM) for a in args])


def exchange(v):
    return lax.ppermute(v, "tmpl", [(0, 1), (1, 0)])


def spread_chunks(v, rows):
    v = lax.all_to_all(v.reshape(128, rows, 128), GROUP, 0, 0, axis_index_groups=[ORDER], tiled=True)
    return v.reshape(128 * rows, 128)


def body(
    template_pair, template_mask, pair_mask, main_pair, update_cotangent,
    gain_in, proj_a, gate_a, proj_b, gate_b, gain_mid, proj_out, gate_out, gain_final,
    key_weight, value_weight, query_weight, output_weight,
):
    gi, gm, gf = gain_in.reshape(1, 64), gain_mid.reshape(1, 64), gain_final.reshape(1, 64)
    sides, x, normed, gat, query, grad_out, wide, kv, gm_wide, gf_wide, gi_wide, absent = call_copying(
        front_kernel,
        [
            ((1024, 128), BF16), ((64, 1024), BF16), ((64, 1024), BF16), ((64, 1024), F32),
            ((64, 512), BF16), ((64, 512), F32), ((256, 256), BF16), ((64, 128), BF16),
            ((256, 128), F32), ((64, 128), F32), ((64, 128), F32), ((8, 1024), F32),
        ],
        template_pair, pair_mask, gi, proj_a, gate_a, proj_b, gate_b, gate_out, main_pair,
        update_cotangent, query_weight.T, output_weight, proj_out, key_weight, value_weight, gm, gf,
        template_mask.reshape(1, 2),
    )
    sides = spread_chunks(sides, 8)
    prod, a, b = call(
        product_kernel, [((512, 128), BF16), ((256, 256), BF16), ((256, 256), BF16)], sides
    )
    prod = spread_chunks(prod, 4)
    stat, weights, along, key, hat_m, rstd_m, out, hat_f, rstd_f = call(
        score_kernel,
        [
            ((2, 4, 512), F32), ((4, 1024), F32), ((4, 1024), F32), ((64, 1024), BF16),
            ((256, 256), F32), ((8, 256), F32), ((64, 1024), F32), ((64, 1024), F32), ((1, 1024), F32),
        ],
        x, prod, gat, query, grad_out, absent, gm_wide, gf_wide, wide, kv,
    )
    other = exchange(stat)
    pg, query_sum, d_updated, d_gate = call(
        grad_kernel,
        [((512, 128), BF16), ((64, 512), F32), ((64, 1024), F32), ((64, 1024), BF16)],
        gat, query, grad_out, key, weights, along, stat, other,
        gm_wide, gf_wide, wide, kv, hat_m, rstd_m, out, hat_f, rstd_f,
    )
    cg, cp, wg, wp, dn = call(
        coef_kernel,
        [
            ((512, 256), F32), ((512, 256), F32), ((256, 512), BF16), ((256, 512), BF16),
            ((64, 1024), F32),
        ],
        normed, pair_mask, d_gate, gate_out, proj_a, gate_a, proj_b, gate_b,
    )
    pg = spread_chunks(pg, 4)
    (grads,) = call(triangle_kernel, [((1024, 128), BF16)], pg, a, b)
    query_other = exchange(query_sum)
    (main_grad,) = call(main_kernel, [((16, 32, 128), BF16)], query_sum, query_other, query_weight.T)
    grads = spread_chunks(grads, 8)
    (pair_grad,) = call(
        finish_kernel, [((2, 16, 32, 64), BF16)], grads, cg, cp, wg, wp, dn, x, d_updated, gi_wide
    )
    return (pair_grad, main_grad)


def solution(mesh):
    pixel = P("row", "col", None)
    placed = (
        P("tmpl", "row", "col", None), P("tmpl"), P("row", "col"), pixel, pixel,
    ) + (P(),) * 13
    return jax.shard_map(
        body,
        mesh=mesh,
        in_specs=placed,
        out_specs=(P("tmpl", "row", "col", None), pixel),
        check_vma=False,
    )
```

```python
import functools
import math

import jax
import jax.numpy as jnp
from jax import lax
from jax.experimental import pallas as pl
from jax.experimental.pallas import tpu as pltpu
from jax.sharding import PartitionSpec as P

EPS = 1e-05
F32 = jnp.float32
BF16 = jnp.bfloat16
HEADS = 4
HEAD_DIM = 16
SCALE = 1.0 / math.sqrt(HEAD_DIM)
GROUP = ("row", "col")
TURN = 12
SIDE_BLOCKS = [(s, side, r) for s in range(2) for side in range(2) for r in range(4)]
PIXEL_ROWS = [4 * q + r for r in range(4) for q in range(4)]
ORDER = [p ^ (8 * TURN) for p in range(128)]


def iota(shape, axis):
    return lax.broadcasted_iota(jnp.int32, shape, axis)


def shr(v, n):
    return lax.shift_right_logical(v, jnp.full(v.shape, n, jnp.int32))


def onehot(cond):
    return jnp.where(cond, 1.0, 0.0).astype(BF16)


def dot(a, b):
    return lax.dot_general(a, b, (((1,), (0,)), ((), ())), preferred_element_type=F32)


def dot_nt(a, b):
    return lax.dot_general(a, b, (((1,), (1,)), ((), ())), preferred_element_type=F32)


def dot_tn(a, b):
    return lax.dot_general(a, b, (((0,), (0,)), ((), ())), preferred_element_type=F32)


def eye64():
    return onehot(iota((64, 64), 0) == iota((64, 64), 1))


def c_to_rc(v):
    return jnp.concatenate(
        [
            jnp.concatenate([v[:, s * 512 + r * 128 : s * 512 + r * 128 + 128] for s in range(2)], axis=1)
            for r in range(4)
        ],
        axis=0,
    )


def rc_to_c(v):
    return jnp.concatenate(
        [v[r * 64 : r * 64 + 64, s * 128 : s * 128 + 128] for s in range(2) for r in range(4)], axis=1
    )


def both(v):
    return jnp.concatenate([v, v], axis=1)


def column(gain_row, repeat):
    pick = shr(iota((64 * repeat, 64), 0), repeat // 2) == iota((64 * repeat, 64), 1)
    return jnp.sum(jnp.where(pick, gain_row, 0.0), axis=1, keepdims=True)


def mean_c(v):
    return jnp.mean(v, axis=0, keepdims=True)


def mean_cr(v):
    part = jnp.sum(v.reshape(32, 8, 256), axis=0)
    return (part + pltpu.roll(part, 4, 0)) * (1.0 / 64.0)


def spread_cr(v):
    return jnp.broadcast_to(v[None], (32, 8, 256)).reshape(256, 256)


def hat_c(v):
    centered = v - mean_c(v)
    rstd = lax.rsqrt(mean_c(centered * centered) + EPS)
    return centered * rstd, rstd


def norm_grad_c(grad, gain, hat, rstd):
    scaled = grad * gain
    return rstd * (scaled - mean_c(scaled) - hat * mean_c(scaled * hat))


def hat_cr(v):
    centered = v - spread_cr(mean_cr(v))
    rstd = spread_cr(lax.rsqrt(mean_cr(centered * centered) + EPS))
    return centered * rstd, rstd


def norm_grad_cr(grad, gain, hat, rstd):
    scaled = grad * gain
    return rstd * (scaled - spread_cr(mean_cr(scaled)) - hat * spread_cr(mean_cr(scaled * hat)))


def wide_out(w):
    row, lane = iota((64, 256), 0), iota((64, 256), 1)
    base = dot_tn(w, onehot(row == shr(lane, 2)))
    return jnp.concatenate([jnp.where((lane & 3) == r, base, 0.0) for r in range(4)], axis=0).astype(BF16)


def mask_row(mask):
    tiled = dot(mask.astype(F32).astype(BF16), onehot(iota((32, 128), 0) == (iota((32, 128), 1) & 31)))
    i, lane = iota((16, 128), 0), iota((16, 128), 1)
    tiled = jnp.where(shr(i, 2) == shr(lane, 5), tiled, 0.0).astype(BF16)
    rows = dot(onehot((iota((8, 16), 0) & 3) == (iota((8, 16), 1) & 3)), tiled)
    return both(jnp.concatenate([rows[r : r + 1] for r in range(4)], axis=1))


def swap_groups(four):
    lane = iota(four[0].shape, 1)
    for bit in (1, 2):
        low = (lane & (32 * bit)) == 0
        out = []
        for a in range(4):
            if a & bit == 0:
                out.append(jnp.where(low, four[a], pltpu.roll(four[a ^ bit], 32 * bit, 1)))
            else:
                out.append(jnp.where(low, pltpu.roll(four[a ^ bit], 128 - 32 * bit, 1), four[a]))
        four = out
    return four


def swap_in(blocks):
    lo, hi = swap_groups(blocks[:4]), swap_groups(blocks[4:])
    return [jnp.concatenate([lo[q], hi[q]], axis=1) for q in range(4)]


def swap_out(rows):
    return swap_groups([v[:, :128] for v in rows]) + swap_groups([v[:, 128:] for v in rows])


def pair_up(even, odd):
    even, odd = even.reshape(8, 8, 128), odd.reshape(8, 8, 128)
    top = iota(even.shape, 1) < 4
    return jnp.where(top, even, pltpu.roll(odd, 4, 1)), jnp.where(top, pltpu.roll(even, 4, 1), odd)


def turn(v):
    return jnp.concatenate([v[n ^ TURN : (n ^ TURN) + 4] for n in range(0, 16, 4)], axis=0)


def front_kernel(
    x_hbm, mask_hbm, gi_hbm, pa_hbm, ga_hbm, pb_hbm, gb_hbm, go_hbm, main_hbm, cot_hbm, wq_hbm, wo_hbm,
    po_hbm, kw_hbm, vw_hbm, gm_hbm, gf_hbm, present_hbm,
    out_ref, x_out, n_out, gat_out, q_out, g_out, wide_out_ref, kv_out, gm_out, gf_out, gi_out, absent_out, sides_out, mask_out,
    x_ref, mask_ref, gi_ref, pa_ref, ga_ref, pb_ref, gb_ref, go_ref, main_ref, cot_ref, wq_ref, wo_ref,
    po_ref, kw_ref, vw_ref, gm_ref, gf_ref, present_ref, tiles_ref, sems,
):
    pairs = [
        (x_hbm, x_ref), (gi_hbm, gi_ref), (pa_hbm, pa_ref), (ga_hbm, ga_ref), (pb_hbm, pb_ref),
        (gb_hbm, gb_ref), (mask_hbm, mask_ref), (go_hbm, go_ref), (main_hbm, main_ref), (cot_hbm, cot_ref),
        (wq_hbm, wq_ref), (wo_hbm, wo_ref), (po_hbm, po_ref), (kw_hbm, kw_ref), (vw_hbm, vw_ref),
        (gm_hbm, gm_ref), (gf_hbm, gf_ref), (present_hbm, present_ref),
    ]
    copies = [pltpu.make_async_copy(a, b, sems.at[n]) for n, (a, b) in enumerate(pairs)]
    for copy in copies:
        copy.start()
    for copy in copies[1:7]:
        copy.wait()
    weights = jnp.concatenate([ga_ref[...], gb_ref[...], pa_ref[...], pb_ref[...]], axis=1)
    sides_out[...] = weights
    mask = mask_row(mask_ref[...])
    mask_out[...] = jnp.broadcast_to(mask, (8, 1024))
    copies[0].wait()
    x = dot_nt(eye64(), jnp.concatenate([x_ref[s, i] for s in range(2) for i in PIXEL_ROWS], axis=0))
    hat, _ = hat_c(x)
    gi = column(gi_ref[...], 1)
    normed = (hat * gi).astype(BF16)
    x_out[...] = x.astype(BF16)
    n_out[...] = normed
    both_sides = dot_tn(weights, normed)
    both_sides = mask * jax.nn.sigmoid(both_sides[:128]) * both_sides[128:]
    for s, side, r in SIDE_BLOCKS:
        tiles_ref[pl.ds(s * 512 + side * 4 + r, 64, stride=8), :] = both_sides[
            side * 64 : side * 64 + 64, s * 512 + r * 128 : s * 512 + r * 128 + 128
        ]
    out_ref[...] = tiles_ref[...].astype(BF16)
    gi_out[...] = jnp.broadcast_to(gi, (64, 128))
    for copy in copies[7:]:
        copy.wait()
    gat_out[...] = jax.nn.sigmoid(dot_tn(go_ref[...], normed))
    q_out[...] = dot_nt(wq_ref[...], jnp.concatenate([main_ref[i] for i in PIXEL_ROWS], axis=0)).astype(BF16)
    g_out[...] = dot_nt(wo_ref[...], jnp.concatenate([cot_ref[i] for i in PIXEL_ROWS], axis=0))
    wide_out_ref[...] = wide_out(po_ref[...])
    kv_out[...] = jnp.concatenate([kw_ref[...], vw_ref[...]], axis=1)
    gm_out[...] = jnp.broadcast_to(column(gm_ref[...], 4), (256, 128))
    gf_out[...] = jnp.broadcast_to(column(gf_ref[...], 1), (64, 128))
    absent_out[...] = jnp.where(
        jnp.concatenate([jnp.broadcast_to(present_ref[:, s : s + 1], (8, 512)) for s in range(2)], axis=1) > 0,
        0.0, -1e30,
    )


def product_kernel(x_ref, out_ref, a_out, b_out):
    tiles = x_ref[...].astype(F32).reshape(16, 8, 8, 128)
    parts = [v.reshape(16, 8, 256) for v in swap_in([tiles[:, c].reshape(128, 128) for c in range(8)])]
    rolled = [pltpu.roll(v, 4, 1) for v in parts]
    top = iota((16, 8, 256), 1) < 4
    a = [
        jnp.where(top[:8], v.reshape(8, 2, 8, 256)[:, 0], w.reshape(8, 2, 8, 256)[:, 1]).reshape(64, 256)
        for v, w in zip(parts, rolled)
    ]
    b = [turn(jnp.where(top, rolled[q], parts[q + 1])) for q in (0, 2)]
    a = jnp.concatenate(a, axis=0).astype(BF16)
    b = jnp.stack(b, axis=1).reshape(256, 256).astype(BF16)
    a_out[...] = a
    b_out[...] = b
    prod = dot_nt(a, b)
    cols = swap_out([prod[q * 64 : q * 64 + 64] for q in range(4)])
    pairs = [jnp.stack(pair_up(cols[c], cols[c + 1]), axis=1) for c in range(0, 8, 2)]
    out_ref[...] = jnp.stack(pairs, axis=2).reshape(512, 128).astype(BF16)


def heads_sum(v):
    return jnp.sum(v.reshape(HEADS, HEAD_DIM, v.shape[-1]), axis=1)


def heads_spread(v):
    return jnp.broadcast_to(v[:, None, :], (HEADS, HEAD_DIM, v.shape[-1])).reshape(64, v.shape[-1])


def tile_lanes(v, n):
    return jnp.concatenate([v] * n, axis=1)


def score_kernel(
    x_ref, prod_ref, gat_ref, q_ref, g_ref, absent_ref, gm_ref, gf_ref, wide_ref, kv_ref,
    stat_out, w_out, along_out, key_out, hat_m_out, rstd_m_out, out_out, hat_f_out, rstd_f_out,
):
    prod = jnp.concatenate([prod_ref[:256, :], prod_ref[256:, :]], axis=1).astype(F32)
    centered = prod - spread_cr(mean_cr(prod))
    rstd_m = lax.rsqrt(mean_cr(centered * centered) + EPS)
    hat_m = centered * spread_cr(rstd_m)
    out = rc_to_c(dot(wide_ref[...], (hat_m * tile_lanes(gm_ref[...], 2)).astype(BF16)))
    hat_f, rstd_f = hat_c(x_ref[...].astype(F32) + gat_ref[...] * out)
    hat_m_out[...] = hat_m
    rstd_m_out[...] = rstd_m
    out_out[...] = out
    hat_f_out[...] = hat_f
    rstd_f_out[...] = rstd_f
    final = (hat_f * tile_lanes(gf_ref[...], 8)).astype(BF16)
    key_val = dot_tn(kv_ref[...], final).astype(BF16)
    key, val = key_val[:64], key_val[64:]
    key_out[...] = key
    score = heads_sum(both(q_ref[...].astype(F32)) * key.astype(F32)) * SCALE
    along = heads_sum(both(g_ref[...]) * val.astype(F32))
    score = jnp.where(absent_ref[:4, :] < 0.0, -1e30, score)
    s0, s1 = score[:, :512], score[:, 512:]
    top = jnp.maximum(s0, s1)
    e0, e1 = jnp.exp(s0 - top), jnp.exp(s1 - top)
    total = e0 + e1
    w0, w1 = e0 / total, e1 / total
    w_out[...] = jnp.concatenate([w0, w1], axis=1)
    along_out[...] = along
    stat_out[0] = top + jnp.log(total)
    stat_out[1] = w0 * along[:, :512] + w1 * along[:, 512:]


def grad_kernel(
    gat_ref, q_ref, g_ref, key_ref, w_ref, along_ref, mine_ref, other_ref,
    gm_ref, gf_ref, wide_ref, kv_ref, hat_m_ref, rstd_m_ref, out_ref, hat_f_ref, rstd_f_ref,
    pg_out, qsum_out, du_out, dgate_out,
):
    share = jax.nn.sigmoid(mine_ref[0] - other_ref[0])
    average = share * mine_ref[1] + jax.nn.sigmoid(other_ref[0] - mine_ref[0]) * other_ref[1]
    weights = w_ref[...] * both(share)
    slope = weights * (along_ref[...] - both(average))
    slope_wide = heads_spread(slope)
    part = slope_wide * key_ref[...].astype(F32)
    qsum_out[...] = (part[:, :512] + part[:, 512:]) * SCALE
    key_grad = (slope_wide * both(q_ref[...].astype(F32) * SCALE)).astype(BF16)
    value_grad = (heads_spread(weights) * both(g_ref[...])).astype(BF16)
    d_final = dot(kv_ref[...], jnp.concatenate([key_grad, value_grad], axis=0))
    d_updated = norm_grad_c(d_final, tile_lanes(gf_ref[...], 8), hat_f_ref[...], rstd_f_ref[...])
    gat = gat_ref[...]
    du_out[...] = d_updated
    d_out = d_updated * gat
    dgate_out[...] = (d_out * out_ref[...] * (1.0 - gat)).astype(BF16)
    d_mixed = dot_tn(wide_ref[...], c_to_rc(d_out.astype(BF16)))
    pg = norm_grad_cr(
        d_mixed, tile_lanes(gm_ref[...], 2), hat_m_ref[...], spread_cr(rstd_m_ref[...])
    ).astype(BF16)
    pg_out[:256, :] = pg[:, :128]
    pg_out[256:, :] = pg[:, 128:]


def coef_kernel(
    n_ref, x_ref, mask_ref, dgate_ref, go_ref, sides_ref, cg_out, cp_out, hat_out, rstd_out, dn_out
):
    both_sides = dot_tn(sides_ref[...], n_ref[...])
    gate = jax.nn.sigmoid(both_sides[:128])
    scaled = mask_ref[:1, :] * gate
    cp_out[...] = scaled
    cg_out[...] = scaled * (1.0 - gate) * both_sides[128:]
    hat_out[...], rstd_out[...] = hat_c(x_ref[...].astype(F32))
    dn_out[...] = dot(go_ref[...], dgate_ref[...])


def triangle_kernel(pg_ref, a_ref, b_ref, out_ref):
    tiles = pg_ref[...].astype(F32).reshape(8, 2, 4, 8, 128)
    blocks = [
        v.reshape(64, 128)
        for m in range(4)
        for v in pair_up(tiles[:, 0, m].reshape(64, 128), tiles[:, 1, m].reshape(64, 128))
    ]
    pg = jnp.concatenate(swap_in(blocks), axis=0).astype(BF16)
    left = dot(pg, b_ref[...]).reshape(4, 8, 8, 256)
    right = dot_tn(pg, a_ref[...]).reshape(16, 2, 8, 256)
    top = iota((16, 8, 256), 1) < 4
    rows = []
    for q in range(4):
        upper = jnp.stack([left[q], pltpu.roll(left[q], 4, 1)], axis=1).reshape(16, 8, 256)
        lower = turn(right[:, q // 2])
        lower = lower if q & 1 else pltpu.roll(lower, 4, 1)
        rows.append(jnp.where(top, upper, lower).reshape(128, 256))
    cols = [v.reshape(16, 8, 128) for v in swap_out(rows)]
    out_ref[...] = jnp.stack(cols, axis=1).reshape(1024, 128).astype(BF16)


def finish_kernel(
    lr_ref, cg_ref, cp_ref, sides_ref, dn_ref, hat_ref, rstd_ref, du_ref, gain_ref, out_ref, tiles_ref
):
    tiles_ref[...] = lr_ref[...].astype(F32)
    blocks = [tiles_ref[pl.ds(s * 512 + side * 4 + r, 64, stride=8), :] for s, side, r in SIDE_BLOCKS]
    grad = jnp.concatenate(
        [
            jnp.concatenate([blocks[s * 8 + side * 4 + r] for s in range(2) for r in range(4)], axis=1)
            for side in range(2)
        ],
        axis=0,
    )
    grad = jnp.concatenate([(grad * cg_ref[...]).astype(BF16), (grad * cp_ref[...]).astype(BF16)], axis=0)
    d_normed = dot(sides_ref[...], grad) + dn_ref[...]
    grad_x = norm_grad_c(d_normed, tile_lanes(gain_ref[...], 8), hat_ref[...], rstd_ref[...]) + du_ref[...]
    out = dot_tn(grad_x.astype(BF16), eye64()).astype(BF16)
    for s in range(2):
        for n, i in enumerate(PIXEL_ROWS):
            out_ref[s, i] = out[s * 512 + n * 32 : s * 512 + n * 32 + 32]


def main_kernel(mine_ref, other_ref, wq_ref, out_ref):
    grad = (mine_ref[...] + other_ref[...]).astype(BF16)
    out = dot_tn(grad, wq_ref[...]).astype(BF16)
    for n, i in enumerate(PIXEL_ROWS):
        out_ref[i] = out[n * 32 : n * 32 + 32]


def call(kernel, outs, *args, scratch=()):
    shapes = [jax.ShapeDtypeStruct(s, t) for s, t in outs]
    nbytes = sum(a.size * a.dtype.itemsize for a in args)
    return pl.pallas_call(
        kernel,
        out_shape=shapes,
        in_specs=[pl.BlockSpec(memory_space=pltpu.VMEM)] * len(args),
        out_specs=[pl.BlockSpec(memory_space=pltpu.VMEM)] * len(shapes),
        scratch_shapes=scratch,
        compiler_params=pltpu.CompilerParams(vmem_limit_bytes=24 * 1024 * 1024),
        cost_estimate=pl.CostEstimate(flops=0, bytes_accessed=nbytes, transcendentals=0),
    )(*args)


def call_copying(kernel, outs, *args):
    shapes = [jax.ShapeDtypeStruct(s, t) for s, t in outs]
    return pl.pallas_call(
        kernel,
        out_shape=shapes,
        in_specs=[pl.BlockSpec(memory_space=pl.ANY)] * len(args),
        out_specs=[pl.BlockSpec(memory_space=pltpu.VMEM)] * len(shapes),
        scratch_shapes=[pltpu.VMEM(a.shape, a.dtype) for a in args]
        + [pltpu.VMEM((1024, 128), F32), pltpu.SemaphoreType.DMA((len(args),))],
        compiler_params=pltpu.CompilerParams(vmem_limit_bytes=24 * 1024 * 1024),
    )(*[pltpu.with_memory_space_constraint(a, pltpu.HBM) for a in args])


def exchange(v):
    return lax.ppermute(v, "tmpl", [(0, 1), (1, 0)])


def spread_chunks(v, rows):
    v = lax.all_to_all(v.reshape(128, rows, 128), GROUP, 0, 0, axis_index_groups=[ORDER], tiled=True)
    return v.reshape(128 * rows, 128)


def body(
    template_pair, template_mask, pair_mask, main_pair, update_cotangent,
    gain_in, proj_a, gate_a, proj_b, gate_b, gain_mid, proj_out, gate_out, gain_final,
    key_weight, value_weight, query_weight, output_weight,
):
    gi, gm, gf = gain_in.reshape(1, 64), gain_mid.reshape(1, 64), gain_final.reshape(1, 64)
    sides, x, normed, gat, query, grad_out, wide, kv, gm_wide, gf_wide, gi_wide, absent, side_weights, mask = call_copying(
        front_kernel,
        [
            ((1024, 128), BF16), ((64, 1024), BF16), ((64, 1024), BF16), ((64, 1024), F32),
            ((64, 512), BF16), ((64, 512), F32), ((256, 256), BF16), ((64, 128), BF16),
            ((256, 128), F32), ((64, 128), F32), ((64, 128), F32), ((8, 1024), F32), ((64, 256), BF16), ((8, 1024), F32),
        ],
        template_pair, pair_mask, gi, proj_a, gate_a, proj_b, gate_b, gate_out, main_pair,
        update_cotangent, query_weight.T, output_weight, proj_out, key_weight, value_weight, gm, gf,
        template_mask.reshape(1, 2),
    )
    sides = spread_chunks(sides, 8)
    prod, a, b = call(
        product_kernel, [((512, 128), BF16), ((256, 256), BF16), ((256, 256), BF16)], sides
    )
    prod = spread_chunks(prod, 4)
    stat, weights, along, key, hat_m, rstd_m, out, hat_f, rstd_f = call(
        score_kernel,
        [
            ((2, 4, 512), F32), ((4, 1024), F32), ((4, 1024), F32), ((64, 1024), BF16),
            ((256, 256), F32), ((8, 256), F32), ((64, 1024), F32), ((64, 1024), F32), ((1, 1024), F32),
        ],
        x, prod, gat, query, grad_out, absent, gm_wide, gf_wide, wide, kv,
    )
    other = exchange(stat)
    pg, query_sum, d_updated, d_gate = call(
        grad_kernel,
        [((512, 128), BF16), ((64, 512), F32), ((64, 1024), F32), ((64, 1024), BF16)],
        gat, query, grad_out, key, weights, along, stat, other,
        gm_wide, gf_wide, wide, kv, hat_m, rstd_m, out, hat_f, rstd_f,
    )
    cg, cp, hat, rstd, dn = call(
        coef_kernel,
        [((128, 1024), F32), ((128, 1024), F32), ((64, 1024), F32), ((1, 1024), F32), ((64, 1024), F32)],
        normed, x, mask, d_gate, gate_out, side_weights,
    )
    pg = spread_chunks(pg, 4)
    (grads,) = call(triangle_kernel, [((1024, 128), BF16)], pg, a, b)
    query_other = exchange(query_sum)
    (main_grad,) = call(main_kernel, [((16, 32, 128), BF16)], query_sum, query_other, query_weight.T)
    grads = spread_chunks(grads, 8)
    (pair_grad,) = call(
        finish_kernel, [((2, 16, 32, 64), BF16)],
        grads, cg, cp, side_weights, dn, hat, rstd, d_updated, gi_wide,
        scratch=[pltpu.VMEM((1024, 128), F32)],
    )
    return (pair_grad, main_grad)


def solution(mesh):
    pixel = P("row", "col", None)
    placed = (
        P("tmpl", "row", "col", None), P("tmpl"), P("row", "col"), pixel, pixel,
    ) + (P(),) * 13
    return jax.shard_map(
        body,
        mesh=mesh,
        in_specs=placed,
        out_specs=(P("tmpl", "row", "col", None), pixel),
        check_vma=False,
    )
```

```python
import functools
import math

import jax
import jax.numpy as jnp
from jax import lax
from jax.experimental import pallas as pl
from jax.experimental.pallas import tpu as pltpu
from jax.sharding import PartitionSpec as P

EPS = 1e-05
F32 = jnp.float32
BF16 = jnp.bfloat16
HEADS = 4
HEAD_DIM = 16
SCALE = 1.0 / math.sqrt(HEAD_DIM)
GROUP = ("row", "col")
TURN = 6
SIDE_BLOCKS = [(s, side, r) for s in range(2) for side in range(2) for r in range(4)]
PIXEL_ROWS = [4 * q + r for r in range(4) for q in range(4)]
ORDER = [[(z ^ TURN) * 16 + core * 8 + col for z in range(8) for col in range(8)] for core in range(2)]


def iota(shape, axis):
    return lax.broadcasted_iota(jnp.int32, shape, axis)


def shr(v, n):
    return lax.shift_right_logical(v, jnp.full(v.shape, n, jnp.int32))


def onehot(cond):
    return jnp.where(cond, 1.0, 0.0).astype(BF16)


def dot(a, b):
    return lax.dot_general(a, b, (((1,), (0,)), ((), ())), preferred_element_type=F32)


def dot_nt(a, b):
    return lax.dot_general(a, b, (((1,), (1,)), ((), ())), preferred_element_type=F32)


def dot_tn(a, b):
    return lax.dot_general(a, b, (((0,), (0,)), ((), ())), preferred_element_type=F32)


def eye64():
    return onehot(iota((64, 64), 0) == iota((64, 64), 1))


def c_to_rc(v):
    return jnp.concatenate(
        [
            jnp.concatenate([v[:, s * 512 + r * 128 : s * 512 + r * 128 + 128] for s in range(2)], axis=1)
            for r in range(4)
        ],
        axis=0,
    )


def rc_to_c(v):
    return jnp.concatenate(
        [v[r * 64 : r * 64 + 64, s * 128 : s * 128 + 128] for s in range(2) for r in range(4)], axis=1
    )


def both(v):
    return jnp.concatenate([v, v], axis=1)


def column(gain_row, repeat):
    pick = shr(iota((64 * repeat, 64), 0), repeat // 2) == iota((64 * repeat, 64), 1)
    return jnp.sum(jnp.where(pick, gain_row, 0.0), axis=1, keepdims=True)


def mean_c(v):
    return jnp.mean(v, axis=0, keepdims=True)


def mean_cr(v):
    part = jnp.sum(v.reshape(32, 8, 256), axis=0)
    return (part + pltpu.roll(part, 4, 0)) * (1.0 / 64.0)


def spread_cr(v):
    return jnp.broadcast_to(v[None], (32, 8, 256)).reshape(256, 256)


def hat_c(v):
    centered = v - mean_c(v)
    rstd = lax.rsqrt(mean_c(centered * centered) + EPS)
    return centered * rstd, rstd


def norm_grad_c(grad, gain, hat, rstd):
    scaled = grad * gain
    return rstd * (scaled - mean_c(scaled) - hat * mean_c(scaled * hat))


def hat_cr(v):
    centered = v - spread_cr(mean_cr(v))
    rstd = spread_cr(lax.rsqrt(mean_cr(centered * centered) + EPS))
    return centered * rstd, rstd


def norm_grad_cr(grad, gain, hat, rstd):
    scaled = grad * gain
    return rstd * (scaled - spread_cr(mean_cr(scaled)) - hat * spread_cr(mean_cr(scaled * hat)))


def wide_out(w):
    row, lane = iota((64, 256), 0), iota((64, 256), 1)
    base = dot_tn(w, onehot(row == shr(lane, 2)))
    return jnp.concatenate([jnp.where((lane & 3) == r, base, 0.0) for r in range(4)], axis=0).astype(BF16)


def mask_row(mask):
    tiled = dot(mask.astype(F32).astype(BF16), onehot(iota((32, 128), 0) == (iota((32, 128), 1) & 31)))
    i, lane = iota((16, 128), 0), iota((16, 128), 1)
    tiled = jnp.where(shr(i, 2) == shr(lane, 5), tiled, 0.0).astype(BF16)
    rows = dot(onehot((iota((8, 16), 0) & 3) == (iota((8, 16), 1) & 3)), tiled)
    return both(jnp.concatenate([rows[r : r + 1] for r in range(4)], axis=1))


def swap_groups(four):
    lane = iota(four[0].shape, 1)
    for bit in (1, 2):
        low = (lane & (32 * bit)) == 0
        out = []
        for a in range(4):
            if a & bit == 0:
                out.append(jnp.where(low, four[a], pltpu.roll(four[a ^ bit], 32 * bit, 1)))
            else:
                out.append(jnp.where(low, pltpu.roll(four[a ^ bit], 128 - 32 * bit, 1), four[a]))
        four = out
    return four


def swap_in(blocks):
    lo, hi = swap_groups(blocks[:4]), swap_groups(blocks[4:])
    return [jnp.concatenate([lo[q], hi[q]], axis=1) for q in range(4)]


def swap_out(rows):
    return swap_groups([v[:, :128] for v in rows]) + swap_groups([v[:, 128:] for v in rows])


def pair_up(even, odd):
    top = iota(even.shape, even.ndim - 2) < 4
    axis = even.ndim - 2
    return jnp.where(top, even, pltpu.roll(odd, 4, axis)), jnp.where(top, pltpu.roll(even, 4, axis), odd)


def turn(v):
    return jnp.concatenate([v[n ^ TURN : (n ^ TURN) + 2] for n in range(0, 8, 2)], axis=0)


def by_core(first, second):
    core0 = (lax.axis_index("row") & 1) == 0
    return jnp.where(core0, first, second), jnp.where(core0, second, first)


def front_kernel(
    x_hbm, mask_hbm, gi_hbm, pa_hbm, ga_hbm, pb_hbm, gb_hbm, go_hbm, main_hbm, cot_hbm, wq_hbm, wo_hbm,
    po_hbm, kw_hbm, vw_hbm, gm_hbm, gf_hbm, present_hbm,
    out_ref, x_out, n_out, gat_out, q_out, g_out, wide_out_ref, kv_out, gm_out, gf_out, gi_out, absent_out, sides_out, mask_out,
    x_ref, mask_ref, gi_ref, pa_ref, ga_ref, pb_ref, gb_ref, go_ref, main_ref, cot_ref, wq_ref, wo_ref,
    po_ref, kw_ref, vw_ref, gm_ref, gf_ref, present_ref, tiles_ref, sems,
):
    pairs = [
        (x_hbm, x_ref), (gi_hbm, gi_ref), (pa_hbm, pa_ref), (ga_hbm, ga_ref), (pb_hbm, pb_ref),
        (gb_hbm, gb_ref), (mask_hbm, mask_ref), (go_hbm, go_ref), (main_hbm, main_ref), (cot_hbm, cot_ref),
        (wq_hbm, wq_ref), (wo_hbm, wo_ref), (po_hbm, po_ref), (kw_hbm, kw_ref), (vw_hbm, vw_ref),
        (gm_hbm, gm_ref), (gf_hbm, gf_ref), (present_hbm, present_ref),
    ]
    copies = [pltpu.make_async_copy(a, b, sems.at[n]) for n, (a, b) in enumerate(pairs)]
    for copy in copies:
        copy.start()
    for copy in copies[1:7]:
        copy.wait()
    weights = jnp.concatenate([ga_ref[...], gb_ref[...], pa_ref[...], pb_ref[...]], axis=1)
    sides_out[...] = weights
    mask = mask_row(mask_ref[...])
    mask_out[...] = jnp.broadcast_to(mask, (8, 1024))
    copies[0].wait()
    x = dot_nt(eye64(), jnp.concatenate([x_ref[s, i] for s in range(2) for i in PIXEL_ROWS], axis=0))
    hat, _ = hat_c(x)
    gi = column(gi_ref[...], 1)
    normed = (hat * gi).astype(BF16)
    x_out[...] = x.astype(BF16)
    n_out[...] = normed
    both_sides = dot_tn(weights, normed)
    both_sides = mask * jax.nn.sigmoid(both_sides[:128]) * both_sides[128:]
    for s, side, r in SIDE_BLOCKS:
        tiles_ref[pl.ds(s * 512 + side * 4 + r, 64, stride=8), :] = both_sides[
            side * 64 : side * 64 + 64, s * 512 + r * 128 : s * 512 + r * 128 + 128
        ]
    out_ref[...] = tiles_ref[...].astype(BF16)
    gi_out[...] = jnp.broadcast_to(gi, (64, 128))
    for copy in copies[7:]:
        copy.wait()
    gat_out[...] = jax.nn.sigmoid(dot_tn(go_ref[...], normed))
    q_out[...] = dot_nt(wq_ref[...], jnp.concatenate([main_ref[i] for i in PIXEL_ROWS], axis=0)).astype(BF16)
    g_out[...] = dot_nt(wo_ref[...], jnp.concatenate([cot_ref[i] for i in PIXEL_ROWS], axis=0))
    wide_out_ref[...] = wide_out(po_ref[...])
    kv_out[...] = jnp.concatenate([kw_ref[...], vw_ref[...]], axis=1)
    gm_out[...] = jnp.broadcast_to(column(gm_ref[...], 4), (256, 128))
    gf_out[...] = jnp.broadcast_to(column(gf_ref[...], 1), (64, 128))
    absent_out[...] = jnp.where(
        jnp.concatenate([jnp.broadcast_to(present_ref[:, s : s + 1], (8, 512)) for s in range(2)], axis=1) > 0,
        0.0, -1e30,
    )


def layout_kernel(x_ref, a_out, b_out):
    tiles = x_ref[...].astype(F32).reshape(8, 8, 2, 8, 128)
    parts = [v.reshape(8, 2, 8, 256) for v in swap_in([tiles[:, c].reshape(128, 128) for c in range(8)])]
    rolled = [pltpu.roll(v.reshape(16, 8, 256), 4, 1).reshape(8, 2, 8, 256) for v in parts]
    top = iota((8, 8, 256), 1) < 4
    a, b = [], []
    for e in range(2):
        for v, w in zip(parts, rolled):
            v, w = v[:, e].reshape(4, 2, 8, 256), w[:, e].reshape(4, 2, 8, 256)
            a.append(jnp.where(top[:4], v[:, 0], w[:, 1]).reshape(32, 256))
        half = [turn(jnp.where(top, rolled[q][:, e], parts[q + 1][:, e])) for q in (0, 2)]
        b.append(jnp.stack(half, axis=1).reshape(128, 256))
    a_out[...] = jnp.concatenate(a, axis=0).astype(BF16)
    b_out[...] = jnp.concatenate(b, axis=0).astype(BF16)


def product_kernel(a_ref, own_ref, other_ref, out_ref, b_out):
    prods = []
    for e in range(2):
        own = own_ref[e * 128 : e * 128 + 128, :].reshape(8, 16, 256)
        other = other_ref[e * 128 : e * 128 + 128, :].reshape(8, 16, 256)
        b = jnp.stack(by_core(own, other), axis=1).reshape(256, 256)
        b_out[e * 256 : e * 256 + 256, :] = b
        prods.append(dot_nt(a_ref[e * 128 : e * 128 + 128, :], b))
    rows = [jnp.concatenate([v[q * 32 : q * 32 + 32] for v in prods], axis=0) for q in range(4)]
    pairs = []
    for v in swap_out(rows):
        v = v.reshape(2, 4, 8, 128)
        pairs.append(jnp.stack(pair_up(v[0], v[1]), axis=1).reshape(8, 8, 128))
    out_ref[...] = jnp.stack(pairs, axis=1).reshape(512, 128).astype(BF16)


def heads_sum(v):
    return jnp.sum(v.reshape(HEADS, HEAD_DIM, v.shape[-1]), axis=1)


def heads_spread(v):
    return jnp.broadcast_to(v[:, None, :], (HEADS, HEAD_DIM, v.shape[-1])).reshape(64, v.shape[-1])


def tile_lanes(v, n):
    return jnp.concatenate([v] * n, axis=1)


def score_kernel(
    x_ref, prod_ref, gat_ref, q_ref, g_ref, absent_ref, gm_ref, gf_ref, wide_ref, kv_ref,
    stat_out, w_out, along_out, key_out, hat_m_out, rstd_m_out, out_out, hat_f_out, rstd_f_out,
):
    prod = jnp.concatenate([prod_ref[:256, :], prod_ref[256:, :]], axis=1).astype(F32)
    centered = prod - spread_cr(mean_cr(prod))
    rstd_m = lax.rsqrt(mean_cr(centered * centered) + EPS)
    hat_m = centered * spread_cr(rstd_m)
    out = rc_to_c(dot(wide_ref[...], (hat_m * tile_lanes(gm_ref[...], 2)).astype(BF16)))
    hat_f, rstd_f = hat_c(x_ref[...].astype(F32) + gat_ref[...] * out)
    hat_m_out[...] = hat_m
    rstd_m_out[...] = rstd_m
    out_out[...] = out
    hat_f_out[...] = hat_f
    rstd_f_out[...] = rstd_f
    final = (hat_f * tile_lanes(gf_ref[...], 8)).astype(BF16)
    key_val = dot_tn(kv_ref[...], final).astype(BF16)
    key, val = key_val[:64], key_val[64:]
    key_out[...] = key
    score = heads_sum(both(q_ref[...].astype(F32)) * key.astype(F32)) * SCALE
    along = heads_sum(both(g_ref[...]) * val.astype(F32))
    score = jnp.where(absent_ref[:4, :] < 0.0, -1e30, score)
    s0, s1 = score[:, :512], score[:, 512:]
    top = jnp.maximum(s0, s1)
    e0, e1 = jnp.exp(s0 - top), jnp.exp(s1 - top)
    total = e0 + e1
    w0, w1 = e0 / total, e1 / total
    w_out[...] = jnp.concatenate([w0, w1], axis=1)
    along_out[...] = along
    stat_out[0] = top + jnp.log(total)
    stat_out[1] = w0 * along[:, :512] + w1 * along[:, 512:]


def grad_kernel(
    gat_ref, q_ref, g_ref, key_ref, w_ref, along_ref, mine_ref, other_ref,
    gm_ref, gf_ref, wide_ref, kv_ref, hat_m_ref, rstd_m_ref, out_ref, hat_f_ref, rstd_f_ref,
    pg_out, qsum_out, du_out, dgate_out,
):
    share = jax.nn.sigmoid(mine_ref[0] - other_ref[0])
    average = share * mine_ref[1] + jax.nn.sigmoid(other_ref[0] - mine_ref[0]) * other_ref[1]
    weights = w_ref[...] * both(share)
    slope = weights * (along_ref[...] - both(average))
    slope_wide = heads_spread(slope)
    part = slope_wide * key_ref[...].astype(F32)
    qsum_out[...] = (part[:, :512] + part[:, 512:]) * SCALE
    key_grad = (slope_wide * both(q_ref[...].astype(F32) * SCALE)).astype(BF16)
    value_grad = (heads_spread(weights) * both(g_ref[...])).astype(BF16)
    d_final = dot(kv_ref[...], jnp.concatenate([key_grad, value_grad], axis=0))
    d_updated = norm_grad_c(d_final, tile_lanes(gf_ref[...], 8), hat_f_ref[...], rstd_f_ref[...])
    gat = gat_ref[...]
    du_out[...] = d_updated
    d_out = d_updated * gat
    dgate_out[...] = (d_out * out_ref[...] * (1.0 - gat)).astype(BF16)
    d_mixed = dot_tn(wide_ref[...], c_to_rc(d_out.astype(BF16)))
    pg = norm_grad_cr(
        d_mixed, tile_lanes(gm_ref[...], 2), hat_m_ref[...], spread_cr(rstd_m_ref[...])
    ).astype(BF16)
    pg_out[:256, :] = pg[:, :128]
    pg_out[256:, :] = pg[:, 128:]


def coef_kernel(
    n_ref, x_ref, mask_ref, dgate_ref, go_ref, sides_ref, cg_out, cp_out, hat_out, rstd_out, dn_out
):
    both_sides = dot_tn(sides_ref[...], n_ref[...])
    gate = jax.nn.sigmoid(both_sides[:128])
    scaled = mask_ref[:1, :] * gate
    cp_out[...] = scaled
    cg_out[...] = scaled * (1.0 - gate) * both_sides[128:]
    hat_out[...], rstd_out[...] = hat_c(x_ref[...].astype(F32))
    dn_out[...] = dot(go_ref[...], dgate_ref[...])


def right_kernel(pg_ref, a_ref, pg_out, own_out, sent_out):
    tiles = pg_ref[...].astype(F32).reshape(8, 8, 8, 128)
    parts = swap_in([tiles[:, c].reshape(64, 128) for c in range(8)])
    split = [pair_up(v.reshape(4, 2, 8, 256)[:, 0], v.reshape(4, 2, 8, 256)[:, 1]) for v in parts]
    for e in range(2):
        pg = jnp.concatenate([v[e].reshape(32, 256) for v in split], axis=0).astype(BF16)
        pg_out[e * 128 : e * 128 + 128, :] = pg
        right = dot_tn(pg, a_ref[e * 128 : e * 128 + 128, :]).reshape(8, 2, 16, 256)
        own, sent = by_core(right[:, 0], right[:, 1])
        own_out[e * 128 : e * 128 + 128, :] = own.reshape(128, 256)
        sent_out[e * 128 : e * 128 + 128, :] = sent.reshape(128, 256).astype(BF16)


def left_kernel(pg_ref, b_ref, out_ref):
    for e in range(2):
        out_ref[e * 128 : e * 128 + 128, :] = dot(
            pg_ref[e * 128 : e * 128 + 128, :], b_ref[e * 256 : e * 256 + 256, :]
        )


def triangle_kernel(left_ref, own_ref, other_ref, out_ref):
    top = iota((8, 8, 256), 1) < 4
    right = (own_ref[...] + other_ref[...].astype(F32)).reshape(2, 8, 2, 8, 256)
    rows = []
    for q in range(4):
        tiles = []
        for e in range(2):
            left = left_ref[e * 128 + q * 32 : e * 128 + q * 32 + 32, :].reshape(4, 8, 256)
            upper = jnp.stack([left, pltpu.roll(left, 4, 1)], axis=1).reshape(8, 8, 256)
            lower = turn(right[e, :, q // 2])
            lower = lower if q & 1 else pltpu.roll(lower, 4, 1)
            tiles.append(jnp.where(top, upper, lower))
        rows.append(jnp.stack(tiles, axis=1).reshape(128, 256))
    cols = [v.reshape(8, 2, 8, 128) for v in swap_out(rows)]
    out_ref[...] = jnp.stack(cols, axis=1).reshape(1024, 128).astype(BF16)


def finish_kernel(
    lr_ref, cg_ref, cp_ref, sides_ref, dn_ref, hat_ref, rstd_ref, du_ref, gain_ref, out_ref, tiles_ref
):
    tiles_ref[...] = lr_ref[...].astype(F32)
    blocks = [tiles_ref[pl.ds(s * 512 + side * 4 + r, 64, stride=8), :] for s, side, r in SIDE_BLOCKS]
    grad = jnp.concatenate(
        [
            jnp.concatenate([blocks[s * 8 + side * 4 + r] for s in range(2) for r in range(4)], axis=1)
            for side in range(2)
        ],
        axis=0,
    )
    grad = jnp.concatenate([(grad * cg_ref[...]).astype(BF16), (grad * cp_ref[...]).astype(BF16)], axis=0)
    d_normed = dot(sides_ref[...], grad) + dn_ref[...]
    grad_x = norm_grad_c(d_normed, tile_lanes(gain_ref[...], 8), hat_ref[...], rstd_ref[...]) + du_ref[...]
    out = dot_tn(grad_x.astype(BF16), eye64()).astype(BF16)
    for s in range(2):
        for n, i in enumerate(PIXEL_ROWS):
            out_ref[s, i] = out[s * 512 + n * 32 : s * 512 + n * 32 + 32]


def main_kernel(mine_ref, other_ref, wq_ref, out_ref):
    grad = (mine_ref[...] + other_ref[...]).astype(BF16)
    out = dot_tn(grad, wq_ref[...]).astype(BF16)
    for n, i in enumerate(PIXEL_ROWS):
        out_ref[i] = out[n * 32 : n * 32 + 32]


def call(kernel, outs, *args, scratch=()):
    shapes = [jax.ShapeDtypeStruct(s, t) for s, t in outs]
    nbytes = sum(a.size * a.dtype.itemsize for a in args)
    return pl.pallas_call(
        kernel,
        out_shape=shapes,
        in_specs=[pl.BlockSpec(memory_space=pltpu.VMEM)] * len(args),
        out_specs=[pl.BlockSpec(memory_space=pltpu.VMEM)] * len(shapes),
        scratch_shapes=scratch,
        compiler_params=pltpu.CompilerParams(vmem_limit_bytes=24 * 1024 * 1024),
        cost_estimate=pl.CostEstimate(flops=0, bytes_accessed=nbytes, transcendentals=0),
    )(*args)


def call_copying(kernel, outs, *args):
    shapes = [jax.ShapeDtypeStruct(s, t) for s, t in outs]
    return pl.pallas_call(
        kernel,
        out_shape=shapes,
        in_specs=[pl.BlockSpec(memory_space=pl.ANY)] * len(args),
        out_specs=[pl.BlockSpec(memory_space=pltpu.VMEM)] * len(shapes),
        scratch_shapes=[pltpu.VMEM(a.shape, a.dtype) for a in args]
        + [pltpu.VMEM((1024, 128), F32), pltpu.SemaphoreType.DMA((len(args),))],
        compiler_params=pltpu.CompilerParams(vmem_limit_bytes=24 * 1024 * 1024),
    )(*[pltpu.with_memory_space_constraint(a, pltpu.HBM) for a in args])


def exchange(v):
    return lax.ppermute(v, "tmpl", [(0, 1), (1, 0)])


def exchange_cores(v):
    return lax.ppermute(v, "row", [(n, n ^ 1) for n in range(16)])


def spread_chunks(v, rows):
    v = lax.all_to_all(v.reshape(64, rows, 128), GROUP, 0, 0, axis_index_groups=ORDER, tiled=True)
    return v.reshape(64 * rows, 128)


def body(
    template_pair, template_mask, pair_mask, main_pair, update_cotangent,
    gain_in, proj_a, gate_a, proj_b, gate_b, gain_mid, proj_out, gate_out, gain_final,
    key_weight, value_weight, query_weight, output_weight,
):
    gi, gm, gf = gain_in.reshape(1, 64), gain_mid.reshape(1, 64), gain_final.reshape(1, 64)
    sides, x, normed, gat, query, grad_out, wide, kv, gm_wide, gf_wide, gi_wide, absent, side_weights, mask = call_copying(
        front_kernel,
        [
            ((1024, 128), BF16), ((64, 1024), BF16), ((64, 1024), BF16), ((64, 1024), F32),
            ((64, 512), BF16), ((64, 512), F32), ((256, 256), BF16), ((64, 128), BF16),
            ((256, 128), F32), ((64, 128), F32), ((64, 128), F32), ((8, 1024), F32), ((64, 256), BF16), ((8, 1024), F32),
        ],
        template_pair, pair_mask, gi, proj_a, gate_a, proj_b, gate_b, gate_out, main_pair,
        update_cotangent, query_weight.T, output_weight, proj_out, key_weight, value_weight, gm, gf,
        template_mask.reshape(1, 2),
    )
    sides = spread_chunks(sides, 16)
    a, b_own = call(layout_kernel, [((256, 256), BF16), ((256, 256), BF16)], sides)
    b_other = exchange_cores(b_own)
    prod, b = call(product_kernel, [((512, 128), BF16), ((512, 256), BF16)], a, b_own, b_other)
    prod = spread_chunks(prod, 8)
    stat, weights, along, key, hat_m, rstd_m, out, hat_f, rstd_f = call(
        score_kernel,
        [
            ((2, 4, 512), F32), ((4, 1024), F32), ((4, 1024), F32), ((64, 1024), BF16),
            ((256, 256), F32), ((8, 256), F32), ((64, 1024), F32), ((64, 1024), F32), ((1, 1024), F32),
        ],
        x, prod, gat, query, grad_out, absent, gm_wide, gf_wide, wide, kv,
    )
    other = exchange(stat)
    pg, query_sum, d_updated, d_gate = call(
        grad_kernel,
        [((512, 128), BF16), ((64, 512), F32), ((64, 1024), F32), ((64, 1024), BF16)],
        gat, query, grad_out, key, weights, along, stat, other,
        gm_wide, gf_wide, wide, kv, hat_m, rstd_m, out, hat_f, rstd_f,
    )
    cg, cp, hat, rstd, dn = call(
        coef_kernel,
        [((128, 1024), F32), ((128, 1024), F32), ((64, 1024), F32), ((1, 1024), F32), ((64, 1024), F32)],
        normed, x, mask, d_gate, gate_out, side_weights,
    )
    pg = spread_chunks(pg, 8)
    pg, right_own, right_sent = call(
        right_kernel, [((256, 256), BF16), ((256, 256), F32), ((256, 256), BF16)], pg, a
    )
    right_other = exchange_cores(right_sent)
    (left,) = call(left_kernel, [((256, 256), F32)], pg, b)
    (grads,) = call(triangle_kernel, [((1024, 128), BF16)], left, right_own, right_other)
    query_other = exchange(query_sum)
    (main_grad,) = call(main_kernel, [((16, 32, 128), BF16)], query_sum, query_other, query_weight.T)
    grads = spread_chunks(grads, 16)
    (pair_grad,) = call(
        finish_kernel, [((2, 16, 32, 64), BF16)],
        grads, cg, cp, side_weights, dn, hat, rstd, d_updated, gi_wide,
        scratch=[pltpu.VMEM((1024, 128), F32)],
    )
    return (pair_grad, main_grad)


def solution(mesh):
    pixel = P("row", "col", None)
    placed = (
        P("tmpl", "row", "col", None), P("tmpl"), P("row", "col"), pixel, pixel,
    ) + (P(),) * 13
    return jax.shard_map(
        body,
        mesh=mesh,
        in_specs=placed,
        out_specs=(P("tmpl", "row", "col", None), pixel),
        check_vma=False,
    )
```

```python
import functools
import math

import jax
import jax.numpy as jnp
from jax import lax
from jax.experimental import pallas as pl
from jax.experimental.pallas import tpu as pltpu
from jax.sharding import PartitionSpec as P

EPS = 1e-05
F32 = jnp.float32
BF16 = jnp.bfloat16
HEADS = 4
HEAD_DIM = 16
SCALE = 1.0 / math.sqrt(HEAD_DIM)
GROUP = ("row", "col")
TURN = 6
LATER = 11
SIDE_BLOCKS = [(s, side, r) for s in range(2) for side in range(2) for r in range(4)]
PIXEL_ROWS = [4 * q + r for r in range(4) for q in range(4)]
ORDER = [[(z ^ TURN) * 16 + core * 8 + col for z in range(8) for col in range(8)] for core in range(2)]


def iota(shape, axis):
    return lax.broadcasted_iota(jnp.int32, shape, axis)


def shr(v, n):
    return lax.shift_right_logical(v, jnp.full(v.shape, n, jnp.int32))


def onehot(cond):
    return jnp.where(cond, 1.0, 0.0).astype(BF16)


def dot(a, b):
    return lax.dot_general(a, b, (((1,), (0,)), ((), ())), preferred_element_type=F32)


def dot_nt(a, b):
    return lax.dot_general(a, b, (((1,), (1,)), ((), ())), preferred_element_type=F32)


def dot_tn(a, b):
    return lax.dot_general(a, b, (((0,), (0,)), ((), ())), preferred_element_type=F32)


def eye64():
    return onehot(iota((64, 64), 0) == iota((64, 64), 1))


def c_to_rc(v):
    return jnp.concatenate(
        [
            jnp.concatenate([v[:, s * 512 + r * 128 : s * 512 + r * 128 + 128] for s in range(2)], axis=1)
            for r in range(4)
        ],
        axis=0,
    )


def rc_to_c(v):
    return jnp.concatenate(
        [v[r * 64 : r * 64 + 64, s * 128 : s * 128 + 128] for s in range(2) for r in range(4)], axis=1
    )


def both(v):
    return jnp.concatenate([v, v], axis=1)


def column(gain_row, repeat):
    pick = shr(iota((64 * repeat, 64), 0), repeat // 2) == iota((64 * repeat, 64), 1)
    return jnp.sum(jnp.where(pick, gain_row, 0.0), axis=1, keepdims=True)


def mean_c(v):
    return jnp.mean(v, axis=0, keepdims=True)


def mean_cr(v):
    part = jnp.sum(v.reshape(32, 8, 256), axis=0)
    return (part + pltpu.roll(part, 4, 0)) * (1.0 / 64.0)


def spread_cr(v):
    return jnp.broadcast_to(v[None], (32, 8, 256)).reshape(256, 256)


def hat_c(v):
    centered = v - mean_c(v)
    rstd = lax.rsqrt(mean_c(centered * centered) + EPS)
    return centered * rstd, rstd


def norm_grad_c(grad, gain, hat, rstd):
    scaled = grad * gain
    return rstd * (scaled - mean_c(scaled) - hat * mean_c(scaled * hat))


def hat_cr(v):
    centered = v - spread_cr(mean_cr(v))
    rstd = spread_cr(lax.rsqrt(mean_cr(centered * centered) + EPS))
    return centered * rstd, rstd


def norm_grad_cr(grad, gain, hat, rstd):
    scaled = grad * gain
    return rstd * (scaled - spread_cr(mean_cr(scaled)) - hat * spread_cr(mean_cr(scaled * hat)))


def wide_out(w):
    row, lane = iota((64, 256), 0), iota((64, 256), 1)
    base = dot_tn(w, onehot(row == shr(lane, 2)))
    return jnp.concatenate([jnp.where((lane & 3) == r, base, 0.0) for r in range(4)], axis=0).astype(BF16)


def mask_row(mask):
    tiled = dot(mask.astype(F32).astype(BF16), onehot(iota((32, 128), 0) == (iota((32, 128), 1) & 31)))
    i, lane = iota((16, 128), 0), iota((16, 128), 1)
    tiled = jnp.where(shr(i, 2) == shr(lane, 5), tiled, 0.0).astype(BF16)
    rows = dot(onehot((iota((8, 16), 0) & 3) == (iota((8, 16), 1) & 3)), tiled)
    return both(jnp.concatenate([rows[r : r + 1] for r in range(4)], axis=1))


def swap_groups(four):
    lane = iota(four[0].shape, 1)
    for bit in (1, 2):
        low = (lane & (32 * bit)) == 0
        out = []
        for a in range(4):
            if a & bit == 0:
                out.append(jnp.where(low, four[a], pltpu.roll(four[a ^ bit], 32 * bit, 1)))
            else:
                out.append(jnp.where(low, pltpu.roll(four[a ^ bit], 128 - 32 * bit, 1), four[a]))
        four = out
    return four


def swap_in(blocks):
    lo, hi = swap_groups(blocks[:4]), swap_groups(blocks[4:])
    return [jnp.concatenate([lo[q], hi[q]], axis=1) for q in range(4)]


def swap_out(rows):
    return swap_groups([v[:, :128] for v in rows]) + swap_groups([v[:, 128:] for v in rows])


def pair_up(even, odd):
    top = iota(even.shape, even.ndim - 2) < 4
    axis = even.ndim - 2
    return jnp.where(top, even, pltpu.roll(odd, 4, axis)), jnp.where(top, pltpu.roll(even, 4, axis), odd)


def turn(v):
    return jnp.concatenate([v[n ^ TURN : (n ^ TURN) + 2] for n in range(0, 8, 2)], axis=0)


def by_core(first, second):
    core0 = (lax.axis_index("row") & 1) == 0
    return jnp.where(core0, first, second), jnp.where(core0, second, first)


def front_kernel(
    x_hbm, mask_hbm, gi_hbm, pa_hbm, ga_hbm, pb_hbm, gb_hbm, *refs
):
    later, refs = refs[:LATER], refs[LATER:]
    out_ref, x_out, n_out, gi_out, sides_out, mask_out = refs[:6]
    later_out, refs = refs[6 : 6 + LATER], refs[6 + LATER :]
    x_ref, mask_ref, gi_ref, pa_ref, ga_ref, pb_ref, gb_ref, tiles_ref, sems = refs
    pairs = [
        (x_hbm, x_ref), (gi_hbm, gi_ref), (pa_hbm, pa_ref), (ga_hbm, ga_ref), (pb_hbm, pb_ref),
        (gb_hbm, gb_ref), (mask_hbm, mask_ref),
    ] + list(zip(later, later_out))
    copies = [pltpu.make_async_copy(a, b, sems.at[n]) for n, (a, b) in enumerate(pairs)]
    for copy in copies:
        copy.start()
    for copy in copies[1:7]:
        copy.wait()
    weights = jnp.concatenate([ga_ref[...], gb_ref[...], pa_ref[...], pb_ref[...]], axis=1)
    sides_out[...] = weights
    mask = mask_row(mask_ref[...])
    mask_out[...] = jnp.broadcast_to(mask, (8, 1024))
    copies[0].wait()
    x = dot_nt(eye64(), jnp.concatenate([x_ref[s, i] for s in range(2) for i in PIXEL_ROWS], axis=0))
    hat, _ = hat_c(x)
    gi = column(gi_ref[...], 1)
    normed = (hat * gi).astype(BF16)
    x_out[...] = x.astype(BF16)
    n_out[...] = normed
    gi_out[...] = jnp.broadcast_to(gi, (64, 128))
    both_sides = dot_tn(weights, normed)
    both_sides = mask * jax.nn.sigmoid(both_sides[:128]) * both_sides[128:]
    for s, side, r in SIDE_BLOCKS:
        tiles_ref[pl.ds(s * 512 + side * 4 + r, 64, stride=8), :] = both_sides[
            side * 64 : side * 64 + 64, s * 512 + r * 128 : s * 512 + r * 128 + 128
        ]
    out_ref[...] = tiles_ref[...].astype(BF16)
    for copy in copies[7:]:
        copy.wait()


def side_kernel(
    n_ref, go_ref, main_ref, cot_ref, wq_ref, wo_ref, po_ref, kw_ref, vw_ref, gm_ref, gf_ref, present_ref,
    gat_out, q_out, g_out, wide_out_ref, kv_out, gm_out, gf_out, absent_out,
):
    gat_out[...] = jax.nn.sigmoid(dot_tn(go_ref[...], n_ref[...]))
    q_out[...] = dot_nt(wq_ref[...], jnp.concatenate([main_ref[i] for i in PIXEL_ROWS], axis=0)).astype(BF16)
    g_out[...] = dot_nt(wo_ref[...], jnp.concatenate([cot_ref[i] for i in PIXEL_ROWS], axis=0))
    wide_out_ref[...] = wide_out(po_ref[...])
    kv_out[...] = jnp.concatenate([kw_ref[...], vw_ref[...]], axis=1)
    gm_out[...] = jnp.broadcast_to(column(gm_ref[...], 4), (256, 128))
    gf_out[...] = jnp.broadcast_to(column(gf_ref[...], 1), (64, 128))
    absent_out[...] = jnp.where(
        jnp.concatenate([jnp.broadcast_to(present_ref[:, s : s + 1], (8, 512)) for s in range(2)], axis=1) > 0,
        0.0, -1e30,
    )


def layout_kernel(x_ref, a_out, b_out):
    tiles = x_ref[...].astype(F32).reshape(8, 8, 2, 8, 128)
    parts = [v.reshape(8, 2, 8, 256) for v in swap_in([tiles[:, c].reshape(128, 128) for c in range(8)])]
    rolled = [pltpu.roll(v.reshape(16, 8, 256), 4, 1).reshape(8, 2, 8, 256) for v in parts]
    top = iota((8, 8, 256), 1) < 4
    a, b = [], []
    for e in range(2):
        for v, w in zip(parts, rolled):
            v, w = v[:, e].reshape(4, 2, 8, 256), w[:, e].reshape(4, 2, 8, 256)
            a.append(jnp.where(top[:4], v[:, 0], w[:, 1]).reshape(32, 256))
        half = [turn(jnp.where(top, rolled[q][:, e], parts[q + 1][:, e])) for q in (0, 2)]
        b.append(jnp.stack(half, axis=1).reshape(128, 256))
    a_out[...] = jnp.concatenate(a, axis=0).astype(BF16)
    b_out[...] = jnp.concatenate(b, axis=0).astype(BF16)


def product_kernel(a_ref, own_ref, other_ref, out_ref, b_out):
    prods = []
    for e in range(2):
        own = own_ref[e * 128 : e * 128 + 128, :].reshape(8, 16, 256)
        other = other_ref[e * 128 : e * 128 + 128, :].reshape(8, 16, 256)
        b = jnp.stack(by_core(own, other), axis=1).reshape(256, 256)
        b_out[e * 256 : e * 256 + 256, :] = b
        prods.append(dot_nt(a_ref[e * 128 : e * 128 + 128, :], b))
    rows = [jnp.concatenate([v[q * 32 : q * 32 + 32] for v in prods], axis=0) for q in range(4)]
    pairs = []
    for v in swap_out(rows):
        v = v.reshape(2, 4, 8, 128)
        pairs.append(jnp.stack(pair_up(v[0], v[1]), axis=1).reshape(8, 8, 128))
    out_ref[...] = jnp.stack(pairs, axis=1).reshape(512, 128).astype(BF16)


def heads_sum(v):
    return jnp.sum(v.reshape(HEADS, HEAD_DIM, v.shape[-1]), axis=1)


def heads_spread(v):
    return jnp.broadcast_to(v[:, None, :], (HEADS, HEAD_DIM, v.shape[-1])).reshape(64, v.shape[-1])


def tile_lanes(v, n):
    return jnp.concatenate([v] * n, axis=1)


def score_kernel(
    x_ref, prod_ref, gat_ref, q_ref, g_ref, absent_ref, gm_ref, gf_ref, wide_ref, kv_ref,
    stat_out, w_out, along_out, key_out, hat_m_out, rstd_m_out, out_out, hat_f_out, rstd_f_out,
):
    prod = jnp.concatenate([prod_ref[:256, :], prod_ref[256:, :]], axis=1).astype(F32)
    centered = prod - spread_cr(mean_cr(prod))
    rstd_m = lax.rsqrt(mean_cr(centered * centered) + EPS)
    hat_m = centered * spread_cr(rstd_m)
    out = rc_to_c(dot(wide_ref[...], (hat_m * tile_lanes(gm_ref[...], 2)).astype(BF16)))
    hat_f, rstd_f = hat_c(x_ref[...].astype(F32) + gat_ref[...] * out)
    hat_m_out[...] = hat_m
    rstd_m_out[...] = rstd_m
    out_out[...] = out
    hat_f_out[...] = hat_f
    rstd_f_out[...] = rstd_f
    final = (hat_f * tile_lanes(gf_ref[...], 8)).astype(BF16)
    key_val = dot_tn(kv_ref[...], final).astype(BF16)
    key, val = key_val[:64], key_val[64:]
    key_out[...] = key
    score = heads_sum(both(q_ref[...].astype(F32)) * key.astype(F32)) * SCALE
    along = heads_sum(both(g_ref[...]) * val.astype(F32))
    score = jnp.where(absent_ref[:4, :] < 0.0, -1e30, score)
    s0, s1 = score[:, :512], score[:, 512:]
    top = jnp.maximum(s0, s1)
    e0, e1 = jnp.exp(s0 - top), jnp.exp(s1 - top)
    total = e0 + e1
    w0, w1 = e0 / total, e1 / total
    w_out[...] = jnp.concatenate([w0, w1], axis=1)
    along_out[...] = along
    stat_out[0] = top + jnp.log(total)
    stat_out[1] = w0 * along[:, :512] + w1 * along[:, 512:]


def grad_kernel(
    gat_ref, q_ref, g_ref, key_ref, w_ref, along_ref, mine_ref, other_ref,
    gm_ref, gf_ref, wide_ref, kv_ref, hat_m_ref, rstd_m_ref, hat_f_ref, rstd_f_ref,
    pg_out, qsum_out, du_out,
):
    share = jax.nn.sigmoid(mine_ref[0] - other_ref[0])
    average = share * mine_ref[1] + jax.nn.sigmoid(other_ref[0] - mine_ref[0]) * other_ref[1]
    weights = w_ref[...] * both(share)
    slope = weights * (along_ref[...] - both(average))
    slope_wide = heads_spread(slope)
    part = slope_wide * key_ref[...].astype(F32)
    qsum_out[...] = (part[:, :512] + part[:, 512:]) * SCALE
    key_grad = (slope_wide * both(q_ref[...].astype(F32) * SCALE)).astype(BF16)
    value_grad = (heads_spread(weights) * both(g_ref[...])).astype(BF16)
    d_final = dot(kv_ref[...], jnp.concatenate([key_grad, value_grad], axis=0))
    d_updated = norm_grad_c(d_final, tile_lanes(gf_ref[...], 8), hat_f_ref[...], rstd_f_ref[...])
    gat = gat_ref[...]
    du_out[...] = d_updated
    d_mixed = dot_tn(wide_ref[...], c_to_rc((d_updated * gat).astype(BF16)))
    pg = norm_grad_cr(
        d_mixed, tile_lanes(gm_ref[...], 2), hat_m_ref[...], spread_cr(rstd_m_ref[...])
    ).astype(BF16)
    pg_out[:256, :] = pg[:, :128]
    pg_out[256:, :] = pg[:, 128:]


def coef_kernel(
    n_ref, x_ref, mask_ref, gat_ref, out_ref, du_ref, go_ref, sides_ref, cg_out, cp_out, hat_out, rstd_out, dn_out
):
    both_sides = dot_tn(sides_ref[...], n_ref[...])
    gate = jax.nn.sigmoid(both_sides[:128])
    scaled = mask_ref[:1, :] * gate
    cp_out[...] = scaled
    cg_out[...] = scaled * (1.0 - gate) * both_sides[128:]
    hat_out[...], rstd_out[...] = hat_c(x_ref[...].astype(F32))
    gat = gat_ref[...]
    d_gate = (du_ref[...] * gat * out_ref[...] * (1.0 - gat)).astype(BF16)
    dn_out[...] = dot(go_ref[...], d_gate)


def right_kernel(pg_ref, a_ref, pg_out, own_out, sent_out):
    tiles = pg_ref[...].astype(F32).reshape(8, 8, 8, 128)
    parts = swap_in([tiles[:, c].reshape(64, 128) for c in range(8)])
    split = [pair_up(v.reshape(4, 2, 8, 256)[:, 0], v.reshape(4, 2, 8, 256)[:, 1]) for v in parts]
    for e in range(2):
        pg = jnp.concatenate([v[e].reshape(32, 256) for v in split], axis=0).astype(BF16)
        pg_out[e * 128 : e * 128 + 128, :] = pg
        right = dot_tn(pg, a_ref[e * 128 : e * 128 + 128, :]).reshape(8, 2, 16, 256)
        own, sent = by_core(right[:, 0], right[:, 1])
        own_out[e * 128 : e * 128 + 128, :] = own.reshape(128, 256)
        sent_out[e * 128 : e * 128 + 128, :] = sent.reshape(128, 256).astype(BF16)


def left_kernel(pg_ref, b_ref, out_ref):
    for e in range(2):
        out_ref[e * 128 : e * 128 + 128, :] = dot(
            pg_ref[e * 128 : e * 128 + 128, :], b_ref[e * 256 : e * 256 + 256, :]
        )


def triangle_kernel(left_ref, own_ref, other_ref, out_ref):
    top = iota((8, 8, 256), 1) < 4
    right = (own_ref[...] + other_ref[...].astype(F32)).reshape(2, 8, 2, 8, 256)
    rows = []
    for q in range(4):
        tiles = []
        for e in range(2):
            left = left_ref[e * 128 + q * 32 : e * 128 + q * 32 + 32, :].reshape(4, 8, 256)
            upper = jnp.stack([left, pltpu.roll(left, 4, 1)], axis=1).reshape(8, 8, 256)
            lower = turn(right[e, :, q // 2])
            lower = lower if q & 1 else pltpu.roll(lower, 4, 1)
            tiles.append(jnp.where(top, upper, lower))
        rows.append(jnp.stack(tiles, axis=1).reshape(128, 256))
    cols = [v.reshape(8, 2, 8, 128) for v in swap_out(rows)]
    out_ref[...] = jnp.stack(cols, axis=1).reshape(1024, 128).astype(BF16)


def finish_kernel(
    lr_ref, cg_ref, cp_ref, sides_ref, dn_ref, hat_ref, rstd_ref, du_ref, gain_ref, out_ref, tiles_ref
):
    tiles_ref[...] = lr_ref[...].astype(F32)
    blocks = [tiles_ref[pl.ds(s * 512 + side * 4 + r, 64, stride=8), :] for s, side, r in SIDE_BLOCKS]
    grad = jnp.concatenate(
        [
            jnp.concatenate([blocks[s * 8 + side * 4 + r] for s in range(2) for r in range(4)], axis=1)
            for side in range(2)
        ],
        axis=0,
    )
    grad = jnp.concatenate([(grad * cg_ref[...]).astype(BF16), (grad * cp_ref[...]).astype(BF16)], axis=0)
    d_normed = dot(sides_ref[...], grad) + dn_ref[...]
    grad_x = norm_grad_c(d_normed, tile_lanes(gain_ref[...], 8), hat_ref[...], rstd_ref[...]) + du_ref[...]
    out = dot_tn(grad_x.astype(BF16), eye64()).astype(BF16)
    for s in range(2):
        for n, i in enumerate(PIXEL_ROWS):
            out_ref[s, i] = out[s * 512 + n * 32 : s * 512 + n * 32 + 32]


def main_kernel(mine_ref, other_ref, wq_ref, out_ref):
    grad = (mine_ref[...] + other_ref[...]).astype(BF16)
    out = dot_tn(grad, wq_ref[...]).astype(BF16)
    for n, i in enumerate(PIXEL_ROWS):
        out_ref[i] = out[n * 32 : n * 32 + 32]


def call(kernel, outs, *args, scratch=()):
    shapes = [jax.ShapeDtypeStruct(s, t) for s, t in outs]
    nbytes = sum(a.size * a.dtype.itemsize for a in args)
    return pl.pallas_call(
        kernel,
        out_shape=shapes,
        in_specs=[pl.BlockSpec(memory_space=pltpu.VMEM)] * len(args),
        out_specs=[pl.BlockSpec(memory_space=pltpu.VMEM)] * len(shapes),
        scratch_shapes=scratch,
        compiler_params=pltpu.CompilerParams(vmem_limit_bytes=24 * 1024 * 1024),
        cost_estimate=pl.CostEstimate(flops=0, bytes_accessed=nbytes, transcendentals=0),
    )(*args)


def call_copying(kernel, outs, now, later):
    shapes = [jax.ShapeDtypeStruct(s, t) for s, t in outs]
    shapes += [jax.ShapeDtypeStruct(a.shape, a.dtype) for a in later]
    args = now + later
    return pl.pallas_call(
        kernel,
        out_shape=shapes,
        in_specs=[pl.BlockSpec(memory_space=pl.ANY)] * len(args),
        out_specs=[pl.BlockSpec(memory_space=pltpu.VMEM)] * len(shapes),
        scratch_shapes=[pltpu.VMEM(a.shape, a.dtype) for a in now]
        + [pltpu.VMEM((1024, 128), F32), pltpu.SemaphoreType.DMA((len(args),))],
        compiler_params=pltpu.CompilerParams(vmem_limit_bytes=24 * 1024 * 1024),
    )(*[pltpu.with_memory_space_constraint(a, pltpu.HBM) for a in args])


def exchange(v):
    return lax.ppermute(v, "tmpl", [(0, 1), (1, 0)])


def exchange_cores(v):
    return lax.ppermute(v, "row", [(n, n ^ 1) for n in range(16)])


def spread_chunks(v, rows):
    v = lax.all_to_all(v.reshape(64, rows, 128), GROUP, 0, 0, axis_index_groups=ORDER, tiled=True)
    return v.reshape(64 * rows, 128)


def body(
    template_pair, template_mask, pair_mask, main_pair, update_cotangent,
    gain_in, proj_a, gate_a, proj_b, gate_b, gain_mid, proj_out, gate_out, gain_final,
    key_weight, value_weight, query_weight, output_weight,
):
    gi, gm, gf = gain_in.reshape(1, 64), gain_mid.reshape(1, 64), gain_final.reshape(1, 64)
    sides, x, normed, gi_wide, side_weights, mask, *later = call_copying(
        front_kernel,
        [
            ((1024, 128), BF16), ((64, 1024), BF16), ((64, 1024), BF16), ((64, 128), F32), ((64, 256), BF16),
            ((8, 1024), F32),
        ],
        [template_pair, pair_mask, gi, proj_a, gate_a, proj_b, gate_b],
        [
            gate_out, main_pair, update_cotangent, query_weight.T, output_weight, proj_out, key_weight,
            value_weight, gm, gf, template_mask.reshape(1, 2),
        ],
    )
    sides = spread_chunks(sides, 16)
    a, b_own = call(layout_kernel, [((256, 256), BF16), ((256, 256), BF16)], sides)
    b_other = exchange_cores(b_own)
    b_own, normed, later = lax.optimization_barrier((b_own, normed, later))
    side = call(
        side_kernel,
        [
            ((64, 1024), F32), ((64, 512), BF16), ((64, 512), F32), ((256, 256), BF16), ((64, 128), BF16),
            ((256, 128), F32), ((64, 128), F32), ((8, 1024), F32),
        ],
        normed, *later,
    )
    b_other, (gat, query, grad_out, wide, kv, gm_wide, gf_wide, absent) = lax.optimization_barrier(
        (b_other, side)
    )
    prod, b = call(product_kernel, [((512, 128), BF16), ((512, 256), BF16)], a, b_own, b_other)
    prod = spread_chunks(prod, 8)
    stat, weights, along, key, hat_m, rstd_m, out, hat_f, rstd_f = call(
        score_kernel,
        [
            ((2, 4, 512), F32), ((4, 1024), F32), ((4, 1024), F32), ((64, 1024), BF16),
            ((256, 256), F32), ((8, 256), F32), ((64, 1024), F32), ((64, 1024), F32), ((1, 1024), F32),
        ],
        x, prod, gat, query, grad_out, absent, gm_wide, gf_wide, wide, kv,
    )
    other = exchange(stat)
    pg, query_sum, d_updated = call(
        grad_kernel,
        [((512, 128), BF16), ((64, 512), F32), ((64, 1024), F32)],
        gat, query, grad_out, key, weights, along, stat, other,
        gm_wide, gf_wide, wide, kv, hat_m, rstd_m, hat_f, rstd_f,
    )
    cg, cp, hat, rstd, dn = call(
        coef_kernel,
        [((128, 1024), F32), ((128, 1024), F32), ((64, 1024), F32), ((1, 1024), F32), ((64, 1024), F32)],
        normed, x, mask, gat, out, d_updated, later[0], side_weights,
    )
    pg = spread_chunks(pg, 8)
    pg, right_own, right_sent = call(
        right_kernel, [((256, 256), BF16), ((256, 256), F32), ((256, 256), BF16)], pg, a
    )
    right_other = exchange_cores(right_sent)
    (left,) = call(left_kernel, [((256, 256), F32)], pg, b)
    (grads,) = call(triangle_kernel, [((1024, 128), BF16)], left, right_own, right_other)
    query_other = exchange(query_sum)
    (main_grad,) = call(main_kernel, [((16, 32, 128), BF16)], query_sum, query_other, later[3])
    grads = spread_chunks(grads, 16)
    (pair_grad,) = call(
        finish_kernel, [((2, 16, 32, 64), BF16)],
        grads, cg, cp, side_weights, dn, hat, rstd, d_updated, gi_wide,
        scratch=[pltpu.VMEM((1024, 128), F32)],
    )
    return (pair_grad, main_grad)


def solution(mesh):
    pixel = P("row", "col", None)
    placed = (
        P("tmpl", "row", "col", None), P("tmpl"), P("row", "col"), pixel, pixel,
    ) + (P(),) * 13
    return jax.shard_map(
        body,
        mesh=mesh,
        in_specs=placed,
        out_specs=(P("tmpl", "row", "col", None), pixel),
        check_vma=False,
    )
```

```python
import functools
import math

import jax
import jax.numpy as jnp
from jax import lax
from jax.experimental import pallas as pl
from jax.experimental.pallas import tpu as pltpu
from jax.sharding import PartitionSpec as P

EPS = 1e-05
F32 = jnp.float32
BF16 = jnp.bfloat16
HEADS = 4
HEAD_DIM = 16
SCALE = 1.0 / math.sqrt(HEAD_DIM)
GROUP = ("row", "col")
TURN = 6
LATER = 11
SIDE_BLOCKS = [(s, side, r) for s in range(2) for side in range(2) for r in range(4)]
PIXEL_ROWS = [4 * q + r for r in range(4) for q in range(4)]
ORDER = [[(z ^ TURN) * 16 + core * 8 + col for z in range(8) for col in range(8)] for core in range(2)]


def iota(shape, axis):
    return lax.broadcasted_iota(jnp.int32, shape, axis)


def shr(v, n):
    return lax.shift_right_logical(v, jnp.full(v.shape, n, jnp.int32))


def onehot(cond):
    return jnp.where(cond, 1.0, 0.0).astype(BF16)


def dot(a, b):
    return lax.dot_general(a, b, (((1,), (0,)), ((), ())), preferred_element_type=F32)


def dot_nt(a, b):
    return lax.dot_general(a, b, (((1,), (1,)), ((), ())), preferred_element_type=F32)


def dot_tn(a, b):
    return lax.dot_general(a, b, (((0,), (0,)), ((), ())), preferred_element_type=F32)


def eye64():
    return onehot(iota((64, 64), 0) == iota((64, 64), 1))


def c_to_rc(v):
    return jnp.concatenate(
        [
            jnp.concatenate([v[:, s * 512 + r * 128 : s * 512 + r * 128 + 128] for s in range(2)], axis=1)
            for r in range(4)
        ],
        axis=0,
    )


def rc_to_c(v):
    return jnp.concatenate(
        [v[r * 64 : r * 64 + 64, s * 128 : s * 128 + 128] for s in range(2) for r in range(4)], axis=1
    )


def both(v):
    return jnp.concatenate([v, v], axis=1)


def column(gain_row, repeat):
    pick = shr(iota((64 * repeat, 64), 0), repeat // 2) == iota((64 * repeat, 64), 1)
    return jnp.sum(jnp.where(pick, gain_row, 0.0), axis=1, keepdims=True)


def mean_c(v):
    return jnp.mean(v, axis=0, keepdims=True)


def mean_cr(v):
    part = jnp.sum(v.reshape(32, 8, 256), axis=0)
    return (part + pltpu.roll(part, 4, 0)) * (1.0 / 64.0)


def spread_cr(v):
    return jnp.broadcast_to(v[None], (32, 8, 256)).reshape(256, 256)


def hat_c(v):
    centered = v - mean_c(v)
    rstd = lax.rsqrt(mean_c(centered * centered) + EPS)
    return centered * rstd, rstd


def norm_grad_c(grad, gain, hat, rstd):
    scaled = grad * gain
    return rstd * (scaled - mean_c(scaled) - hat * mean_c(scaled * hat))


def hat_cr(v):
    centered = v - spread_cr(mean_cr(v))
    rstd = spread_cr(lax.rsqrt(mean_cr(centered * centered) + EPS))
    return centered * rstd, rstd


def norm_grad_cr(grad, gain, hat, rstd):
    scaled = grad * gain
    return rstd * (scaled - spread_cr(mean_cr(scaled)) - hat * spread_cr(mean_cr(scaled * hat)))


def wide_out(w):
    row, lane = iota((64, 256), 0), iota((64, 256), 1)
    base = dot_tn(w, onehot(row == shr(lane, 2)))
    return jnp.concatenate([jnp.where((lane & 3) == r, base, 0.0) for r in range(4)], axis=0).astype(BF16)


def mask_row(mask):
    tiled = dot(mask.astype(F32).astype(BF16), onehot(iota((32, 128), 0) == (iota((32, 128), 1) & 31)))
    i, lane = iota((16, 128), 0), iota((16, 128), 1)
    tiled = jnp.where(shr(i, 2) == shr(lane, 5), tiled, 0.0).astype(BF16)
    rows = dot(onehot((iota((8, 16), 0) & 3) == (iota((8, 16), 1) & 3)), tiled)
    return both(jnp.concatenate([rows[r : r + 1] for r in range(4)], axis=1))


def swap_groups(four):
    lane = iota(four[0].shape, 1)
    for bit in (1, 2):
        low = (lane & (32 * bit)) == 0
        out = []
        for a in range(4):
            if a & bit == 0:
                out.append(jnp.where(low, four[a], pltpu.roll(four[a ^ bit], 32 * bit, 1)))
            else:
                out.append(jnp.where(low, pltpu.roll(four[a ^ bit], 128 - 32 * bit, 1), four[a]))
        four = out
    return four


def swap_in(blocks):
    lo, hi = swap_groups(blocks[:4]), swap_groups(blocks[4:])
    return [jnp.concatenate([lo[q], hi[q]], axis=1) for q in range(4)]


def swap_out(rows):
    return swap_groups([v[:, :128] for v in rows]) + swap_groups([v[:, 128:] for v in rows])


def pair_up(even, odd):
    top = iota(even.shape, even.ndim - 2) < 4
    axis = even.ndim - 2
    return jnp.where(top, even, pltpu.roll(odd, 4, axis)), jnp.where(top, pltpu.roll(even, 4, axis), odd)


def turn(v):
    return jnp.concatenate([v[n ^ TURN : (n ^ TURN) + 2] for n in range(0, 8, 2)], axis=0)


def by_core(first, second):
    core0 = (lax.axis_index("row") & 1) == 0
    return jnp.where(core0, first, second), jnp.where(core0, second, first)


def front_kernel(
    x_hbm, mask_hbm, gi_hbm, pa_hbm, ga_hbm, pb_hbm, gb_hbm, *refs
):
    later, refs = refs[:LATER], refs[LATER:]
    out_ref, x_out, n_out, gi_out, sides_out, mask_out = refs[:6]
    later_out, refs = refs[6 : 6 + LATER], refs[6 + LATER :]
    x_ref, mask_ref, gi_ref, pa_ref, ga_ref, pb_ref, gb_ref, tiles_ref, sems = refs
    pairs = [
        (x_hbm, x_ref), (gi_hbm, gi_ref), (pa_hbm, pa_ref), (ga_hbm, ga_ref), (pb_hbm, pb_ref),
        (gb_hbm, gb_ref), (mask_hbm, mask_ref),
    ] + list(zip(later, later_out))
    copies = [pltpu.make_async_copy(a, b, sems.at[n]) for n, (a, b) in enumerate(pairs)]
    for copy in copies:
        copy.start()
    for copy in copies[1:7]:
        copy.wait()
    weights = jnp.concatenate([ga_ref[...], gb_ref[...], pa_ref[...], pb_ref[...]], axis=1)
    sides_out[...] = weights
    mask = mask_row(mask_ref[...])
    mask_out[...] = jnp.broadcast_to(mask, (8, 1024))
    copies[0].wait()
    x = dot_nt(eye64(), jnp.concatenate([x_ref[s, i] for s in range(2) for i in PIXEL_ROWS], axis=0))
    hat, _ = hat_c(x)
    gi = column(gi_ref[...], 1)
    normed = (hat * gi).astype(BF16)
    x_out[...] = x.astype(BF16)
    n_out[...] = normed
    gi_out[...] = jnp.broadcast_to(gi, (64, 128))
    both_sides = dot_tn(weights, normed)
    both_sides = mask * jax.nn.sigmoid(both_sides[:128]) * both_sides[128:]
    for s, side, r in SIDE_BLOCKS:
        tiles_ref[pl.ds(s * 512 + side * 4 + r, 64, stride=8), :] = both_sides[
            side * 64 : side * 64 + 64, s * 512 + r * 128 : s * 512 + r * 128 + 128
        ]
    out_ref[...] = tiles_ref[...].astype(BF16)
    for copy in copies[7:]:
        copy.wait()


def side_kernel(
    n_ref, go_ref, main_ref, cot_ref, wq_ref, wo_ref, po_ref, kw_ref, vw_ref, gm_ref, gf_ref, present_ref,
    gat_out, q_out, g_out, wide_out_ref, kv_out, gm_out, gf_out, absent_out,
):
    gat_out[...] = jax.nn.sigmoid(dot_tn(go_ref[...], n_ref[...]))
    q_out[...] = dot_nt(wq_ref[...], jnp.concatenate([main_ref[i] for i in PIXEL_ROWS], axis=0)).astype(BF16)
    g_out[...] = dot_nt(wo_ref[...], jnp.concatenate([cot_ref[i] for i in PIXEL_ROWS], axis=0))
    wide_out_ref[...] = wide_out(po_ref[...])
    kv_out[...] = jnp.concatenate([kw_ref[...], vw_ref[...]], axis=1)
    gm_out[...] = jnp.broadcast_to(column(gm_ref[...], 4), (256, 128))
    gf_out[...] = jnp.broadcast_to(column(gf_ref[...], 1), (64, 128))
    absent_out[...] = jnp.where(
        jnp.concatenate([jnp.broadcast_to(present_ref[:, s : s + 1], (8, 512)) for s in range(2)], axis=1) > 0,
        0.0, -1e30,
    )


def layout_kernel(x_ref, a_out, b_out):
    tiles = x_ref[...].astype(F32).reshape(8, 8, 2, 8, 128)
    parts = [v.reshape(8, 2, 8, 256) for v in swap_in([tiles[:, c].reshape(128, 128) for c in range(8)])]
    rolled = [pltpu.roll(v.reshape(16, 8, 256), 4, 1).reshape(8, 2, 8, 256) for v in parts]
    top = iota((8, 8, 256), 1) < 4
    a, b = [], []
    for e in range(2):
        for v, w in zip(parts, rolled):
            v, w = v[:, e].reshape(4, 2, 8, 256), w[:, e].reshape(4, 2, 8, 256)
            a.append(jnp.where(top[:4], v[:, 0], w[:, 1]).reshape(32, 256))
        half = [turn(jnp.where(top, rolled[q][:, e], parts[q + 1][:, e])) for q in (0, 2)]
        b.append(jnp.stack(half, axis=1).reshape(128, 256))
    a_out[...] = jnp.concatenate(a, axis=0).astype(BF16)
    b_out[...] = jnp.concatenate(b, axis=0).astype(BF16)


def product_kernel(a_ref, own_ref, other_ref, out_ref, b_out):
    prods = []
    for e in range(2):
        own = own_ref[e * 128 : e * 128 + 128, :].reshape(8, 16, 256)
        other = other_ref[e * 128 : e * 128 + 128, :].reshape(8, 16, 256)
        b = jnp.stack(by_core(own, other), axis=1).reshape(256, 256)
        b_out[e * 256 : e * 256 + 256, :] = b
        prods.append(dot_nt(a_ref[e * 128 : e * 128 + 128, :], b))
    rows = [jnp.concatenate([v[q * 32 : q * 32 + 32] for v in prods], axis=0) for q in range(4)]
    pairs = []
    for v in swap_out(rows):
        v = v.reshape(2, 4, 8, 128)
        pairs.append(jnp.stack(pair_up(v[0], v[1]), axis=1).reshape(8, 8, 128))
    out_ref[...] = jnp.stack(pairs, axis=1).reshape(512, 128).astype(BF16)


def heads_sum(v):
    return jnp.sum(v.reshape(HEADS, HEAD_DIM, v.shape[-1]), axis=1)


def heads_spread(v):
    return jnp.broadcast_to(v[:, None, :], (HEADS, HEAD_DIM, v.shape[-1])).reshape(64, v.shape[-1])


def tile_lanes(v, n):
    return jnp.concatenate([v] * n, axis=1)


def score_kernel(
    x_ref, prod_ref, gat_ref, q_ref, g_ref, absent_ref, gm_ref, gf_ref, wide_ref, kv_ref,
    stat_out, w_out, along_out, key_out, hat_m_out, rstd_m_out, out_out, hat_f_out, rstd_f_out,
):
    prod = jnp.concatenate([prod_ref[:256, :], prod_ref[256:, :]], axis=1).astype(F32)
    centered = prod - spread_cr(mean_cr(prod))
    rstd_m = lax.rsqrt(mean_cr(centered * centered) + EPS)
    hat_m = centered * spread_cr(rstd_m)
    out = rc_to_c(dot(wide_ref[...], (hat_m * tile_lanes(gm_ref[...], 2)).astype(BF16)))
    hat_f, rstd_f = hat_c(x_ref[...].astype(F32) + gat_ref[...] * out)
    hat_m_out[...] = hat_m
    rstd_m_out[...] = rstd_m
    out_out[...] = out
    hat_f_out[...] = hat_f
    rstd_f_out[...] = rstd_f
    final = (hat_f * tile_lanes(gf_ref[...], 8)).astype(BF16)
    key_val = dot_tn(kv_ref[...], final).astype(BF16)
    key, val = key_val[:64], key_val[64:]
    key_out[...] = key
    score = heads_sum(both(q_ref[...].astype(F32)) * key.astype(F32)) * SCALE
    along = heads_sum(both(g_ref[...]) * val.astype(F32))
    score = jnp.where(absent_ref[:4, :] < 0.0, -1e30, score)
    s0, s1 = score[:, :512], score[:, 512:]
    top = jnp.maximum(s0, s1)
    e0, e1 = jnp.exp(s0 - top), jnp.exp(s1 - top)
    total = e0 + e1
    w0, w1 = e0 / total, e1 / total
    w_out[...] = jnp.concatenate([w0, w1], axis=1)
    along_out[...] = along
    stat_out[0] = top + jnp.log(total)
    stat_out[1] = w0 * along[:, :512] + w1 * along[:, 512:]


def grad_kernel(
    gat_ref, q_ref, g_ref, key_ref, w_ref, along_ref, mine_ref, other_ref,
    gm_ref, gf_ref, wide_ref, kv_ref, hat_m_ref, rstd_m_ref, hat_f_ref, rstd_f_ref,
    pg_out, qsum_out, du_out,
):
    share = jax.nn.sigmoid(mine_ref[0] - other_ref[0])
    average = share * mine_ref[1] + jax.nn.sigmoid(other_ref[0] - mine_ref[0]) * other_ref[1]
    weights = w_ref[...] * both(share)
    slope = weights * (along_ref[...] - both(average))
    slope_wide = heads_spread(slope)
    part = slope_wide * key_ref[...].astype(F32)
    qsum_out[...] = (part[:, :512] + part[:, 512:]) * SCALE
    key_grad = (slope_wide * both(q_ref[...].astype(F32) * SCALE)).astype(BF16)
    value_grad = (heads_spread(weights) * both(g_ref[...])).astype(BF16)
    d_final = dot(kv_ref[...], jnp.concatenate([key_grad, value_grad], axis=0))
    d_updated = norm_grad_c(d_final, tile_lanes(gf_ref[...], 8), hat_f_ref[...], rstd_f_ref[...])
    gat = gat_ref[...]
    du_out[...] = d_updated
    d_mixed = dot_tn(wide_ref[...], c_to_rc((d_updated * gat).astype(BF16)))
    pg = norm_grad_cr(
        d_mixed, tile_lanes(gm_ref[...], 2), hat_m_ref[...], spread_cr(rstd_m_ref[...])
    ).astype(BF16)
    pg_out[:256, :] = pg[:, :128]
    pg_out[256:, :] = pg[:, 128:]


def coef_kernel(
    n_ref, x_ref, mask_ref, gat_ref, out_ref, du_ref, go_ref, sides_ref, cg_out, cp_out, hat_out, rstd_out, dn_out
):
    both_sides = dot_tn(sides_ref[...], n_ref[...])
    gate = jax.nn.sigmoid(both_sides[:128])
    scaled = mask_ref[:1, :] * gate
    cp_out[...] = scaled
    cg_out[...] = scaled * (1.0 - gate) * both_sides[128:]
    hat_out[...], rstd_out[...] = hat_c(x_ref[...].astype(F32))
    gat = gat_ref[...]
    d_gate = (du_ref[...] * gat * out_ref[...] * (1.0 - gat)).astype(BF16)
    dn_out[...] = dot(go_ref[...], d_gate)


def right_kernel(pg_ref, a_ref, pg_out, own_out, sent_out):
    tiles = pg_ref[...].astype(F32).reshape(8, 8, 8, 128)
    parts = swap_in([tiles[:, c].reshape(64, 128) for c in range(8)])
    split = [pair_up(v.reshape(4, 2, 8, 256)[:, 0], v.reshape(4, 2, 8, 256)[:, 1]) for v in parts]
    for e in range(2):
        pg = jnp.concatenate([v[e].reshape(32, 256) for v in split], axis=0).astype(BF16)
        pg_out[e * 128 : e * 128 + 128, :] = pg
        right = dot_tn(pg, a_ref[e * 128 : e * 128 + 128, :]).reshape(8, 2, 16, 256)
        own, sent = by_core(right[:, 0], right[:, 1])
        own_out[e * 128 : e * 128 + 128, :] = own.reshape(128, 256)
        sent_out[e * 128 : e * 128 + 128, :] = sent.reshape(128, 256).astype(BF16)


def left_kernel(pg_ref, b_ref, out_ref):
    for e in range(2):
        out_ref[e * 128 : e * 128 + 128, :] = dot(
            pg_ref[e * 128 : e * 128 + 128, :], b_ref[e * 256 : e * 256 + 256, :]
        )


def triangle_kernel(left_ref, own_ref, other_ref, out_ref):
    top = iota((8, 8, 256), 1) < 4
    right = (own_ref[...] + other_ref[...].astype(F32)).reshape(2, 8, 2, 8, 256)
    rows = []
    for q in range(4):
        tiles = []
        for e in range(2):
            left = left_ref[e * 128 + q * 32 : e * 128 + q * 32 + 32, :].reshape(4, 8, 256)
            upper = jnp.stack([left, pltpu.roll(left, 4, 1)], axis=1).reshape(8, 8, 256)
            lower = turn(right[e, :, q // 2])
            lower = lower if q & 1 else pltpu.roll(lower, 4, 1)
            tiles.append(jnp.where(top, upper, lower))
        rows.append(jnp.stack(tiles, axis=1).reshape(128, 256))
    cols = [v.reshape(8, 2, 8, 128) for v in swap_out(rows)]
    out_ref[...] = jnp.stack(cols, axis=1).reshape(1024, 128).astype(BF16)


def finish_kernel(
    lr_ref, cg_ref, cp_ref, sides_ref, dn_ref, hat_ref, rstd_ref, du_ref, gain_ref,
    mine_ref, other_ref, wq_ref, out_ref, main_out, tiles_ref,
):
    tiles_ref[...] = lr_ref[...].astype(F32)
    blocks = [tiles_ref[pl.ds(s * 512 + side * 4 + r, 64, stride=8), :] for s, side, r in SIDE_BLOCKS]
    grad = jnp.concatenate(
        [
            jnp.concatenate([blocks[s * 8 + side * 4 + r] for s in range(2) for r in range(4)], axis=1)
            for side in range(2)
        ],
        axis=0,
    )
    grad = jnp.concatenate([(grad * cg_ref[...]).astype(BF16), (grad * cp_ref[...]).astype(BF16)], axis=0)
    d_normed = dot(sides_ref[...], grad) + dn_ref[...]
    grad_x = norm_grad_c(d_normed, tile_lanes(gain_ref[...], 8), hat_ref[...], rstd_ref[...]) + du_ref[...]
    out = dot_tn(grad_x.astype(BF16), eye64()).astype(BF16)
    for s in range(2):
        for n, i in enumerate(PIXEL_ROWS):
            out_ref[s, i] = out[s * 512 + n * 32 : s * 512 + n * 32 + 32]
    grad = (mine_ref[...] + other_ref[...]).astype(BF16)
    out = dot_tn(grad, wq_ref[...]).astype(BF16)
    for n, i in enumerate(PIXEL_ROWS):
        main_out[i] = out[n * 32 : n * 32 + 32]


def call(kernel, outs, *args, scratch=()):
    shapes = [jax.ShapeDtypeStruct(s, t) for s, t in outs]
    nbytes = sum(a.size * a.dtype.itemsize for a in args)
    return pl.pallas_call(
        kernel,
        out_shape=shapes,
        in_specs=[pl.BlockSpec(memory_space=pltpu.VMEM)] * len(args),
        out_specs=[pl.BlockSpec(memory_space=pltpu.VMEM)] * len(shapes),
        scratch_shapes=scratch,
        compiler_params=pltpu.CompilerParams(vmem_limit_bytes=24 * 1024 * 1024),
        cost_estimate=pl.CostEstimate(flops=0, bytes_accessed=nbytes, transcendentals=0),
    )(*args)


def call_copying(kernel, outs, now, later):
    shapes = [jax.ShapeDtypeStruct(s, t) for s, t in outs]
    shapes += [jax.ShapeDtypeStruct(a.shape, a.dtype) for a in later]
    args = now + later
    return pl.pallas_call(
        kernel,
        out_shape=shapes,
        in_specs=[pl.BlockSpec(memory_space=pl.ANY)] * len(args),
        out_specs=[pl.BlockSpec(memory_space=pltpu.VMEM)] * len(shapes),
        scratch_shapes=[pltpu.VMEM(a.shape, a.dtype) for a in now]
        + [pltpu.VMEM((1024, 128), F32), pltpu.SemaphoreType.DMA((len(args),))],
        compiler_params=pltpu.CompilerParams(vmem_limit_bytes=24 * 1024 * 1024),
    )(*[pltpu.with_memory_space_constraint(a, pltpu.HBM) for a in args])


def exchange(v):
    return lax.ppermute(v, "tmpl", [(0, 1), (1, 0)])


def exchange_cores(v):
    return lax.ppermute(v, "row", [(n, n ^ 1) for n in range(16)])


def spread_chunks(v, rows):
    v = lax.all_to_all(v.reshape(64, rows, 128), GROUP, 0, 0, axis_index_groups=ORDER, tiled=True)
    return v.reshape(64 * rows, 128)


def body(
    template_pair, template_mask, pair_mask, main_pair, update_cotangent,
    gain_in, proj_a, gate_a, proj_b, gate_b, gain_mid, proj_out, gate_out, gain_final,
    key_weight, value_weight, query_weight, output_weight,
):
    gi, gm, gf = gain_in.reshape(1, 64), gain_mid.reshape(1, 64), gain_final.reshape(1, 64)
    sides, x, normed, gi_wide, side_weights, mask, *later = call_copying(
        front_kernel,
        [
            ((1024, 128), BF16), ((64, 1024), BF16), ((64, 1024), BF16), ((64, 128), F32), ((64, 256), BF16),
            ((8, 1024), F32),
        ],
        [template_pair, pair_mask, gi, proj_a, gate_a, proj_b, gate_b],
        [
            gate_out, main_pair, update_cotangent, query_weight.T, output_weight, proj_out, key_weight,
            value_weight, gm, gf, template_mask.reshape(1, 2),
        ],
    )
    sides = spread_chunks(sides, 16)
    a, b_own = call(layout_kernel, [((256, 256), BF16), ((256, 256), BF16)], sides)
    b_other = exchange_cores(b_own)
    b_own, normed, later = lax.optimization_barrier((b_own, normed, later))
    side = call(
        side_kernel,
        [
            ((64, 1024), F32), ((64, 512), BF16), ((64, 512), F32), ((256, 256), BF16), ((64, 128), BF16),
            ((256, 128), F32), ((64, 128), F32), ((8, 1024), F32),
        ],
        normed, *later,
    )
    b_other, (gat, query, grad_out, wide, kv, gm_wide, gf_wide, absent) = lax.optimization_barrier(
        (b_other, side)
    )
    prod, b = call(product_kernel, [((512, 128), BF16), ((512, 256), BF16)], a, b_own, b_other)
    prod = spread_chunks(prod, 8)
    stat, weights, along, key, hat_m, rstd_m, out, hat_f, rstd_f = call(
        score_kernel,
        [
            ((2, 4, 512), F32), ((4, 1024), F32), ((4, 1024), F32), ((64, 1024), BF16),
            ((256, 256), F32), ((8, 256), F32), ((64, 1024), F32), ((64, 1024), F32), ((1, 1024), F32),
        ],
        x, prod, gat, query, grad_out, absent, gm_wide, gf_wide, wide, kv,
    )
    other = exchange(stat)
    pg, query_sum, d_updated = call(
        grad_kernel,
        [((512, 128), BF16), ((64, 512), F32), ((64, 1024), F32)],
        gat, query, grad_out, key, weights, along, stat, other,
        gm_wide, gf_wide, wide, kv, hat_m, rstd_m, hat_f, rstd_f,
    )
    pg = spread_chunks(pg, 8)
    pg, right_own, right_sent = call(
        right_kernel, [((256, 256), BF16), ((256, 256), F32), ((256, 256), BF16)], pg, a
    )
    right_other = exchange_cores(right_sent)
    right_own, normed, gate_weight = lax.optimization_barrier((right_own, normed, later[0]))
    cg, cp, hat, rstd, dn = call(
        coef_kernel,
        [((128, 1024), F32), ((128, 1024), F32), ((64, 1024), F32), ((1, 1024), F32), ((64, 1024), F32)],
        normed, x, mask, gat, out, d_updated, gate_weight, side_weights,
    )
    right_other, query_other, cg, cp, hat, rstd, dn = lax.optimization_barrier(
        (right_other, exchange(query_sum), cg, cp, hat, rstd, dn)
    )
    (left,) = call(left_kernel, [((256, 256), F32)], pg, b)
    (grads,) = call(triangle_kernel, [((1024, 128), BF16)], left, right_own, right_other)
    grads = spread_chunks(grads, 16)
    pair_grad, main_grad = call(
        finish_kernel, [((2, 16, 32, 64), BF16), ((16, 32, 128), BF16)],
        grads, cg, cp, side_weights, dn, hat, rstd, d_updated, gi_wide, query_sum, query_other, later[3],
        scratch=[pltpu.VMEM((1024, 128), F32)],
    )
    return (pair_grad, main_grad)


def solution(mesh):
    pixel = P("row", "col", None)
    placed = (
        P("tmpl", "row", "col", None), P("tmpl"), P("row", "col"), pixel, pixel,
    ) + (P(),) * 13
    return jax.shard_map(
        body,
        mesh=mesh,
        in_specs=placed,
        out_specs=(P("tmpl", "row", "col", None), pixel),
        check_vma=False,
    )
```

```python
import functools
import math

import jax
import jax.numpy as jnp
from jax import lax
from jax.experimental import pallas as pl
from jax.experimental.pallas import tpu as pltpu
from jax.sharding import PartitionSpec as P

EPS = 1e-05
F32 = jnp.float32
BF16 = jnp.bfloat16
HEADS = 4
HEAD_DIM = 16
SCALE = 1.0 / math.sqrt(HEAD_DIM)
GROUP = ("row", "col")
TURN = 6
LATER = 11
SIDE_BLOCKS = [(s, side, r) for s in range(2) for side in range(2) for r in range(4)]
PIXEL_ROWS = [4 * q + r for r in range(4) for q in range(4)]
COLS = [x * 4 + y for y in range(4) for x in range(2)]
PLACES = [COLS.index(col) for col in range(8)]
ORDER = [[(z ^ TURN) * 16 + core * 8 + col for z in range(8) for col in COLS] for core in range(2)]


def iota(shape, axis):
    return lax.broadcasted_iota(jnp.int32, shape, axis)


def shr(v, n):
    return lax.shift_right_logical(v, jnp.full(v.shape, n, jnp.int32))


def onehot(cond):
    return jnp.where(cond, 1.0, 0.0).astype(BF16)


def dot(a, b):
    return lax.dot_general(a, b, (((1,), (0,)), ((), ())), preferred_element_type=F32)


def dot_nt(a, b):
    return lax.dot_general(a, b, (((1,), (1,)), ((), ())), preferred_element_type=F32)


def dot_tn(a, b):
    return lax.dot_general(a, b, (((0,), (0,)), ((), ())), preferred_element_type=F32)


def eye64():
    return onehot(iota((64, 64), 0) == iota((64, 64), 1))


def c_to_rc(v):
    return jnp.concatenate(
        [
            jnp.concatenate([v[:, s * 512 + r * 128 : s * 512 + r * 128 + 128] for s in range(2)], axis=1)
            for r in range(4)
        ],
        axis=0,
    )


def rc_to_c(v):
    return jnp.concatenate(
        [v[r * 64 : r * 64 + 64, s * 128 : s * 128 + 128] for s in range(2) for r in range(4)], axis=1
    )


def both(v):
    return jnp.concatenate([v, v], axis=1)


def column(gain_row, repeat):
    pick = shr(iota((64 * repeat, 64), 0), repeat // 2) == iota((64 * repeat, 64), 1)
    return jnp.sum(jnp.where(pick, gain_row, 0.0), axis=1, keepdims=True)


def mean_c(v):
    return jnp.mean(v, axis=0, keepdims=True)


def mean_cr(v):
    part = jnp.sum(v.reshape(32, 8, 256), axis=0)
    return (part + pltpu.roll(part, 4, 0)) * (1.0 / 64.0)


def spread_cr(v):
    return jnp.broadcast_to(v[None], (32, 8, 256)).reshape(256, 256)


def hat_c(v):
    centered = v - mean_c(v)
    rstd = lax.rsqrt(mean_c(centered * centered) + EPS)
    return centered * rstd, rstd


def norm_grad_c(grad, gain, hat, rstd):
    scaled = grad * gain
    return rstd * (scaled - mean_c(scaled) - hat * mean_c(scaled * hat))


def hat_cr(v):
    centered = v - spread_cr(mean_cr(v))
    rstd = spread_cr(lax.rsqrt(mean_cr(centered * centered) + EPS))
    return centered * rstd, rstd


def norm_grad_cr(grad, gain, hat, rstd):
    scaled = grad * gain
    return rstd * (scaled - spread_cr(mean_cr(scaled)) - hat * spread_cr(mean_cr(scaled * hat)))


def wide_out(w):
    row, lane = iota((64, 256), 0), iota((64, 256), 1)
    base = dot_tn(w, onehot(row == shr(lane, 2)))
    return jnp.concatenate([jnp.where((lane & 3) == r, base, 0.0) for r in range(4)], axis=0).astype(BF16)


def mask_row(mask):
    tiled = dot(mask.astype(F32).astype(BF16), onehot(iota((32, 128), 0) == (iota((32, 128), 1) & 31)))
    i, lane = iota((16, 128), 0), iota((16, 128), 1)
    tiled = jnp.where(shr(i, 2) == shr(lane, 5), tiled, 0.0).astype(BF16)
    rows = dot(onehot((iota((8, 16), 0) & 3) == (iota((8, 16), 1) & 3)), tiled)
    return both(jnp.concatenate([rows[r : r + 1] for r in range(4)], axis=1))


def swap_groups(four):
    lane = iota(four[0].shape, 1)
    for bit in (1, 2):
        low = (lane & (32 * bit)) == 0
        out = []
        for a in range(4):
            if a & bit == 0:
                out.append(jnp.where(low, four[a], pltpu.roll(four[a ^ bit], 32 * bit, 1)))
            else:
                out.append(jnp.where(low, pltpu.roll(four[a ^ bit], 128 - 32 * bit, 1), four[a]))
        four = out
    return four


def swap_in(blocks):
    lo, hi = swap_groups(blocks[:4]), swap_groups(blocks[4:])
    return [jnp.concatenate([lo[q], hi[q]], axis=1) for q in range(4)]


def swap_out(rows):
    return swap_groups([v[:, :128] for v in rows]) + swap_groups([v[:, 128:] for v in rows])


def pair_up(even, odd):
    top = iota(even.shape, even.ndim - 2) < 4
    axis = even.ndim - 2
    return jnp.where(top, even, pltpu.roll(odd, 4, axis)), jnp.where(top, pltpu.roll(even, 4, axis), odd)


def turn(v):
    return jnp.concatenate([v[n ^ TURN : (n ^ TURN) + 2] for n in range(0, 8, 2)], axis=0)


def by_core(first, second):
    core0 = (lax.axis_index("row") & 1) == 0
    return jnp.where(core0, first, second), jnp.where(core0, second, first)


def front_kernel(
    x_hbm, mask_hbm, gi_hbm, pa_hbm, ga_hbm, pb_hbm, gb_hbm, *refs
):
    later, refs = refs[:LATER], refs[LATER:]
    out_ref, x_out, n_out, gi_out, sides_out, mask_out = refs[:6]
    later_out, refs = refs[6 : 6 + LATER], refs[6 + LATER :]
    x_ref, mask_ref, gi_ref, pa_ref, ga_ref, pb_ref, gb_ref, tiles_ref, sems = refs
    pairs = [
        (x_hbm, x_ref), (gi_hbm, gi_ref), (pa_hbm, pa_ref), (ga_hbm, ga_ref), (pb_hbm, pb_ref),
        (gb_hbm, gb_ref), (mask_hbm, mask_ref),
    ] + list(zip(later, later_out))
    copies = [pltpu.make_async_copy(a, b, sems.at[n]) for n, (a, b) in enumerate(pairs)]
    for copy in copies:
        copy.start()
    for copy in copies[1:7]:
        copy.wait()
    weights = jnp.concatenate([ga_ref[...], gb_ref[...], pa_ref[...], pb_ref[...]], axis=1)
    sides_out[...] = weights
    mask = mask_row(mask_ref[...])
    mask_out[...] = jnp.broadcast_to(mask, (8, 1024))
    copies[0].wait()
    x = dot_nt(eye64(), jnp.concatenate([x_ref[s, i] for s in range(2) for i in PIXEL_ROWS], axis=0))
    hat, _ = hat_c(x)
    gi = column(gi_ref[...], 1)
    normed = (hat * gi).astype(BF16)
    x_out[...] = x.astype(BF16)
    n_out[...] = normed
    gi_out[...] = jnp.broadcast_to(gi, (64, 128))
    both_sides = dot_tn(weights, normed)
    both_sides = mask * jax.nn.sigmoid(both_sides[:128]) * both_sides[128:]
    for s, side, r in SIDE_BLOCKS:
        tiles_ref[pl.ds(s * 512 + side * 4 + r, 64, stride=8), :] = both_sides[
            side * 64 : side * 64 + 64, s * 512 + r * 128 : s * 512 + r * 128 + 128
        ]
    out_ref[...] = tiles_ref[...].astype(BF16)
    for copy in copies[7:]:
        copy.wait()


def side_kernel(
    n_ref, go_ref, main_ref, cot_ref, wq_ref, wo_ref, po_ref, kw_ref, vw_ref, gm_ref, gf_ref, present_ref,
    gat_out, q_out, g_out, wide_out_ref, kv_out, gm_out, gf_out, absent_out,
):
    gat_out[...] = jax.nn.sigmoid(dot_tn(go_ref[...], n_ref[...]))
    q_out[...] = dot_nt(wq_ref[...], jnp.concatenate([main_ref[i] for i in PIXEL_ROWS], axis=0)).astype(BF16)
    g_out[...] = dot_nt(wo_ref[...], jnp.concatenate([cot_ref[i] for i in PIXEL_ROWS], axis=0))
    wide_out_ref[...] = wide_out(po_ref[...])
    kv_out[...] = jnp.concatenate([kw_ref[...], vw_ref[...]], axis=1)
    gm_out[...] = jnp.broadcast_to(column(gm_ref[...], 4), (256, 128))
    gf_out[...] = jnp.broadcast_to(column(gf_ref[...], 1), (64, 128))
    absent_out[...] = jnp.where(
        jnp.concatenate([jnp.broadcast_to(present_ref[:, s : s + 1], (8, 512)) for s in range(2)], axis=1) > 0,
        0.0, -1e30,
    )


def layout_kernel(x_ref, a_out, b_out):
    tiles = x_ref[...].astype(F32).reshape(8, 8, 2, 8, 128)
    parts = [v.reshape(8, 2, 8, 256) for v in swap_in([tiles[:, c].reshape(128, 128) for c in PLACES])]
    rolled = [pltpu.roll(v.reshape(16, 8, 256), 4, 1).reshape(8, 2, 8, 256) for v in parts]
    top = iota((8, 8, 256), 1) < 4
    a, b = [], []
    for e in range(2):
        for v, w in zip(parts, rolled):
            v, w = v[:, e].reshape(4, 2, 8, 256), w[:, e].reshape(4, 2, 8, 256)
            a.append(jnp.where(top[:4], v[:, 0], w[:, 1]).reshape(32, 256))
        half = [turn(jnp.where(top, rolled[q][:, e], parts[q + 1][:, e])) for q in (0, 2)]
        b.append(jnp.stack(half, axis=1).reshape(128, 256))
    a_out[...] = jnp.concatenate(a, axis=0).astype(BF16)
    b_out[...] = jnp.concatenate(b, axis=0).astype(BF16)


def product_kernel(a_ref, own_ref, other_ref, out_ref, b_out):
    prods = []
    for e in range(2):
        own = own_ref[e * 128 : e * 128 + 128, :].reshape(8, 16, 256)
        other = other_ref[e * 128 : e * 128 + 128, :].reshape(8, 16, 256)
        b = jnp.stack(by_core(own, other), axis=1).reshape(256, 256)
        b_out[e * 256 : e * 256 + 256, :] = b
        prods.append(dot_nt(a_ref[e * 128 : e * 128 + 128, :], b))
    rows = [jnp.concatenate([v[q * 32 : q * 32 + 32] for v in prods], axis=0) for q in range(4)]
    pairs = []
    for v in swap_out(rows):
        v = v.reshape(2, 4, 8, 128)
        pairs.append(jnp.stack(pair_up(v[0], v[1]), axis=1).reshape(8, 8, 128))
    out_ref[...] = jnp.stack([pairs[c] for c in COLS], axis=1).reshape(512, 128).astype(BF16)


def heads_sum(v):
    return jnp.sum(v.reshape(HEADS, HEAD_DIM, v.shape[-1]), axis=1)


def heads_spread(v):
    return jnp.broadcast_to(v[:, None, :], (HEADS, HEAD_DIM, v.shape[-1])).reshape(64, v.shape[-1])


def tile_lanes(v, n):
    return jnp.concatenate([v] * n, axis=1)


def score_kernel(
    x_ref, prod_ref, gat_ref, q_ref, g_ref, absent_ref, gm_ref, gf_ref, wide_ref, kv_ref,
    stat_out, w_out, along_out, key_out, hat_m_out, rstd_m_out, out_out, hat_f_out, rstd_f_out,
):
    prod = jnp.concatenate([prod_ref[:256, :], prod_ref[256:, :]], axis=1).astype(F32)
    centered = prod - spread_cr(mean_cr(prod))
    rstd_m = lax.rsqrt(mean_cr(centered * centered) + EPS)
    hat_m = centered * spread_cr(rstd_m)
    out = rc_to_c(dot(wide_ref[...], (hat_m * tile_lanes(gm_ref[...], 2)).astype(BF16)))
    hat_f, rstd_f = hat_c(x_ref[...].astype(F32) + gat_ref[...] * out)
    hat_m_out[...] = hat_m
    rstd_m_out[...] = rstd_m
    out_out[...] = out
    hat_f_out[...] = hat_f
    rstd_f_out[...] = rstd_f
    final = (hat_f * tile_lanes(gf_ref[...], 8)).astype(BF16)
    key_val = dot_tn(kv_ref[...], final).astype(BF16)
    key, val = key_val[:64], key_val[64:]
    key_out[...] = key
    score = heads_sum(both(q_ref[...].astype(F32)) * key.astype(F32)) * SCALE
    along = heads_sum(both(g_ref[...]) * val.astype(F32))
    score = jnp.where(absent_ref[:4, :] < 0.0, -1e30, score)
    s0, s1 = score[:, :512], score[:, 512:]
    top = jnp.maximum(s0, s1)
    e0, e1 = jnp.exp(s0 - top), jnp.exp(s1 - top)
    total = e0 + e1
    w0, w1 = e0 / total, e1 / total
    w_out[...] = jnp.concatenate([w0, w1], axis=1)
    along_out[...] = along
    stat_out[0] = top + jnp.log(total)
    stat_out[1] = w0 * along[:, :512] + w1 * along[:, 512:]


def grad_kernel(
    gat_ref, q_ref, g_ref, w_ref, along_ref, mine_ref, other_ref,
    gm_ref, gf_ref, wide_ref, kv_ref, hat_m_ref, rstd_m_ref, hat_f_ref, rstd_f_ref,
    pg_out, slope_out, du_out,
):
    share = jax.nn.sigmoid(mine_ref[0] - other_ref[0])
    average = share * mine_ref[1] + jax.nn.sigmoid(other_ref[0] - mine_ref[0]) * other_ref[1]
    weights = w_ref[...] * both(share)
    slope = weights * (along_ref[...] - both(average))
    slope_wide = heads_spread(slope)
    slope_out[...] = slope
    key_grad = (slope_wide * both(q_ref[...].astype(F32) * SCALE)).astype(BF16)
    value_grad = (heads_spread(weights) * both(g_ref[...])).astype(BF16)
    d_final = dot(kv_ref[...], jnp.concatenate([key_grad, value_grad], axis=0))
    d_updated = norm_grad_c(d_final, tile_lanes(gf_ref[...], 8), hat_f_ref[...], rstd_f_ref[...])
    gat = gat_ref[...]
    du_out[...] = d_updated
    d_mixed = dot_tn(wide_ref[...], c_to_rc((d_updated * gat).astype(BF16)))
    pg = norm_grad_cr(
        d_mixed, tile_lanes(gm_ref[...], 2), hat_m_ref[...], spread_cr(rstd_m_ref[...])
    ).astype(BF16)
    pg_out[:256, :] = pg[:, :128]
    pg_out[256:, :] = pg[:, 128:]


def query_kernel(key_ref, slope_ref, out_ref):
    part = heads_spread(slope_ref[...]) * key_ref[...].astype(F32)
    out_ref[...] = (part[:, :512] + part[:, 512:]) * SCALE


def coef_kernel(
    n_ref, x_ref, mask_ref, gat_ref, out_ref, du_ref, go_ref, sides_ref, cg_out, cp_out, hat_out, rstd_out, dn_out
):
    both_sides = dot_tn(sides_ref[...], n_ref[...])
    gate = jax.nn.sigmoid(both_sides[:128])
    scaled = mask_ref[:1, :] * gate
    cp_out[...] = scaled
    cg_out[...] = scaled * (1.0 - gate) * both_sides[128:]
    hat_out[...], rstd_out[...] = hat_c(x_ref[...].astype(F32))
    gat = gat_ref[...]
    d_gate = (du_ref[...] * gat * out_ref[...] * (1.0 - gat)).astype(BF16)
    dn_out[...] = dot(go_ref[...], d_gate)


def right_kernel(pg_ref, a_ref, pg_out, own_out, sent_out):
    tiles = pg_ref[...].astype(F32).reshape(8, 8, 8, 128)
    parts = swap_in([tiles[:, c].reshape(64, 128) for c in PLACES])
    split = [pair_up(v.reshape(4, 2, 8, 256)[:, 0], v.reshape(4, 2, 8, 256)[:, 1]) for v in parts]
    for e in range(2):
        pg = jnp.concatenate([v[e].reshape(32, 256) for v in split], axis=0).astype(BF16)
        pg_out[e * 128 : e * 128 + 128, :] = pg
        right = dot_tn(pg, a_ref[e * 128 : e * 128 + 128, :]).reshape(8, 2, 16, 256)
        own, sent = by_core(right[:, 0], right[:, 1])
        own_out[e * 128 : e * 128 + 128, :] = own.reshape(128, 256)
        sent_out[e * 128 : e * 128 + 128, :] = sent.reshape(128, 256).astype(BF16)


def left_kernel(pg_ref, b_ref, out_ref):
    for e in range(2):
        out_ref[e * 128 : e * 128 + 128, :] = dot(
            pg_ref[e * 128 : e * 128 + 128, :], b_ref[e * 256 : e * 256 + 256, :]
        )


def triangle_kernel(left_ref, own_ref, other_ref, out_ref):
    top = iota((8, 8, 256), 1) < 4
    right = (own_ref[...] + other_ref[...].astype(F32)).reshape(2, 8, 2, 8, 256)
    rows = []
    for q in range(4):
        tiles = []
        for e in range(2):
            left = left_ref[e * 128 + q * 32 : e * 128 + q * 32 + 32, :].reshape(4, 8, 256)
            upper = jnp.stack([left, pltpu.roll(left, 4, 1)], axis=1).reshape(8, 8, 256)
            lower = turn(right[e, :, q // 2])
            lower = lower if q & 1 else pltpu.roll(lower, 4, 1)
            tiles.append(jnp.where(top, upper, lower))
        rows.append(jnp.stack(tiles, axis=1).reshape(128, 256))
    cols = [v.reshape(8, 2, 8, 128) for v in swap_out(rows)]
    out_ref[...] = jnp.stack([cols[c] for c in COLS], axis=1).reshape(1024, 128).astype(BF16)


def finish_kernel(
    lr_ref, cg_ref, cp_ref, sides_ref, dn_ref, hat_ref, rstd_ref, du_ref, gain_ref,
    mine_ref, other_ref, wq_ref, out_ref, main_out, tiles_ref,
):
    tiles_ref[...] = lr_ref[...].astype(F32)
    blocks = [tiles_ref[pl.ds(s * 512 + side * 4 + r, 64, stride=8), :] for s, side, r in SIDE_BLOCKS]
    grad = jnp.concatenate(
        [
            jnp.concatenate([blocks[s * 8 + side * 4 + r] for s in range(2) for r in range(4)], axis=1)
            for side in range(2)
        ],
        axis=0,
    )
    grad = jnp.concatenate([(grad * cg_ref[...]).astype(BF16), (grad * cp_ref[...]).astype(BF16)], axis=0)
    d_normed = dot(sides_ref[...], grad) + dn_ref[...]
    grad_x = norm_grad_c(d_normed, tile_lanes(gain_ref[...], 8), hat_ref[...], rstd_ref[...]) + du_ref[...]
    out = dot_tn(grad_x.astype(BF16), eye64()).astype(BF16)
    for s in range(2):
        for n, i in enumerate(PIXEL_ROWS):
            out_ref[s, i] = out[s * 512 + n * 32 : s * 512 + n * 32 + 32]
    grad = (mine_ref[...] + other_ref[...]).astype(BF16)
    out = dot_tn(grad, wq_ref[...]).astype(BF16)
    for n, i in enumerate(PIXEL_ROWS):
        main_out[i] = out[n * 32 : n * 32 + 32]


def call(kernel, outs, *args, scratch=()):
    shapes = [jax.ShapeDtypeStruct(s, t) for s, t in outs]
    nbytes = sum(a.size * a.dtype.itemsize for a in args)
    return pl.pallas_call(
        kernel,
        out_shape=shapes,
        in_specs=[pl.BlockSpec(memory_space=pltpu.VMEM)] * len(args),
        out_specs=[pl.BlockSpec(memory_space=pltpu.VMEM)] * len(shapes),
        scratch_shapes=scratch,
        compiler_params=pltpu.CompilerParams(vmem_limit_bytes=24 * 1024 * 1024),
        cost_estimate=pl.CostEstimate(flops=0, bytes_accessed=nbytes, transcendentals=0),
    )(*args)


def call_copying(kernel, outs, now, later):
    shapes = [jax.ShapeDtypeStruct(s, t) for s, t in outs]
    shapes += [jax.ShapeDtypeStruct(a.shape, a.dtype) for a in later]
    args = now + later
    return pl.pallas_call(
        kernel,
        out_shape=shapes,
        in_specs=[pl.BlockSpec(memory_space=pl.ANY)] * len(args),
        out_specs=[pl.BlockSpec(memory_space=pltpu.VMEM)] * len(shapes),
        scratch_shapes=[pltpu.VMEM(a.shape, a.dtype) for a in now]
        + [pltpu.VMEM((1024, 128), F32), pltpu.SemaphoreType.DMA((len(args),))],
        compiler_params=pltpu.CompilerParams(vmem_limit_bytes=24 * 1024 * 1024),
    )(*[pltpu.with_memory_space_constraint(a, pltpu.HBM) for a in args])


def exchange(v):
    return lax.ppermute(v, "tmpl", [(0, 1), (1, 0)])


def exchange_cores(v):
    return lax.ppermute(v, "row", [(n, n ^ 1) for n in range(16)])


def spread_chunks(v, rows):
    v = lax.all_to_all(v.reshape(64, rows, 128), GROUP, 0, 0, axis_index_groups=ORDER, tiled=True)
    return v.reshape(64 * rows, 128)


def body(
    template_pair, template_mask, pair_mask, main_pair, update_cotangent,
    gain_in, proj_a, gate_a, proj_b, gate_b, gain_mid, proj_out, gate_out, gain_final,
    key_weight, value_weight, query_weight, output_weight,
):
    gi, gm, gf = gain_in.reshape(1, 64), gain_mid.reshape(1, 64), gain_final.reshape(1, 64)
    sides, x, normed, gi_wide, side_weights, mask, *later = call_copying(
        front_kernel,
        [
            ((1024, 128), BF16), ((64, 1024), BF16), ((64, 1024), BF16), ((64, 128), F32), ((64, 256), BF16),
            ((8, 1024), F32),
        ],
        [template_pair, pair_mask, gi, proj_a, gate_a, proj_b, gate_b],
        [
            gate_out, main_pair, update_cotangent, query_weight.T, output_weight, proj_out, key_weight,
            value_weight, gm, gf, template_mask.reshape(1, 2),
        ],
    )
    sides = spread_chunks(sides, 16)
    a, b_own = call(layout_kernel, [((256, 256), BF16), ((256, 256), BF16)], sides)
    b_other = exchange_cores(b_own)
    b_own, normed, later = lax.optimization_barrier((b_own, normed, later))
    side = call(
        side_kernel,
        [
            ((64, 1024), F32), ((64, 512), BF16), ((64, 512), F32), ((256, 256), BF16), ((64, 128), BF16),
            ((256, 128), F32), ((64, 128), F32), ((8, 1024), F32),
        ],
        normed, *later,
    )
    b_other, (gat, query, grad_out, wide, kv, gm_wide, gf_wide, absent) = lax.optimization_barrier(
        (b_other, side)
    )
    prod, b = call(product_kernel, [((512, 128), BF16), ((512, 256), BF16)], a, b_own, b_other)
    prod = spread_chunks(prod, 8)
    stat, weights, along, key, hat_m, rstd_m, out, hat_f, rstd_f = call(
        score_kernel,
        [
            ((2, 4, 512), F32), ((4, 1024), F32), ((4, 1024), F32), ((64, 1024), BF16),
            ((256, 256), F32), ((8, 256), F32), ((64, 1024), F32), ((64, 1024), F32), ((1, 1024), F32),
        ],
        x, prod, gat, query, grad_out, absent, gm_wide, gf_wide, wide, kv,
    )
    other = exchange(stat)
    pg, slope, d_updated = call(
        grad_kernel,
        [((512, 128), BF16), ((4, 1024), F32), ((64, 1024), F32)],
        gat, query, grad_out, weights, along, stat, other,
        gm_wide, gf_wide, wide, kv, hat_m, rstd_m, hat_f, rstd_f,
    )
    (query_sum,) = call(query_kernel, [((64, 512), F32)], key, slope)
    pg = spread_chunks(pg, 8)
    pg, right_own, right_sent = call(
        right_kernel, [((256, 256), BF16), ((256, 256), F32), ((256, 256), BF16)], pg, a
    )
    right_other = exchange_cores(right_sent)
    right_own, normed, gate_weight = lax.optimization_barrier((right_own, normed, later[0]))
    cg, cp, hat, rstd, dn = call(
        coef_kernel,
        [((128, 1024), F32), ((128, 1024), F32), ((64, 1024), F32), ((1, 1024), F32), ((64, 1024), F32)],
        normed, x, mask, gat, out, d_updated, gate_weight, side_weights,
    )
    right_other, query_other, cg, cp, hat, rstd, dn = lax.optimization_barrier(
        (right_other, exchange(query_sum), cg, cp, hat, rstd, dn)
    )
    (left,) = call(left_kernel, [((256, 256), F32)], pg, b)
    (grads,) = call(triangle_kernel, [((1024, 128), BF16)], left, right_own, right_other)
    grads = spread_chunks(grads, 16)
    pair_grad, main_grad = call(
        finish_kernel, [((2, 16, 32, 64), BF16), ((16, 32, 128), BF16)],
        grads, cg, cp, side_weights, dn, hat, rstd, d_updated, gi_wide, query_sum, query_other, later[3],
        scratch=[pltpu.VMEM((1024, 128), F32)],
    )
    return (pair_grad, main_grad)


def solution(mesh):
    pixel = P("row", "col", None)
    placed = (
        P("tmpl", "row", "col", None), P("tmpl"), P("row", "col"), pixel, pixel,
    ) + (P(),) * 13
    return jax.shard_map(
        body,
        mesh=mesh,
        in_specs=placed,
        out_specs=(P("tmpl", "row", "col", None), pixel),
        check_vma=False,
    )
```

```python
import functools
import math

import jax
import jax.numpy as jnp
from jax import lax
from jax.experimental import pallas as pl
from jax.experimental.pallas import tpu as pltpu
from jax.sharding import PartitionSpec as P

EPS = 1e-05
F32 = jnp.float32
BF16 = jnp.bfloat16
HEADS = 4
HEAD_DIM = 16
SCALE = 1.0 / math.sqrt(HEAD_DIM)
GROUP = ("row", "col")
TURN = 6
LATER = 11
SIDE_BLOCKS = [(s, side, r) for s in range(2) for side in range(2) for r in range(4)]
PIXEL_ROWS = [4 * q + r for r in range(4) for q in range(4)]
COLS = [x * 4 + y for y in range(4) for x in range(2)]
PLACES = [COLS.index(col) for col in range(8)]
ORDER = [[(z ^ TURN) * 16 + core * 8 + col for z in range(8) for col in COLS] for core in range(2)]


def iota(shape, axis):
    return lax.broadcasted_iota(jnp.int32, shape, axis)


def shr(v, n):
    return lax.shift_right_logical(v, jnp.full(v.shape, n, jnp.int32))


def onehot(cond):
    return jnp.where(cond, 1.0, 0.0).astype(BF16)


def dot(a, b):
    return lax.dot_general(a, b, (((1,), (0,)), ((), ())), preferred_element_type=F32)


def dot_nt(a, b):
    return lax.dot_general(a, b, (((1,), (1,)), ((), ())), preferred_element_type=F32)


def dot_tn(a, b):
    return lax.dot_general(a, b, (((0,), (0,)), ((), ())), preferred_element_type=F32)


def eye64():
    return onehot(iota((64, 64), 0) == iota((64, 64), 1))


def c_to_rc(v):
    return jnp.concatenate(
        [
            jnp.concatenate([v[:, s * 512 + r * 128 : s * 512 + r * 128 + 128] for s in range(2)], axis=1)
            for r in range(4)
        ],
        axis=0,
    )


def rc_to_c(v):
    return jnp.concatenate(
        [v[r * 64 : r * 64 + 64, s * 128 : s * 128 + 128] for s in range(2) for r in range(4)], axis=1
    )


def both(v):
    return jnp.concatenate([v, v], axis=1)


def column(gain_row, repeat):
    pick = shr(iota((64 * repeat, 64), 0), repeat // 2) == iota((64 * repeat, 64), 1)
    return jnp.sum(jnp.where(pick, gain_row, 0.0), axis=1, keepdims=True)


def mean_c(v):
    return jnp.mean(v, axis=0, keepdims=True)


def mean_cr(v):
    part = jnp.sum(v.reshape(32, 8, 256), axis=0)
    return (part + pltpu.roll(part, 4, 0)) * (1.0 / 64.0)


def spread_cr(v):
    return jnp.broadcast_to(v[None], (32, 8, 256)).reshape(256, 256)


def hat_c(v):
    centered = v - mean_c(v)
    rstd = lax.rsqrt(mean_c(centered * centered) + EPS)
    return centered * rstd, rstd


def norm_grad_c(grad, gain, hat, rstd):
    scaled = grad * gain
    return rstd * (scaled - mean_c(scaled) - hat * mean_c(scaled * hat))


def hat_cr(v):
    centered = v - spread_cr(mean_cr(v))
    rstd = spread_cr(lax.rsqrt(mean_cr(centered * centered) + EPS))
    return centered * rstd, rstd


def norm_grad_cr(grad, gain, hat, rstd):
    scaled = grad * gain
    return rstd * (scaled - spread_cr(mean_cr(scaled)) - hat * spread_cr(mean_cr(scaled * hat)))


def wide_out(w):
    row, lane = iota((64, 256), 0), iota((64, 256), 1)
    base = dot_tn(w, onehot(row == shr(lane, 2)))
    return jnp.concatenate([jnp.where((lane & 3) == r, base, 0.0) for r in range(4)], axis=0).astype(BF16)


def mask_row(mask):
    tiled = dot(mask.astype(F32).astype(BF16), onehot(iota((32, 128), 0) == (iota((32, 128), 1) & 31)))
    i, lane = iota((16, 128), 0), iota((16, 128), 1)
    tiled = jnp.where(shr(i, 2) == shr(lane, 5), tiled, 0.0).astype(BF16)
    rows = dot(onehot((iota((8, 16), 0) & 3) == (iota((8, 16), 1) & 3)), tiled)
    return both(jnp.concatenate([rows[r : r + 1] for r in range(4)], axis=1))


def swap_groups(four):
    lane = iota(four[0].shape, 1)
    for bit in (1, 2):
        low = (lane & (32 * bit)) == 0
        out = []
        for a in range(4):
            if a & bit == 0:
                out.append(jnp.where(low, four[a], pltpu.roll(four[a ^ bit], 32 * bit, 1)))
            else:
                out.append(jnp.where(low, pltpu.roll(four[a ^ bit], 128 - 32 * bit, 1), four[a]))
        four = out
    return four


def swap_in(blocks):
    lo, hi = swap_groups(blocks[:4]), swap_groups(blocks[4:])
    return [jnp.concatenate([lo[q], hi[q]], axis=1) for q in range(4)]


def swap_out(rows):
    return swap_groups([v[:, :128] for v in rows]) + swap_groups([v[:, 128:] for v in rows])


def pair_up(even, odd):
    top = iota(even.shape, even.ndim - 2) < 4
    axis = even.ndim - 2
    return jnp.where(top, even, pltpu.roll(odd, 4, axis)), jnp.where(top, pltpu.roll(even, 4, axis), odd)


def turn(v):
    return jnp.concatenate([v[n ^ TURN : (n ^ TURN) + 2] for n in range(0, 8, 2)], axis=0)


def by_core(first, second):
    core0 = (lax.axis_index("row") & 1) == 0
    return jnp.where(core0, first, second), jnp.where(core0, second, first)


def front_kernel(
    x_hbm, mask_hbm, gi_hbm, pa_hbm, ga_hbm, pb_hbm, gb_hbm, *refs
):
    later, refs = refs[:LATER], refs[LATER:]
    out_ref, x_out, n_out, gi_out, sides_out, mask_out = refs[:6]
    later_out, refs = refs[6 : 6 + LATER], refs[6 + LATER :]
    x_ref, mask_ref, gi_ref, pa_ref, ga_ref, pb_ref, gb_ref, tiles_ref, sems = refs
    pairs = [
        (x_hbm, x_ref), (gi_hbm, gi_ref), (pa_hbm, pa_ref), (ga_hbm, ga_ref), (pb_hbm, pb_ref),
        (gb_hbm, gb_ref), (mask_hbm, mask_ref),
    ] + list(zip(later, later_out))
    copies = [pltpu.make_async_copy(a, b, sems.at[n]) for n, (a, b) in enumerate(pairs)]
    for copy in copies:
        copy.start()
    for copy in copies[1:7]:
        copy.wait()
    weights = jnp.concatenate([ga_ref[...], gb_ref[...], pa_ref[...], pb_ref[...]], axis=1)
    sides_out[...] = weights
    mask = mask_row(mask_ref[...])
    mask_out[...] = jnp.broadcast_to(mask, (8, 1024))
    copies[0].wait()
    x = dot_nt(eye64(), jnp.concatenate([x_ref[s, i] for s in range(2) for i in PIXEL_ROWS], axis=0))
    hat, _ = hat_c(x)
    gi = column(gi_ref[...], 1)
    normed = (hat * gi).astype(BF16)
    x_out[...] = x.astype(BF16)
    n_out[...] = normed
    gi_out[...] = jnp.broadcast_to(gi, (64, 128))
    both_sides = dot_tn(weights, normed)
    both_sides = mask * jax.nn.sigmoid(both_sides[:128]) * both_sides[128:]
    for s, side, r in SIDE_BLOCKS:
        tiles_ref[pl.ds(s * 512 + side * 4 + r, 64, stride=8), :] = both_sides[
            side * 64 : side * 64 + 64, s * 512 + r * 128 : s * 512 + r * 128 + 128
        ]
    out_ref[...] = tiles_ref[...].astype(BF16)
    for copy in copies[7:]:
        copy.wait()


def side_kernel(
    n_ref, go_ref, main_ref, cot_ref, wq_ref, wo_ref, po_ref, kw_ref, vw_ref, gm_ref, gf_ref, present_ref,
    gat_out, q_out, g_out, wide_out_ref, kv_out, gm_out, gf_out, absent_out,
):
    gat_out[...] = jax.nn.sigmoid(dot_tn(go_ref[...], n_ref[...]))
    q_out[...] = dot_nt(wq_ref[...], jnp.concatenate([main_ref[i] for i in PIXEL_ROWS], axis=0)).astype(BF16)
    g_out[...] = dot_nt(wo_ref[...], jnp.concatenate([cot_ref[i] for i in PIXEL_ROWS], axis=0))
    wide_out_ref[...] = wide_out(po_ref[...])
    kv_out[...] = jnp.concatenate([kw_ref[...], vw_ref[...]], axis=1)
    gm_out[...] = jnp.broadcast_to(column(gm_ref[...], 4), (256, 128))
    gf_out[...] = jnp.broadcast_to(column(gf_ref[...], 1), (64, 128))
    absent_out[...] = jnp.where(
        jnp.concatenate([jnp.broadcast_to(present_ref[:, s : s + 1], (8, 512)) for s in range(2)], axis=1) > 0,
        0.0, -1e30,
    )


def layout_kernel(x_ref, a_out, b_out):
    tiles = x_ref[...].astype(F32).reshape(8, 8, 2, 8, 128)
    parts = [v.reshape(8, 2, 8, 256) for v in swap_in([tiles[:, c].reshape(128, 128) for c in PLACES])]
    rolled = [pltpu.roll(v.reshape(16, 8, 256), 4, 1).reshape(8, 2, 8, 256) for v in parts]
    top = iota((8, 8, 256), 1) < 4
    a, b = [], []
    for e in range(2):
        for v, w in zip(parts, rolled):
            v, w = v[:, e].reshape(4, 2, 8, 256), w[:, e].reshape(4, 2, 8, 256)
            a.append(jnp.where(top[:4], v[:, 0], w[:, 1]).reshape(32, 256))
        half = [turn(jnp.where(top, rolled[q][:, e], parts[q + 1][:, e])) for q in (0, 2)]
        b.append(jnp.stack(half, axis=1).reshape(128, 256))
    a_out[...] = jnp.concatenate(a, axis=0).astype(BF16)
    b_out[...] = jnp.concatenate(b, axis=0).astype(BF16)


def whole_b(own_ref, other_ref, e):
    own = own_ref[e * 128 : e * 128 + 128, :].reshape(8, 16, 256)
    other = other_ref[e * 128 : e * 128 + 128, :].reshape(8, 16, 256)
    return jnp.stack(by_core(own, other), axis=1).reshape(256, 256)


def product_kernel(a_ref, own_ref, other_ref, out_ref):
    prods = [dot_nt(a_ref[e * 128 : e * 128 + 128, :], whole_b(own_ref, other_ref, e)) for e in range(2)]
    rows = [jnp.concatenate([v[q * 32 : q * 32 + 32] for v in prods], axis=0) for q in range(4)]
    pairs = []
    for v in swap_out(rows):
        v = v.reshape(2, 4, 8, 128)
        pairs.append(jnp.stack(pair_up(v[0], v[1]), axis=1).reshape(8, 8, 128))
    out_ref[...] = jnp.stack([pairs[c] for c in COLS], axis=1).reshape(512, 128).astype(BF16)


def heads_sum(v):
    return jnp.sum(v.reshape(HEADS, HEAD_DIM, v.shape[-1]), axis=1)


def heads_spread(v):
    return jnp.broadcast_to(v[:, None, :], (HEADS, HEAD_DIM, v.shape[-1])).reshape(64, v.shape[-1])


def tile_lanes(v, n):
    return jnp.concatenate([v] * n, axis=1)


def score_kernel(
    x_ref, prod_ref, gat_ref, q_ref, g_ref, absent_ref, gm_ref, gf_ref, wide_ref, kv_ref,
    stat_out, w_out, along_out, key_out, hat_m_out, rstd_m_out, out_out, hat_f_out, rstd_f_out,
):
    prod = jnp.concatenate([prod_ref[:256, :], prod_ref[256:, :]], axis=1).astype(F32)
    centered = prod - spread_cr(mean_cr(prod))
    rstd_m = lax.rsqrt(mean_cr(centered * centered) + EPS)
    hat_m = centered * spread_cr(rstd_m)
    out = rc_to_c(dot(wide_ref[...], (hat_m * tile_lanes(gm_ref[...], 2)).astype(BF16)))
    hat_f, rstd_f = hat_c(x_ref[...].astype(F32) + gat_ref[...] * out)
    hat_m_out[...] = hat_m
    rstd_m_out[...] = rstd_m
    out_out[...] = out
    hat_f_out[...] = hat_f
    rstd_f_out[...] = rstd_f
    final = (hat_f * tile_lanes(gf_ref[...], 8)).astype(BF16)
    key_val = dot_tn(kv_ref[...], final).astype(BF16)
    key, val = key_val[:64], key_val[64:]
    key_out[...] = key
    score = heads_sum(both(q_ref[...].astype(F32)) * key.astype(F32)) * SCALE
    along = heads_sum(both(g_ref[...]) * val.astype(F32))
    score = jnp.where(absent_ref[:4, :] < 0.0, -1e30, score)
    s0, s1 = score[:, :512], score[:, 512:]
    top = jnp.maximum(s0, s1)
    e0, e1 = jnp.exp(s0 - top), jnp.exp(s1 - top)
    total = e0 + e1
    w0, w1 = e0 / total, e1 / total
    w_out[...] = jnp.concatenate([w0, w1], axis=1)
    along_out[...] = along
    stat_out[0] = top + jnp.log(total)
    stat_out[1] = w0 * along[:, :512] + w1 * along[:, 512:]


def grad_kernel(
    gat_ref, q_ref, g_ref, w_ref, along_ref, mine_ref, other_ref,
    gm_ref, gf_ref, wide_ref, kv_ref, hat_m_ref, rstd_m_ref, hat_f_ref, rstd_f_ref,
    pg_out, slope_out, du_out,
):
    share = jax.nn.sigmoid(mine_ref[0] - other_ref[0])
    average = share * mine_ref[1] + jax.nn.sigmoid(other_ref[0] - mine_ref[0]) * other_ref[1]
    weights = w_ref[...] * both(share)
    slope = weights * (along_ref[...] - both(average))
    slope_wide = heads_spread(slope)
    slope_out[...] = slope
    key_grad = (slope_wide * both(q_ref[...].astype(F32) * SCALE)).astype(BF16)
    value_grad = (heads_spread(weights) * both(g_ref[...])).astype(BF16)
    d_final = dot(kv_ref[...], jnp.concatenate([key_grad, value_grad], axis=0))
    d_updated = norm_grad_c(d_final, tile_lanes(gf_ref[...], 8), hat_f_ref[...], rstd_f_ref[...])
    gat = gat_ref[...]
    du_out[...] = d_updated
    d_mixed = dot_tn(wide_ref[...], c_to_rc((d_updated * gat).astype(BF16)))
    pg = norm_grad_cr(
        d_mixed, tile_lanes(gm_ref[...], 2), hat_m_ref[...], spread_cr(rstd_m_ref[...])
    ).astype(BF16)
    pg_out[:256, :] = pg[:, :128]
    pg_out[256:, :] = pg[:, 128:]


def query_kernel(key_ref, slope_ref, out_ref):
    part = heads_spread(slope_ref[...]) * key_ref[...].astype(F32)
    out_ref[...] = (part[:, :512] + part[:, 512:]) * SCALE


def coef_kernel(
    n_ref, x_ref, mask_ref, gat_ref, out_ref, du_ref, go_ref, sides_ref, cg_out, cp_out, hat_out, rstd_out, dn_out
):
    both_sides = dot_tn(sides_ref[...], n_ref[...])
    gate = jax.nn.sigmoid(both_sides[:128])
    scaled = mask_ref[:1, :] * gate
    cp_out[...] = scaled
    cg_out[...] = scaled * (1.0 - gate) * both_sides[128:]
    hat_out[...], rstd_out[...] = hat_c(x_ref[...].astype(F32))
    gat = gat_ref[...]
    d_gate = (du_ref[...] * gat * out_ref[...] * (1.0 - gat)).astype(BF16)
    dn_out[...] = dot(go_ref[...], d_gate)


def right_kernel(pg_ref, a_ref, pg_out, own_out, sent_out):
    tiles = pg_ref[...].astype(F32).reshape(8, 8, 8, 128)
    parts = swap_in([tiles[:, c].reshape(64, 128) for c in PLACES])
    split = [pair_up(v.reshape(4, 2, 8, 256)[:, 0], v.reshape(4, 2, 8, 256)[:, 1]) for v in parts]
    for e in range(2):
        pg = jnp.concatenate([v[e].reshape(32, 256) for v in split], axis=0).astype(BF16)
        pg_out[e * 128 : e * 128 + 128, :] = pg
        right = dot_tn(pg, a_ref[e * 128 : e * 128 + 128, :]).reshape(8, 2, 16, 256)
        own, sent = by_core(right[:, 0], right[:, 1])
        own_out[e * 128 : e * 128 + 128, :] = own.reshape(128, 256)
        sent_out[e * 128 : e * 128 + 128, :] = sent.reshape(128, 256).astype(BF16)


def left_kernel(pg_ref, own_ref, other_ref, out_ref):
    for e in range(2):
        out_ref[e * 128 : e * 128 + 128, :] = dot(
            pg_ref[e * 128 : e * 128 + 128, :], whole_b(own_ref, other_ref, e)
        )


def triangle_kernel(left_ref, own_ref, other_ref, out_ref):
    top = iota((8, 8, 256), 1) < 4
    right = (own_ref[...] + other_ref[...].astype(F32)).reshape(2, 8, 2, 8, 256)
    rows = []
    for q in range(4):
        tiles = []
        for e in range(2):
            left = left_ref[e * 128 + q * 32 : e * 128 + q * 32 + 32, :].reshape(4, 8, 256)
            upper = jnp.stack([left, pltpu.roll(left, 4, 1)], axis=1).reshape(8, 8, 256)
            lower = turn(right[e, :, q // 2])
            lower = lower if q & 1 else pltpu.roll(lower, 4, 1)
            tiles.append(jnp.where(top, upper, lower))
        rows.append(jnp.stack(tiles, axis=1).reshape(128, 256))
    cols = [v.reshape(8, 2, 8, 128) for v in swap_out(rows)]
    out_ref[...] = jnp.stack([cols[c] for c in COLS], axis=1).reshape(1024, 128).astype(BF16)


def finish_kernel(
    lr_ref, cg_ref, cp_ref, sides_ref, dn_ref, hat_ref, rstd_ref, du_ref, gain_ref,
    mine_ref, other_ref, wq_ref, out_ref, main_out, tiles_ref,
):
    tiles_ref[...] = lr_ref[...].astype(F32)
    blocks = [tiles_ref[pl.ds(s * 512 + side * 4 + r, 64, stride=8), :] for s, side, r in SIDE_BLOCKS]
    grad = jnp.concatenate(
        [
            jnp.concatenate([blocks[s * 8 + side * 4 + r] for s in range(2) for r in range(4)], axis=1)
            for side in range(2)
        ],
        axis=0,
    )
    grad = jnp.concatenate([(grad * cg_ref[...]).astype(BF16), (grad * cp_ref[...]).astype(BF16)], axis=0)
    d_normed = dot(sides_ref[...], grad) + dn_ref[...]
    grad_x = norm_grad_c(d_normed, tile_lanes(gain_ref[...], 8), hat_ref[...], rstd_ref[...]) + du_ref[...]
    out = dot_tn(grad_x.astype(BF16), eye64()).astype(BF16)
    for s in range(2):
        for n, i in enumerate(PIXEL_ROWS):
            out_ref[s, i] = out[s * 512 + n * 32 : s * 512 + n * 32 + 32]
    grad = (mine_ref[...] + other_ref[...]).astype(BF16)
    out = dot_tn(grad, wq_ref[...]).astype(BF16)
    for n, i in enumerate(PIXEL_ROWS):
        main_out[i] = out[n * 32 : n * 32 + 32]


def call(kernel, outs, *args, scratch=()):
    shapes = [jax.ShapeDtypeStruct(s, t) for s, t in outs]
    nbytes = sum(a.size * a.dtype.itemsize for a in args)
    return pl.pallas_call(
        kernel,
        out_shape=shapes,
        in_specs=[pl.BlockSpec(memory_space=pltpu.VMEM)] * len(args),
        out_specs=[pl.BlockSpec(memory_space=pltpu.VMEM)] * len(shapes),
        scratch_shapes=scratch,
        compiler_params=pltpu.CompilerParams(vmem_limit_bytes=24 * 1024 * 1024),
        cost_estimate=pl.CostEstimate(flops=0, bytes_accessed=nbytes, transcendentals=0),
    )(*args)


def call_copying(kernel, outs, now, later):
    shapes = [jax.ShapeDtypeStruct(s, t) for s, t in outs]
    shapes += [jax.ShapeDtypeStruct(a.shape, a.dtype) for a in later]
    args = now + later
    return pl.pallas_call(
        kernel,
        out_shape=shapes,
        in_specs=[pl.BlockSpec(memory_space=pl.ANY)] * len(args),
        out_specs=[pl.BlockSpec(memory_space=pltpu.VMEM)] * len(shapes),
        scratch_shapes=[pltpu.VMEM(a.shape, a.dtype) for a in now]
        + [pltpu.VMEM((1024, 128), F32), pltpu.SemaphoreType.DMA((len(args),))],
        compiler_params=pltpu.CompilerParams(vmem_limit_bytes=24 * 1024 * 1024),
    )(*[pltpu.with_memory_space_constraint(a, pltpu.HBM) for a in args])


def exchange(v):
    return lax.ppermute(v, "tmpl", [(0, 1), (1, 0)])


def exchange_cores(v):
    return lax.ppermute(v, "row", [(n, n ^ 1) for n in range(16)])


def spread_chunks(v, rows):
    v = lax.all_to_all(v.reshape(64, rows, 128), GROUP, 0, 0, axis_index_groups=ORDER, tiled=True)
    return v.reshape(64 * rows, 128)


def body(
    template_pair, template_mask, pair_mask, main_pair, update_cotangent,
    gain_in, proj_a, gate_a, proj_b, gate_b, gain_mid, proj_out, gate_out, gain_final,
    key_weight, value_weight, query_weight, output_weight,
):
    gi, gm, gf = gain_in.reshape(1, 64), gain_mid.reshape(1, 64), gain_final.reshape(1, 64)
    sides, x, normed, gi_wide, side_weights, mask, *later = call_copying(
        front_kernel,
        [
            ((1024, 128), BF16), ((64, 1024), BF16), ((64, 1024), BF16), ((64, 128), F32), ((64, 256), BF16),
            ((8, 1024), F32),
        ],
        [template_pair, pair_mask, gi, proj_a, gate_a, proj_b, gate_b],
        [
            gate_out, main_pair, update_cotangent, query_weight.T, output_weight, proj_out, key_weight,
            value_weight, gm, gf, template_mask.reshape(1, 2),
        ],
    )
    sides = spread_chunks(sides, 16)
    a, b_own = call(layout_kernel, [((256, 256), BF16), ((256, 256), BF16)], sides)
    b_other = exchange_cores(b_own)
    b_own, normed, later = lax.optimization_barrier((b_own, normed, later))
    side = call(
        side_kernel,
        [
            ((64, 1024), F32), ((64, 512), BF16), ((64, 512), F32), ((256, 256), BF16), ((64, 128), BF16),
            ((256, 128), F32), ((64, 128), F32), ((8, 1024), F32),
        ],
        normed, *later,
    )
    b_other, (gat, query, grad_out, wide, kv, gm_wide, gf_wide, absent) = lax.optimization_barrier(
        (b_other, side)
    )
    (prod,) = call(product_kernel, [((512, 128), BF16)], a, b_own, b_other)
    prod = spread_chunks(prod, 8)
    stat, weights, along, key, hat_m, rstd_m, out, hat_f, rstd_f = call(
        score_kernel,
        [
            ((2, 4, 512), F32), ((4, 1024), F32), ((4, 1024), F32), ((64, 1024), BF16),
            ((256, 256), F32), ((8, 256), F32), ((64, 1024), F32), ((64, 1024), F32), ((1, 1024), F32),
        ],
        x, prod, gat, query, grad_out, absent, gm_wide, gf_wide, wide, kv,
    )
    other = exchange(stat)
    pg, slope, d_updated = call(
        grad_kernel,
        [((512, 128), BF16), ((4, 1024), F32), ((64, 1024), F32)],
        gat, query, grad_out, weights, along, stat, other,
        gm_wide, gf_wide, wide, kv, hat_m, rstd_m, hat_f, rstd_f,
    )
    (query_sum,) = call(query_kernel, [((64, 512), F32)], key, slope)
    pg = spread_chunks(pg, 8)
    pg, right_own, right_sent = call(
        right_kernel, [((256, 256), BF16), ((256, 256), F32), ((256, 256), BF16)], pg, a
    )
    right_other = exchange_cores(right_sent)
    right_own, normed, gate_weight = lax.optimization_barrier((right_own, normed, later[0]))
    cg, cp, hat, rstd, dn = call(
        coef_kernel,
        [((128, 1024), F32), ((128, 1024), F32), ((64, 1024), F32), ((1, 1024), F32), ((64, 1024), F32)],
        normed, x, mask, gat, out, d_updated, gate_weight, side_weights,
    )
    right_other, query_other, cg, cp, hat, rstd, dn = lax.optimization_barrier(
        (right_other, exchange(query_sum), cg, cp, hat, rstd, dn)
    )
    (left,) = call(left_kernel, [((256, 256), F32)], pg, b_own, b_other)
    (grads,) = call(triangle_kernel, [((1024, 128), BF16)], left, right_own, right_other)
    grads = spread_chunks(grads, 16)
    pair_grad, main_grad = call(
        finish_kernel, [((2, 16, 32, 64), BF16), ((16, 32, 128), BF16)],
        grads, cg, cp, side_weights, dn, hat, rstd, d_updated, gi_wide, query_sum, query_other, later[3],
        scratch=[pltpu.VMEM((1024, 128), F32)],
    )
    return (pair_grad, main_grad)


def solution(mesh):
    pixel = P("row", "col", None)
    placed = (
        P("tmpl", "row", "col", None), P("tmpl"), P("row", "col"), pixel, pixel,
    ) + (P(),) * 13
    return jax.shard_map(
        body,
        mesh=mesh,
        in_specs=placed,
        out_specs=(P("tmpl", "row", "col", None), pixel),
        check_vma=False,
    )
```
